32 devices in a mesh: dp: 16 (over z, x, core), seq: 2 (over y).
Axes of the slice: x: 2, y: 2, z: 4, core: 2. Of those that a mesh axis runs over, the one named last changes fastest.
Arguments:
- tokens: bfloat16 [32, 1024, 768], P('dp', 'seq'), may hold values from -6 to 6
- lengths: int32 [32], P('dp'), may hold values from 256 to 1024, as said below
- gain_one: float32 [768], replicated, may hold values from 0.5 to 1.5
- w_query: bfloat16 [768, 768], replicated, may hold values from -0.21875 to 0.21875
- w_key: bfloat16 [768, 768], replicated, may hold values from -0.21875 to 0.21875
- w_value: bfloat16 [768, 768], replicated, may hold values from -0.21875 to 0.21875
- w_out: bfloat16 [768, 768], replicated, may hold values from -0.21875 to 0.21875
- gain_two: float32 [768], replicated, may hold values from 0.5 to 1.5
- w_up: bfloat16 [768, 3072], replicated, may hold values from -0.21875 to 0.21875
- w_down: bfloat16 [3072, 768], replicated, may hold values from -0.109375 to 0.109375
- shift_taps: float32 [768, 64], P('seq'), may hold values from -0.75 to 0.75
- diag_coef: float32 [768, 64], P('seq'), may hold values from -0.09375 to 0.09375
- diag_rate: float32 [768, 64], P('seq'), may hold values from 0.001 to 0.3
- cotangent: bfloat16 [32, 1024, 768], P('dp', 'seq'), may hold values from -6 to 6
Outputs:
- out: bfloat16 [32, 1024, 768], P('dp', 'seq')
- d_tokens: bfloat16 [32, 1024, 768], P('dp', 'seq')
- grad_gain_one: float32 [768], P('dp')
- grad_w_query: float32 [768, 768], P('dp')
- grad_w_key: float32 [768, 768], P('dp')
- grad_w_value: float32 [768, 768], P('dp')
- grad_w_out: float32 [768, 768], P('dp')
- grad_gain_two: float32 [768], P('dp')
- grad_w_up: float32 [768, 3072], P('dp')
- grad_w_down: float32 [3072, 768], P('dp')
- grad_shift_taps: float32 [768, 64], P('seq', 'dp')
- grad_diag_coef: float32 [768, 64], P('seq', 'dp')
- grad_diag_rate: float32 [768, 64], P('seq', 'dp')
The draws below stay inside these ranges and needn't reach their ends.
Inputs may be any that keep to these rules, and one draw needn't show every extreme that they name: `lengths`: in each aligned block of 2 rows at least one row has length 1024.
All inputs are finite; a program needn't handle non-finite values.
Results may differ from the reference program's by a relative error of at most 0.02.
Values may be sent and summed in bfloat16 or wider, within the bound.
A program may use at most 256 MiB of HBM per device.

```python
import math
import jax
import jax.numpy as jnp
from jax import lax

D = 768
FF = 3072
STATE = 64
LENGTH = 1024
ROWS_DEV = 2
ROWS = 32


def draw_lengths(key, part):
    key = jax.random.fold_in(key, 7)
    first_key, second_key = jax.random.split(key)
    rough = jax.random.randint(first_key, (ROWS,), LENGTH // 4, LENGTH + 1)
    chosen = jax.random.randint(second_key, (ROWS // ROWS_DEV,), 0, ROWS_DEV)
    slots = jnp.arange(ROWS, dtype=jnp.int32)
    picked = slots % ROWS_DEV == jnp.repeat(chosen, ROWS_DEV)
    return jnp.where(picked, LENGTH, rough).astype(jnp.int32)


def shard_levels(own_key, dims, shards, smallest, top_value):
    def one(axis_at, blocks):
        draws = jax.random.uniform(jax.random.fold_in(jax.random.fold_in(own_key, 6), axis_at), (blocks,), jnp.float32, smallest / len(shards), top_value / len(shards))
        return jnp.repeat(jnp.exp(draws), dims[axis_at] // blocks).reshape((-1,) + (1,) * (len(dims) - axis_at - 1))

    level = one(*shards[0])
    for cut in shards[1:]:
        level = level * one(*cut)
    return level


def noise(key, dims, deviation, limit, cuts=(), kind=jnp.bfloat16):
    values = jax.random.normal(key, dims, jnp.float32) * deviation
    if len(cuts) > 0:
        values = shard_levels(key, dims, cuts, -0.22, 0.18) * values
    return jnp.clip(values, min=-limit, max=limit).astype(kind)


def setup_inputs(seed: int = 0) -> dict:
    streams_of = jax.random.split(jax.random.key(seed), 15)
    return {
        "tokens": noise(streams_of[0], (ROWS, LENGTH, D), 1.0, 6.0, ((0, 16), (1, 2))),
        "lengths": draw_lengths(jax.random.fold_in(streams_of[14], 71), 0),
        "gain_one": jnp.clip(1.0 + 0.1 * jax.random.normal(streams_of[2], (D,), jnp.float32), 0.5, 1.5),
        "w_query": noise(streams_of[3], (D, D), D ** -0.5, 0.21875),
        "w_key": noise(streams_of[4], (D, D), D ** -0.5, 0.21875),
        "w_value": noise(streams_of[5], (D, D), D ** -0.5, 0.21875),
        "w_out": noise(streams_of[6], (D, D), D ** -0.5, 0.21875),
        "gain_two": jnp.clip(1.0 + 0.1 * jax.random.normal(streams_of[7], (D,), jnp.float32), 0.5, 1.5),
        "w_up": noise(streams_of[8], (D, FF), D ** -0.5, 0.21875),
        "w_down": noise(streams_of[9], (FF, D), FF ** -0.5, 0.109375),
        "shift_taps": noise(streams_of[10], (D, STATE), STATE ** -0.5, 0.75, ((0, 2),), jnp.float32),
        "diag_coef": noise(streams_of[11], (D, STATE), (STATE * 64) ** -0.5, 0.09375, ((0, 2),), jnp.float32),
        "diag_rate": jnp.clip(jnp.exp(math.log(0.3) - 5.7037825 * jax.random.uniform(streams_of[12], (D, STATE), jnp.float32) ** shard_levels(streams_of[12], (D, STATE), ((0, 2),), -0.2, 0.2)), 0.001, 0.3),
        "cotangent": noise(streams_of[13], (ROWS, LENGTH, D), 1.0, 6.0, ((0, 16), (1, 2))),
    }


epsilon = 1e-05
highest = lax.Precision.HIGHEST

@jax.custom_vjp
def low(v):
    return lax.optimization_barrier(v.astype(jnp.bfloat16)).astype(jnp.float32)

@jax.custom_vjp
def low_back(v):
    return v

def low_keep(v):
    return (low(v), None)

def low_pass(kept, grad):
    return (grad,)

def back_keep(v):
    return (v, None)

def back_low(kept, grad):
    return (low(grad),)
low.defvjp(low_keep, low_pass)
low_back.defvjp(back_keep, back_low)

def layer_norm(rows, gain):
    center = rows - lax.optimization_barrier(jnp.mean(rows, axis=-1, keepdims=True))
    spread = lax.optimization_barrier(jnp.mean(center * center, axis=-1, keepdims=True))
    return center * lax.rsqrt(spread + epsilon) * gain

def project(rows, weight):
    return jnp.einsum('rtd,de->rte', rows, weight, precision=highest)

def shift_conv(signal, taps):
    width_taps = taps.shape[1]
    length = signal.shape[1]
    padded = jnp.pad(signal, ((0, 0), (width_taps, 0), (0, 0)))
    summed = jnp.zeros_like(signal)
    for offset in range(width_taps):
        summed = summed + taps[:, offset] * padded[:, width_taps - offset:width_taps - offset + length, :]
    return summed

def diag_kernel(coef, rate, length):
    steps = jnp.arange(length).astype(coef.dtype)
    return lax.optimization_barrier(jnp.sum(coef[:, :, None] * jnp.exp(-rate[:, :, None] * steps), axis=1))

def causal_conv(signal, kernel):
    length = signal.shape[1]
    signal_spec = jnp.fft.rfft(signal, n=2 * length, axis=1)
    kernel_spec = jnp.fft.rfft(kernel, n=2 * length, axis=1)
    joined = signal_spec * jnp.transpose(kernel_spec)[None]
    return jnp.fft.irfft(joined, n=2 * length, axis=1)[:, :length, :]

def forward(rows_in, mask_rows, gain_one, w_query, w_key, w_value, w_out, gain_two, w_up, w_down, shift_taps, diag_coef, diag_rate):
    live_mask = mask_rows[:, :, None]
    a_one = low(layer_norm(rows_in, gain_one))
    query_rows = low_back(project(a_one, w_query))
    key_rows = low(low_back(project(a_one, w_key) * live_mask))
    value_rows = low(low_back(project(a_one, w_value) * live_mask))
    shifted = shift_conv(key_rows, shift_taps)
    mixed = low(low_back(shifted * value_rows))
    kernel = diag_kernel(diag_coef, diag_rate, rows_in.shape[1])
    state = low(low_back(causal_conv(mixed, kernel)))
    gated_rows = low(query_rows * state)
    hidden = rows_in + live_mask * low_back(project(gated_rows, w_out))
    a_two = low(layer_norm(hidden, gain_two))
    activation = low(jax.nn.gelu(low_back(project(a_two, w_up)), approximate=False))
    return hidden + live_mask * low_back(project(activation, w_down))

def reference(tokens, lengths, gain_one, w_query, w_key, w_value, w_out, gain_two, w_up, w_down, shift_taps, diag_coef, diag_rate, cotangent):
    positions = jnp.arange(LENGTH).astype(jnp.int32)
    live_mask = (positions[None, :] < lengths[:, None].astype(jnp.int32)).astype(jnp.float32)
    weights = (gain_one, w_query.astype(jnp.float32), w_key.astype(jnp.float32), w_value.astype(jnp.float32), w_out.astype(jnp.float32), gain_two, w_up.astype(jnp.float32), w_down.astype(jnp.float32), shift_taps, diag_coef, diag_rate)
    groups = ROWS // ROWS_DEV
    batches = (tokens.reshape(groups, ROWS_DEV, LENGTH, D), live_mask.reshape(groups, ROWS_DEV, LENGTH), cotangent.reshape(groups, ROWS_DEV, LENGTH, D))

    def group_step(carry, batch_rows):
        token_rows, mask_rows, grad_rows = batch_rows

        def run(rows_in, *params):
            return forward(rows_in, mask_rows, *params)
        result, pullback = jax.vjp(run, token_rows.astype(jnp.float32), *weights)
        grads = pullback(grad_rows.astype(jnp.float32))
        carry = tuple((summed + piece for summed, piece in zip(carry, grads[1:])))
        return (carry, (result.astype(jnp.bfloat16), grads[0].astype(jnp.bfloat16)))
    initial = tuple((jnp.zeros_like(item) for item in weights))
    sums, (results, d_rows) = lax.scan(group_step, initial, batches)
    return (results.reshape(ROWS, LENGTH, D), d_rows.reshape(ROWS, LENGTH, D), sums[0], sums[1], sums[2], sums[3], sums[4], sums[5], sums[6], sums[7], sums[8], sums[9], sums[10])
```

```python
import functools
import math

import jax
import jax.numpy as jnp
import numpy as np
from jax import lax
from jax.experimental import pallas as pl
from jax.experimental.pallas import tpu as pltpu
from jax.sharding import PartitionSpec as P

BLOCK = 256
CHUNK = 16
LANES = 128
EPS = 1e-05
F32 = jnp.float32
BF16 = jnp.bfloat16
VMEM_BYTES = 60 * 1024 * 1024


def dot(a, b):
    return lax.dot_general(a, b, (((1,), (0,)), ((), ())), preferred_element_type=F32)


def dot_nt(a, b):
    return lax.dot_general(a, b, (((1,), (1,)), ((), ())), preferred_element_type=F32)


def dot_tn(a, b):
    return lax.dot_general(a, b, (((0,), (0,)), ((), ())), preferred_element_type=F32)


def params():
    return pltpu.CompilerParams(vmem_limit_bytes=VMEM_BYTES)


def cost(flops, byte_count):
    return pl.CostEstimate(flops=int(flops), bytes_accessed=int(byte_count), transcendentals=0)


def transform_tables():
    freq = np.concatenate([np.arange(0, BLOCK, 2), np.arange(1, BLOCK, 2)]).astype(np.float64)
    time = np.arange(BLOCK, dtype=np.float64)
    angle = (2.0 * math.pi / (2 * BLOCK)) * (freq[:, None] + 0.5) * time[None, :]
    table = np.concatenate([np.cos(angle), -np.sin(angle)], axis=0)
    return jnp.asarray(table, dtype=BF16), jnp.asarray(table.T.copy(), dtype=BF16)


def norm_stats(rows):
    center = rows - jnp.mean(rows, axis=-1, keepdims=True)
    spread = jnp.mean(center * center, axis=-1, keepdims=True)
    inv = lax.rsqrt(spread + EPS)
    return center * inv, inv


def norm_pull(grad, normed, inv, gain):
    scaled = grad * gain
    mean_one = jnp.mean(scaled, axis=-1, keepdims=True)
    mean_two = jnp.mean(scaled * normed, axis=-1, keepdims=True)
    return (scaled - mean_one - normed * mean_two) * inv


def live_rows(length, first, count):
    rows = lax.broadcasted_iota(jnp.int32, (count, 1), 0) + first
    return (rows < length).astype(F32)


def spectral_loop(channels, body):
    half = BLOCK // 2
    for parity in range(2):
        sign = 1.0 if parity == 0 else -1.0
        for lane in range(channels // LANES):
            lanes = slice(lane * LANES, (lane + 1) * LANES)

            def step(index, carry, sign=sign, lanes=lanes, parity=parity):
                low = pl.multiple_of(parity * half + index * CHUNK, CHUNK)
                body(sign, pl.ds(low, CHUNK), pl.ds(low + BLOCK, CHUNK), lanes)
                return carry

            lax.fori_loop(0, half // CHUNK, step, 0)


def multiply(ar, ai, br, bi):
    return ar * br - ai * bi, ar * bi + ai * br


def multiply_conj(ar, ai, br, bi):
    return ar * br + ai * bi, ar * bi - ai * br


def spectra_body(coef_ref, rate_ref, taps_ref, table_ref, kern_out, taps_out, near, far, taps_time, spec):
    states, channels = coef_ref.shape
    blocks = kern_out.shape[0]
    length = blocks * BLOCK
    step_count = 32
    groups = length // step_count
    together = 8
    near_time = lax.broadcasted_iota(jnp.int32, (step_count, 1), 0).astype(F32)
    far_time = lax.broadcasted_iota(jnp.int32, (groups, 1), 0).astype(F32) * step_count

    def fill(n, carry):
        rate = rate_ref[pl.ds(n, 1), :]
        near[n] = jnp.exp(-rate * near_time)
        steps = coef_ref[pl.ds(n, 1), :] * jnp.exp(-rate * far_time)
        for g in range(groups // together):
            far[g, n] = steps[g * together : (g + 1) * together, :]
        return carry

    lax.fori_loop(0, states, fill, 0)
    for lane in range(channels // LANES):
        lanes = slice(lane * LANES, (lane + 1) * LANES)

        def group_step(g, carry, lanes=lanes):
            def add(n, sums):
                near_n = near[n, :, lanes]
                return tuple(
                    sums[i] + far[g, n, i : i + 1, lanes] * near_n for i in range(together)
                )

            zeros = tuple(jnp.zeros((step_count, LANES), F32) for _ in range(together))
            sums = lax.fori_loop(0, states, add, zeros, unroll=4)
            for i in range(together):
                place = pl.multiple_of((g * together + i) * step_count, step_count)
                taps_time[pl.ds(place, step_count), lanes] = sums[i].astype(BF16)
            return carry

        lax.fori_loop(0, groups // together, group_step, 0)
    for j in range(blocks):
        spec[j] = dot(table_ref[...], taps_time[j * BLOCK : (j + 1) * BLOCK, :])
    scale = 1.0 / BLOCK

    def combine(sign, re, im, lanes):
        for j in range(blocks):
            out_re = spec[j, re, lanes]
            out_im = spec[j, im, lanes]
            if j > 0:
                out_re = out_re - sign * spec[j - 1, im, lanes]
                out_im = out_im + sign * spec[j - 1, re, lanes]
            kern_out[j, re, lanes] = out_re * scale
            kern_out[j, im, lanes] = out_im * scale

    spectral_loop(channels, combine)
    taps_out[...] = dot(table_ref[:, : taps_ref.shape[0]], taps_ref[...].astype(BF16)) * scale


def spectra_call(coef, rate, taps, table, length, tile):
    states, channels = coef.shape
    blocks = length // BLOCK
    column = lambda j: (0, j)
    return pl.pallas_call(
        spectra_body,
        grid=(channels // tile,),
        in_specs=[
            pl.BlockSpec((states, tile), column),
            pl.BlockSpec((states, tile), column),
            pl.BlockSpec((taps.shape[0], tile), column),
            pl.BlockSpec(table.shape, lambda j: (0, 0)),
        ],
        out_specs=[
            pl.BlockSpec((blocks, 2 * BLOCK, tile), lambda j: (0, 0, j)),
            pl.BlockSpec((2 * BLOCK, tile), column),
        ],
        out_shape=[
            jax.ShapeDtypeStruct((blocks, 2 * BLOCK, channels), F32),
            jax.ShapeDtypeStruct((2 * BLOCK, channels), F32),
        ],
        scratch_shapes=[
            pltpu.VMEM((states, 32, tile), F32),
            pltpu.VMEM((length // 256, states, 8, tile), F32),
            pltpu.VMEM((length, tile), BF16),
            pltpu.VMEM((blocks, 2 * BLOCK, tile), F32),
        ],
        compiler_params=params(),
        cost_estimate=cost(6e9, 20e6),
        name="spectra",
    )(coef, rate, taps, table)


def mixer_body(
    length_ref, x_ref, gain_one_ref, wq_ref, wk_ref, wv_ref, wout_ref, gain_two_ref, kern_ref, tapspec_ref,
    table_ref, back_ref,
    a_one_ref, q_ref, k_ref, v_ref, shifted_ref, mixed_ref, state_ref, gated_ref, hidden_ref, a_two_ref,
    total, spec, prod,
):
    j = pl.program_id(0)
    length, width = x_ref.shape
    tile = q_ref.shape[1]
    blocks = length // BLOCK
    live = length_ref[0]

    @pl.when(j == 0)
    def _():
        for b in range(blocks):
            rows = slice(b * BLOCK, (b + 1) * BLOCK)
            normed, _ = norm_stats(x_ref[rows, :].astype(F32))
            a_one_ref[rows, :] = (normed * gain_one_ref[...]).astype(BF16)
        total[...] = jnp.zeros_like(total)

    for b in range(blocks):
        rows = slice(b * BLOCK, (b + 1) * BLOCK)
        mask = live_rows(live, b * BLOCK, BLOCK)
        a_rows = a_one_ref[rows, :]
        k_ref[rows, :] = (dot(a_rows, wk_ref[...]) * mask).astype(BF16)
        v_ref[rows, :] = (dot(a_rows, wv_ref[...]) * mask).astype(BF16)
        q_ref[rows, :] = dot(a_rows, wq_ref[...]).astype(BF16)
        spec[b] = dot(table_ref[...], k_ref[rows, :])

    def shift_product(sign, re, im, lanes):
        tr = tapspec_ref[re, lanes]
        ti = tapspec_ref[im, lanes]
        before = None
        for b in range(blocks):
            xr = spec[b, re, lanes]
            xi = spec[b, im, lanes]
            if b == 0:
                sr, si = xr, xi
            else:
                sr, si = xr - sign * before[1], xi + sign * before[0]
            before = (xr, xi)
            yr, yi = multiply(sr, si, tr, ti)
            prod[b, re, lanes] = yr.astype(BF16)
            prod[b, im, lanes] = yi.astype(BF16)

    spectral_loop(tile, shift_product)
    for b in range(blocks):
        rows = slice(b * BLOCK, (b + 1) * BLOCK)
        shifted = dot(back_ref[...], prod[b])
        shifted_ref[rows, :] = shifted.astype(BF16)
        mixed_ref[rows, :] = (shifted * v_ref[rows, :].astype(F32)).astype(BF16)
        spec[b] = dot(table_ref[...], mixed_ref[rows, :])

    def state_product(sign, re, im, lanes):
        x = [(spec[b, re, lanes], spec[b, im, lanes]) for b in range(blocks)]
        h = [(kern_ref[b, re, lanes], kern_ref[b, im, lanes]) for b in range(blocks)]
        for i in range(blocks):
            yr, yi = multiply(*x[i], *h[0])
            for d in range(1, i + 1):
                pr, pi = multiply(*x[i - d], *h[d])
                yr, yi = yr + pr, yi + pi
            prod[i, re, lanes] = yr.astype(BF16)
            prod[i, im, lanes] = yi.astype(BF16)

    spectral_loop(tile, state_product)
    for b in range(blocks):
        rows = slice(b * BLOCK, (b + 1) * BLOCK)
        state = dot(back_ref[...], prod[b]).astype(BF16)
        state_ref[rows, :] = state
        gated_ref[rows, :] = (q_ref[rows, :].astype(F32) * state.astype(F32)).astype(BF16)
        total[rows, :] += dot(gated_ref[rows, :], wout_ref[...])

    @pl.when(j == pl.num_programs(0) - 1)
    def _():
        for b in range(blocks):
            rows = slice(b * BLOCK, (b + 1) * BLOCK)
            mask = live_rows(live, b * BLOCK, BLOCK)
            hidden = x_ref[rows, :].astype(F32) + mask * total[rows, :]
            hidden_ref[rows, :] = hidden
            normed, _ = norm_stats(hidden)
            a_two_ref[rows, :] = (normed * gain_two_ref[...]).astype(BF16)


def mixer_call(live, x, gain_one, wq, wk, wv, wout, gain_two, kern, tapspec, tables, tile):
    length, width = x.shape
    blocks = length // BLOCK
    table, back = tables
    whole = lambda j, n: (0, 0)
    column = lambda j, n: (0, j)
    rows_full = pl.BlockSpec((length, width), whole)
    rows_tile = pl.BlockSpec((length, tile), column)
    gain_spec = pl.BlockSpec((1, width), whole)
    low = jax.ShapeDtypeStruct((length, width), BF16)
    return pl.pallas_call(
        mixer_body,
        grid_spec=pltpu.PrefetchScalarGridSpec(
            num_scalar_prefetch=1,
            grid=(width // tile,),
            in_specs=[
                rows_full,
                gain_spec,
                pl.BlockSpec((width, tile), column),
                pl.BlockSpec((width, tile), column),
                pl.BlockSpec((width, tile), column),
                pl.BlockSpec((tile, width), lambda j, n: (j, 0)),
                gain_spec,
                pl.BlockSpec((blocks, 2 * BLOCK, tile), lambda j, n: (0, 0, j)),
                pl.BlockSpec((2 * BLOCK, tile), column),
                pl.BlockSpec(table.shape, whole),
                pl.BlockSpec(back.shape, whole),
            ],
            out_specs=[rows_full] + [rows_tile] * 7 + [rows_full] * 2,
            scratch_shapes=[
                pltpu.VMEM((length, width), F32),
                pltpu.VMEM((blocks, 2 * BLOCK, tile), F32),
                pltpu.VMEM((blocks, 2 * BLOCK, tile), BF16),
            ],
        ),
        out_shape=[low] * 8 + [jax.ShapeDtypeStruct((length, width), F32), low],
        compiler_params=params(),
        cost_estimate=cost(10e9, 30e6),
        name="mixer_forward",
    )(live, x, gain_one, wq, wk, wv, wout, gain_two, kern, tapspec, table, back)


def gelu_pair(x):
    bell = jnp.exp(x * x * -0.5)
    size = jnp.abs(x)
    t = 1.0 / (1.0 + (0.3275911 / math.sqrt(2.0)) * size)
    poly = t * (
        0.5 * 0.254829592
        + t * (0.5 * -0.284496736 + t * (0.5 * 1.421413741 + t * (0.5 * -1.453152027 + t * (0.5 * 1.061405429))))
    )
    tail = poly * bell
    phi = jnp.where(x >= 0.0, 1.0 - tail, tail)
    return x * phi, phi + x * bell * (1.0 / math.sqrt(2.0 * math.pi))


def share_out(grad, send_ref, keep_ref, mine, share):
    bits = [send_ref.shape[i] for i in range(send_ref.ndim - 3)]
    count = math.prod(bits)
    for half, ref in ((0, keep_ref), (1, send_ref)):
        for spot in range(count):
            relative, left, place = 0, spot, []
            for size in reversed(bits):
                place.append(left % size)
                left //= size
            place = place[::-1]
            for axis, bit in enumerate(place):
                relative += bit << axis
            owner = jnp.bitwise_xor(mine, 2 * relative + half)
            low = pl.multiple_of(owner * share, share)
            ref[(*place, 0)] = grad[pl.ds(low, share), :].astype(BF16)


def ffn_body(
    length_ref, place_ref, a_two_ref, cot_ref, hidden_ref, up_ref, down_ref,
    out_ref, d_pre_ref, send_ref, keep_ref, total, act, d_down, grad,
):
    j = pl.program_id(0)
    length, width = a_two_ref.shape
    tile = up_ref.shape[1]
    live = length_ref[0]
    rows_count = 256

    @pl.when(j == 0)
    def _():
        for low in range(0, length, rows_count):
            rows = slice(low, low + rows_count)
            d_down[rows, :] = (cot_ref[rows, :].astype(F32) * live_rows(live, low, rows_count)).astype(BF16)
        total[...] = jnp.zeros_like(total)

    for low in range(0, length, rows_count):
        rows = slice(low, low + rows_count)
        pre = dot(a_two_ref[rows, :], up_ref[...])
        d_act = dot_nt(d_down[rows, :], down_ref[...])
        value, slope = gelu_pair(pre)
        act[rows, :] = value.astype(BF16)
        d_pre_ref[rows, :] = (d_act * slope).astype(BF16)
        total[rows, :] += dot(act[rows, :], down_ref[...])
    grad[...] = dot_tn(act[...], d_down[...])
    share = tile // 4
    share_out(grad, send_ref.at[:, 0], keep_ref.at[:, 0], place_ref[0] & 3, share)

    @pl.when(j == pl.num_programs(0) - 1)
    def _():
        for low in range(0, length, rows_count):
            rows = slice(low, low + rows_count)
            mask = live_rows(live, low, rows_count)
            out_ref[rows, :] = (hidden_ref[rows, :] + mask * total[rows, :]).astype(BF16)


def ffn_call(live, place, a_two, cot, hidden, up, down):
    length, width = a_two.shape
    hidden_units = up.shape[1]
    tile = hidden_units // 4
    share = tile // 4
    whole = lambda j, n, p: (0, 0)
    rows_full = pl.BlockSpec((length, width), whole)

    def z_place(j, n, p):
        z = jnp.bitwise_xor(j, p[0] >> 2)
        return (0, z & 1, z >> 1, 0, 0)

    half_spec = pl.BlockSpec((2, 1, 1, share, width), z_place)
    half_shape = jax.ShapeDtypeStruct((2, 2, 2, share, width), BF16)
    return pl.pallas_call(
        ffn_body,
        grid_spec=pltpu.PrefetchScalarGridSpec(
            num_scalar_prefetch=2,
            grid=(4,),
            in_specs=[
                rows_full,
                rows_full,
                rows_full,
                pl.BlockSpec((width, tile), lambda j, n, p: (0, j)),
                pl.BlockSpec((tile, width), lambda j, n, p: (j, 0)),
            ],
            out_specs=[
                rows_full,
                pl.BlockSpec((length, tile), lambda j, n, p: (0, j)),
                half_spec,
                half_spec,
            ],
            scratch_shapes=[
                pltpu.VMEM((length, width), F32),
                pltpu.VMEM((length, tile), BF16),
                pltpu.VMEM((length, width), BF16),
                pltpu.VMEM((tile, width), F32),
            ],
        ),
        out_shape=[
            jax.ShapeDtypeStruct((length, width), BF16),
            jax.ShapeDtypeStruct((length, hidden_units), BF16),
            half_shape,
            half_shape,
        ],
        compiler_params=params(),
        cost_estimate=cost(8 * length * width * hidden_units, 40e6),
        name="feed_forward",
    )(live, place, a_two, cot, hidden, up, down)


def ffn_back_body(
    length_ref, place_ref, a_two_ref, d_pre_ref, up_ref, cot_ref, hidden_ref, gain_ref,
    d_hidden_ref, d_mixer_ref, gain_grad_ref, send_ref, keep_ref, total, grad,
):
    j = pl.program_id(0)
    length, width = a_two_ref.shape
    live = length_ref[0]
    rows_count = 256
    grad[...] = dot_tn(a_two_ref[...], d_pre_ref[...])
    share_out(grad, send_ref, keep_ref, place_ref[0], send_ref.shape[-2])

    @pl.when(j == 0)
    def _():
        total[...] = jnp.zeros_like(total)

    for low in range(0, length, rows_count):
        rows = slice(low, low + rows_count)
        total[rows, :] += dot_nt(d_pre_ref[rows, :], up_ref[...])

    @pl.when(j == pl.num_programs(0) - 1)
    def _():
        gain_sum = jnp.zeros((1, width), F32)
        for low in range(0, length, rows_count):
            rows = slice(low, low + rows_count)
            mask = live_rows(live, low, rows_count)
            normed, inv = norm_stats(hidden_ref[rows, :])
            grad_in = total[rows, :]
            gain_sum = gain_sum + jnp.sum(grad_in * normed, axis=0, keepdims=True)
            d_hidden = cot_ref[rows, :].astype(F32) + norm_pull(grad_in, normed, inv, gain_ref[...])
            d_hidden_ref[rows, :] = d_hidden
            d_mixer_ref[rows, :] = (mask * d_hidden).astype(BF16)
        gain_grad_ref[...] = gain_sum


def ffn_back_call(live, place, a_two, d_pre, up, cot, hidden, gain):
    length, width = a_two.shape
    hidden_units = up.shape[1]
    tile = hidden_units // 4
    share = width // 16
    whole = lambda j, n, p: (0, 0)
    rows_full = pl.BlockSpec((length, width), whole)
    half_spec = pl.BlockSpec((2, 2, 2, 1, share, tile), lambda j, n, p: (0, 0, 0, j, 0, 0))
    half_shape = jax.ShapeDtypeStruct((2, 2, 2, 4, share, tile), BF16)
    return pl.pallas_call(
        ffn_back_body,
        grid_spec=pltpu.PrefetchScalarGridSpec(
            num_scalar_prefetch=2,
            grid=(4,),
            in_specs=[
                rows_full,
                pl.BlockSpec((length, tile), lambda j, n, p: (0, j)),
                pl.BlockSpec((width, tile), lambda j, n, p: (0, j)),
                rows_full,
                rows_full,
                pl.BlockSpec((1, width), whole),
            ],
            out_specs=[rows_full, rows_full, pl.BlockSpec((1, width), whole), half_spec, half_spec],
            scratch_shapes=[pltpu.VMEM((length, width), F32), pltpu.VMEM((width, tile), F32)],
        ),
        out_shape=[
            jax.ShapeDtypeStruct((length, width), F32),
            jax.ShapeDtypeStruct((length, width), BF16),
            jax.ShapeDtypeStruct((1, width), F32),
            half_shape,
            half_shape,
        ],
        compiler_params=params(),
        cost_estimate=cost(4 * length * width * hidden_units, 40e6),
        name="feed_forward_back",
    )(live, place, a_two, d_pre, up, cot, hidden, gain)


def gate_back_body(
    place_ref, d_mixer_ref, wout_ref, state_ref, q_ref, gated_ref, a_one_ref,
    d_query_ref, d_state_ref, send_ref, keep_ref, grad,
):
    length, width = d_mixer_ref.shape
    rows_count = 256
    share = width // 16
    mine = place_ref[0]
    grad[...] = dot_tn(gated_ref[...], d_mixer_ref[...])
    share_out(grad, send_ref.at[:, :, :, 0:1], keep_ref.at[:, :, :, 0:1], mine, share)
    for low in range(0, length, rows_count):
        rows = slice(low, low + rows_count)
        d_gated = dot_nt(d_mixer_ref[rows, :], wout_ref[...])
        d_query_ref[rows, :] = (d_gated * state_ref[rows, :].astype(F32)).astype(BF16)
        d_state_ref[rows, :] = (d_gated * q_ref[rows, :].astype(F32)).astype(BF16)
    grad[...] = dot_tn(a_one_ref[...], d_query_ref[...])
    share_out(grad, send_ref.at[:, :, :, 1:2], keep_ref.at[:, :, :, 1:2], mine, share)


def gate_back_call(place, d_mixer, wout, state, q, gated, a_one):
    length, width = d_mixer.shape
    share = width // 16
    whole = lambda i, p: (0, 0)
    rows_full = pl.BlockSpec((length, width), whole)
    half_spec = pl.BlockSpec((2, 2, 2, 2, share, width), lambda i, p: (0, 0, 0, 0, 0, 0))
    half_shape = jax.ShapeDtypeStruct((2, 2, 2, 2, share, width), BF16)
    low = jax.ShapeDtypeStruct((length, width), BF16)
    return pl.pallas_call(
        gate_back_body,
        grid_spec=pltpu.PrefetchScalarGridSpec(
            num_scalar_prefetch=1,
            grid=(1,),
            in_specs=[rows_full, pl.BlockSpec(wout.shape, whole)] + [rows_full] * 4,
            out_specs=[rows_full, rows_full, half_spec, half_spec],
            scratch_shapes=[pltpu.VMEM((width, width), F32)],
        ),
        out_shape=[low, low, half_shape, half_shape],
        compiler_params=params(),
        cost_estimate=cost(6 * length * width * width, 15e6),
        name="gate_back",
    )(place, d_mixer, wout, state, q, gated, a_one)


def mixer_back_body(
    length_ref, place_ref, d_state_ref, d_query_ref, mixed_ref, shifted_ref, k_ref, v_ref, a_one_ref,
    wq_ref, wk_ref, wv_ref, kern_ref, tapspec_ref, table_ref, back_ref, x_ref, gain_ref, d_hidden_ref,
    d_x_ref, gain_grad_ref, d_taps_ref, send_ref, keep_ref, dk_send_ref, dk_keep_ref,
    total, spec_one, spec_two, prod, kern_prod, d_keys, d_values, grad, d_kern,
):
    j = pl.program_id(0)
    length, width = a_one_ref.shape
    tile = k_ref.shape[1]
    blocks = length // BLOCK
    live = length_ref[0]
    mine = place_ref[0]

    for b in range(blocks):
        rows = slice(b * BLOCK, (b + 1) * BLOCK)
        spec_one[b] = dot(table_ref[...], d_state_ref[rows, :])
        spec_two[b] = dot(table_ref[...], mixed_ref[rows, :])

    def state_product(sign, re, im, lanes):
        s = [(spec_one[b, re, lanes], spec_one[b, im, lanes]) for b in range(blocks)]
        h = [(kern_ref[b, re, lanes], kern_ref[b, im, lanes]) for b in range(blocks)]
        for b in range(blocks):
            yr, yi = multiply_conj(*h[0], *s[b])
            for i in range(b + 1, blocks):
                pr, pi = multiply_conj(*h[i - b], *s[i])
                yr, yi = yr + pr, yi + pi
            prod[b, re, lanes] = yr.astype(BF16)
            prod[b, im, lanes] = yi.astype(BF16)

    spectral_loop(tile, state_product)

    def kernel_product(sign, re, im, lanes):
        s = [(spec_one[b, re, lanes], spec_one[b, im, lanes]) for b in range(blocks)]
        x = [(spec_two[b, re, lanes], spec_two[b, im, lanes]) for b in range(blocks)]
        after = None
        for d in range(blocks - 1, -1, -1):
            yr, yi = multiply_conj(*x[0], *s[d])
            for i in range(d + 1, blocks):
                pr, pi = multiply_conj(*x[i - d], *s[i])
                yr, yi = yr + pr, yi + pi
            if after is None:
                hr, hi = yr, yi
            else:
                hr, hi = yr + sign * after[1], yi - sign * after[0]
            after = (yr, yi)
            kern_prod[d, re, lanes] = hr.astype(BF16)
            kern_prod[d, im, lanes] = hi.astype(BF16)

    spectral_loop(tile, kernel_product)
    for b in range(blocks):
        rows = slice(b * BLOCK, (b + 1) * BLOCK)
        mask = live_rows(live, b * BLOCK, BLOCK)
        d_mixed = dot(back_ref[...], prod[b]).astype(BF16).astype(F32)
        d_values[rows, :] = (mask * d_mixed * shifted_ref[rows, :].astype(F32)).astype(BF16)
        d_shifted = (d_mixed * v_ref[rows, :].astype(F32)).astype(BF16)
        spec_one[b] = dot(table_ref[...], d_shifted)
        spec_two[b] = dot(table_ref[...], k_ref[rows, :])
        d_kern[rows, :] = dot(back_ref[...], kern_prod[b]) * (1.0 / BLOCK)

    def shift_product(sign, re, im, lanes):
        tr = tapspec_ref[re, lanes]
        ti = tapspec_ref[im, lanes]
        s = [(spec_one[b, re, lanes], spec_one[b, im, lanes]) for b in range(blocks)]
        x = [(spec_two[b, re, lanes], spec_two[b, im, lanes]) for b in range(blocks)]
        u = [multiply_conj(tr, ti, *s[b]) for b in range(blocks)]
        sum_re, sum_im = multiply_conj(*x[0], *s[0])
        for b in range(blocks):
            yr, yi = u[b]
            if b < blocks - 1:
                yr, yi = yr + sign * u[b + 1][1], yi - sign * u[b + 1][0]
            prod[b, re, lanes] = yr.astype(BF16)
            prod[b, im, lanes] = yi.astype(BF16)
            if b > 0:
                wr = x[b][0] - sign * x[b - 1][1]
                wi = x[b][1] + sign * x[b - 1][0]
                pr, pi = multiply_conj(wr, wi, *s[b])
                sum_re, sum_im = sum_re + pr, sum_im + pi
        kern_prod[0, re, lanes] = sum_re.astype(BF16)
        kern_prod[0, im, lanes] = sum_im.astype(BF16)

    spectral_loop(tile, shift_product)
    for b in range(blocks):
        rows = slice(b * BLOCK, (b + 1) * BLOCK)
        mask = live_rows(live, b * BLOCK, BLOCK)
        d_keys[rows, :] = (mask * dot(back_ref[...], prod[b])).astype(BF16)
    taps = d_taps_ref.shape[0]
    d_taps_ref[...] = dot(back_ref[:taps, :], kern_prod[0]) * (1.0 / BLOCK)

    share_out(d_kern, dk_send_ref, dk_keep_ref, mine, length // 16)
    share = width // 16
    grad[...] = dot_tn(a_one_ref[...], d_keys[...])
    share_out(grad, send_ref.at[:, :, :, 0:1], keep_ref.at[:, :, :, 0:1], mine, share)
    grad[...] = dot_tn(a_one_ref[...], d_values[...])
    share_out(grad, send_ref.at[:, :, :, 1:2], keep_ref.at[:, :, :, 1:2], mine, share)

    @pl.when(j == 0)
    def _():
        total[...] = jnp.zeros_like(total)

    for b in range(blocks):
        rows = slice(b * BLOCK, (b + 1) * BLOCK)
        total[rows, :] += (
            dot_nt(d_query_ref[rows, :], wq_ref[...])
            + dot_nt(d_keys[rows, :], wk_ref[...])
            + dot_nt(d_values[rows, :], wv_ref[...])
        )

    @pl.when(j == pl.num_programs(0) - 1)
    def _():
        gain_sum = jnp.zeros((1, width), F32)
        for b in range(blocks):
            rows = slice(b * BLOCK, (b + 1) * BLOCK)
            normed, inv = norm_stats(x_ref[rows, :].astype(F32))
            grad_in = total[rows, :]
            gain_sum = gain_sum + jnp.sum(grad_in * normed, axis=0, keepdims=True)
            d_x_ref[rows, :] = (d_hidden_ref[rows, :] + norm_pull(grad_in, normed, inv, gain_ref[...])).astype(BF16)
        gain_grad_ref[...] = gain_sum


def mixer_back_call(
    live, place, d_state, d_query, mixed, shifted, k, v, a_one, wq, wk, wv, kern, tapspec, tables, x, gain, d_hidden,
    taps_count, tile
):
    length, width = a_one.shape
    blocks = length // BLOCK
    table, back = tables
    share = width // 16
    whole = lambda j, n, p: (0, 0)
    column = lambda j, n, p: (0, j)
    rows_full = pl.BlockSpec((length, width), whole)
    rows_tile = pl.BlockSpec((length, tile), column)
    weight = pl.BlockSpec((width, tile), column)
    half_spec = pl.BlockSpec((2, 2, 2, 2, share, tile), lambda j, n, p: (0, 0, 0, 0, 0, j))
    half_shape = jax.ShapeDtypeStruct((2, 2, 2, 2, share, width), BF16)
    kern_spec = pl.BlockSpec((2, 2, 2, 1, length // 16, tile), lambda j, n, p: (0, 0, 0, 0, 0, j))
    kern_shape = jax.ShapeDtypeStruct((2, 2, 2, 1, length // 16, width), BF16)
    spectrum = pltpu.VMEM((blocks, 2 * BLOCK, tile), F32)
    spectrum_low = pltpu.VMEM((blocks, 2 * BLOCK, tile), BF16)
    return pl.pallas_call(
        mixer_back_body,
        grid_spec=pltpu.PrefetchScalarGridSpec(
            num_scalar_prefetch=2,
            grid=(width // tile,),
            in_specs=[rows_tile] * 6
            + [rows_full, weight, weight, weight]
            + [
                pl.BlockSpec((blocks, 2 * BLOCK, tile), lambda j, n, p: (0, 0, j)),
                pl.BlockSpec((2 * BLOCK, tile), column),
                pl.BlockSpec(table.shape, whole),
                pl.BlockSpec(back.shape, whole),
                rows_full,
                pl.BlockSpec((1, width), whole),
                rows_full,
            ],
            out_specs=[
                rows_full,
                pl.BlockSpec((1, width), whole),
                pl.BlockSpec((taps_count, tile), column),
                half_spec,
                half_spec,
                kern_spec,
                kern_spec,
            ],
            scratch_shapes=[
                pltpu.VMEM((length, width), F32),
                spectrum,
                spectrum,
                spectrum_low,
                spectrum_low,
                pltpu.VMEM((length, tile), BF16),
                pltpu.VMEM((length, tile), BF16),
                pltpu.VMEM((width, tile), F32),
                pltpu.VMEM((length, tile), F32),
            ],
        ),
        out_shape=[
            jax.ShapeDtypeStruct((length, width), BF16),
            jax.ShapeDtypeStruct((1, width), F32),
            jax.ShapeDtypeStruct((taps_count, width), F32),
            half_shape,
            half_shape,
            kern_shape,
            kern_shape,
        ],
        compiler_params=params(),
        cost_estimate=cost(16e9, 40e6),
        name="mixer_back",
    )(
        live, place, d_state, d_query, mixed, shifted, k, v, a_one, wq, wk, wv, kern, tapspec, table, back, x, gain,
        d_hidden,
    )


MICRO = 2


epsilon = 1e-05
highest = lax.Precision.HIGHEST


def layer_norm(rows, gain):
    center = rows - jnp.mean(rows, axis=-1, keepdims=True)
    spread = jnp.mean(center * center, axis=-1, keepdims=True)
    return center * lax.rsqrt(spread + epsilon) * gain


def exact_gelu(values):
    return jax.nn.gelu(values, approximate=False)


def project(rows, weight):
    return jnp.einsum("rtd,de->rte", rows, weight, preferred_element_type=jnp.float32)


def project_back(rows, weight):
    return jnp.einsum("rte,de->rtd", rows, weight, preferred_element_type=jnp.float32)


def weight_grad(left, right):
    return jnp.einsum("rtd,rte->de", left, right, preferred_element_type=jnp.float32)


def depth_conv(signal, kernel_taps):
    channels = signal.shape[2]
    return lax.conv_general_dilated(
        signal,
        kernel_taps,
        (1,),
        "VALID",
        dimension_numbers=("NWC", "WIO", "NWC"),
        feature_group_count=channels,
        precision=highest,
    )


def shift_conv(extended, taps, length):
    flipped = jnp.transpose(taps[:, ::-1])[:, None, :]
    return depth_conv(extended[:, 1:, :], flipped)[:, :length, :]


def shift_back(extended, taps, length):
    forward_taps = jnp.transpose(taps)[:, None, :]
    return depth_conv(extended, forward_taps)[:, :length, :]


def taps_grad(grad_rows, extended, width_taps):
    rows_count, span, channels = extended.shape
    left = jnp.transpose(extended, (2, 0, 1)).reshape(1, channels * rows_count, span)
    right = jnp.transpose(grad_rows, (2, 0, 1))
    result = lax.conv_general_dilated(
        left,
        right,
        (1,),
        "VALID",
        dimension_numbers=("NCW", "OIW", "NCW"),
        feature_group_count=channels,
        precision=highest,
    )
    return result[0][:, ::-1][:, :width_taps]


def diag_kernel(coef, rate, length):
    steps = lax.iota(jnp.float32, length)
    return jnp.sum(coef[:, :, None] * jnp.exp(-rate[:, :, None] * steps), axis=1)


def dft_tables(length):
    period = 2 * length
    time_index = lax.iota(jnp.int32, length)[:, None]
    freq_index = lax.iota(jnp.int32, length + 1)[None, :]
    phase_index = time_index * freq_index % period
    angles = phase_index.astype(jnp.float32) * (2.0 * math.pi / period)
    cos_table = jnp.cos(angles)
    sin_table = jnp.sin(angles)
    edges = (freq_index == 0) | (freq_index == length)
    weights = jnp.where(edges, 1.0, 2.0).astype(jnp.float32) / period
    return (cos_table, sin_table, cos_table * weights, sin_table * weights)


def spectrum(signal, cos_table, sin_table):
    real_part = jnp.einsum("rtc,tf->rfc", signal, cos_table, precision=highest)
    imag_part = -jnp.einsum("rtc,tf->rfc", signal, sin_table, precision=highest)
    return (real_part, imag_part)


def inverse(real_part, imag_part, cos_weighted, sin_weighted):
    first = jnp.einsum("rfc,tf->rtc", real_part, cos_weighted, precision=highest)
    second = jnp.einsum("rfc,tf->rtc", imag_part, sin_weighted, precision=highest)
    return first - second


def split_channels(
    tokens,
    lengths,
    gain_one,
    w_query,
    w_key,
    w_value,
    w_out,
    gain_two,
    w_up,
    w_down,
    shift_taps,
    diag_coef,
    diag_rate,
    cotangent,
):
    rows_dev, tok_len, model_width = tokens.shape
    length = tok_len * lax.axis_size("seq")
    width_taps = shift_taps.shape[1]
    first_pos = lax.axis_index("seq") * tok_len
    positions = first_pos + lax.iota(jnp.int32, tok_len)
    mask_all = (positions[None, :] < lengths[:, None]).astype(jnp.float32)[:, :, None]
    cos_table, sin_table, cos_weighted, sin_weighted = dft_tables(length)

    def kernel_of(coef_in, rate_in):
        return diag_kernel(coef_in, rate_in, length)

    kernel, kernel_pull = jax.vjp(kernel_of, diag_coef, diag_rate)
    kernel_real = jnp.einsum("ct,tf->fc", kernel, cos_table, precision=highest)
    kernel_imag = -jnp.einsum("ct,tf->fc", kernel, sin_table, precision=highest)
    taps_acc = jnp.zeros(shift_taps.shape, jnp.float32)
    spec_real_acc = jnp.zeros((length + 1, shift_taps.shape[0]), jnp.float32)
    spec_imag_acc = jnp.zeros((length + 1, shift_taps.shape[0]), jnp.float32)
    grad_gain_one = jnp.zeros(gain_one.shape, jnp.float32)
    grad_gain_two = jnp.zeros(gain_two.shape, jnp.float32)
    grad_query = jnp.zeros(w_query.shape, jnp.float32)
    grad_key = jnp.zeros(w_key.shape, jnp.float32)
    grad_value = jnp.zeros(w_value.shape, jnp.float32)
    grad_out = jnp.zeros(w_out.shape, jnp.float32)
    grad_up = jnp.zeros(w_up.shape, jnp.float32)
    grad_down = jnp.zeros(w_down.shape, jnp.float32)
    rows_mb = rows_dev // MICRO
    out_list = []
    dx_list = []
    for micro_step in range(MICRO):
        low_row = micro_step * rows_mb
        x_rows = tokens[low_row : low_row + rows_mb].astype(jnp.float32)
        live_mask = mask_all[low_row : low_row + rows_mb]
        grad_rows = cotangent[low_row : low_row + rows_mb].astype(jnp.float32)
        norm_one, norm_one_pull = jax.vjp(layer_norm, x_rows, gain_one)
        a_one = norm_one.astype(jnp.bfloat16)
        query_rows = project(a_one, w_query)
        key_rows = (project(a_one, w_key) * live_mask).astype(jnp.bfloat16)
        value_rows = (project(a_one, w_value) * live_mask).astype(jnp.bfloat16)
        keys_ch, values_ch = (
            lax.all_to_all(key_rows, "seq", split_axis=2, concat_axis=1, tiled=True),
            lax.all_to_all(value_rows, "seq", split_axis=2, concat_axis=1, tiled=True),
        )
        key_ext = jnp.pad(keys_ch.astype(jnp.float32), ((0, 0), (width_taps, 0), (0, 0)))
        shifted = shift_conv(key_ext, shift_taps, length)
        values_here = values_ch.astype(jnp.float32)
        mixed_ch = (shifted * values_here).astype(jnp.bfloat16)
        mixed_real, mixed_imag = spectrum(mixed_ch.astype(jnp.float32), cos_table, sin_table)
        state = inverse(
            mixed_real * kernel_real - mixed_imag * kernel_imag,
            mixed_real * kernel_imag + mixed_imag * kernel_real,
            cos_weighted,
            sin_weighted,
        )
        state_tok = lax.all_to_all(
            state.astype(jnp.bfloat16), "seq", split_axis=1, concat_axis=2, tiled=True
        )
        state_rows = state_tok.astype(jnp.float32)
        gated_rows = (query_rows * state_rows).astype(jnp.bfloat16)
        hidden = x_rows + live_mask * project(gated_rows, w_out)
        norm_two, norm_two_pull = jax.vjp(layer_norm, hidden, gain_two)
        a_two = norm_two.astype(jnp.bfloat16)
        pre_act = project(a_two, w_up)
        act_value, gelu_pull = jax.vjp(exact_gelu, pre_act)
        activation = act_value.astype(jnp.bfloat16)
        result = hidden + live_mask * project(activation, w_down)
        out_list.append(result.astype(jnp.bfloat16))
        d_down = (live_mask * grad_rows).astype(jnp.bfloat16)
        grad_down = grad_down + weight_grad(activation, d_down)
        d_act = project_back(d_down, w_down)
        d_pre = gelu_pull(d_act)[0].astype(jnp.bfloat16)
        grad_up = grad_up + weight_grad(a_two, d_pre)
        d_a_two = project_back(d_pre, w_up)
        d_hidden_norm, d_gain_two = norm_two_pull(d_a_two)
        grad_gain_two = grad_gain_two + d_gain_two
        d_hidden = grad_rows + d_hidden_norm
        d_mixer = (live_mask * d_hidden).astype(jnp.bfloat16)
        grad_out = grad_out + weight_grad(gated_rows, d_mixer)
        d_gated = project_back(d_mixer, w_out)
        d_query = (d_gated * state_rows).astype(jnp.bfloat16)
        d_state = (d_gated * query_rows).astype(jnp.bfloat16)
        d_state_ch = lax.all_to_all(d_state, "seq", split_axis=2, concat_axis=1, tiled=True)
        grad_real, grad_imag = spectrum(d_state_ch.astype(jnp.float32), cos_table, sin_table)
        d_mixed = inverse(
            kernel_real * grad_real + kernel_imag * grad_imag,
            kernel_real * grad_imag - kernel_imag * grad_real,
            cos_weighted,
            sin_weighted,
        )
        spec_real_acc = spec_real_acc + jnp.sum(
            mixed_real * grad_real + mixed_imag * grad_imag, axis=0
        )
        spec_imag_acc = spec_imag_acc + jnp.sum(
            mixed_real * grad_imag - mixed_imag * grad_real, axis=0
        )
        d_mixed_low = d_mixed.astype(jnp.bfloat16)
        d_mix_ch = d_mixed_low.astype(jnp.float32)
        d_shifted = d_mix_ch * values_here
        d_values_ch = (d_mix_ch * shifted).astype(jnp.bfloat16)
        grad_ext = jnp.pad(d_shifted, ((0, 0), (0, width_taps), (0, 0)))
        d_keys_ch = shift_back(grad_ext, shift_taps, length).astype(jnp.bfloat16)
        taps_acc = taps_acc + taps_grad(d_shifted, key_ext, width_taps)
        keys_back, values_back = (
            lax.all_to_all(d_keys_ch, "seq", split_axis=1, concat_axis=2, tiled=True),
            lax.all_to_all(d_values_ch, "seq", split_axis=1, concat_axis=2, tiled=True),
        )
        mask_low = live_mask.astype(jnp.bfloat16)
        d_keys = keys_back * mask_low
        d_values = values_back * mask_low
        grad_query = grad_query + weight_grad(a_one, d_query)
        grad_key = grad_key + weight_grad(a_one, d_keys)
        grad_value = grad_value + weight_grad(a_one, d_values)
        d_a_one = (
            project_back(d_query, w_query)
            + project_back(d_keys, w_key)
            + project_back(d_values, w_value)
        )
        d_x_norm, d_gain_one = norm_one_pull(d_a_one)
        grad_gain_one = grad_gain_one + d_gain_one
        dx_list.append((d_hidden + d_x_norm).astype(jnp.bfloat16))
    d_kernel = jnp.einsum("fc,tf->ct", spec_real_acc, cos_weighted, precision=highest) - jnp.einsum(
        "fc,tf->ct", spec_imag_acc, sin_weighted, precision=highest
    )
    d_coef, d_rate = kernel_pull(d_kernel)
    taps_part, coef_part, rate_part = (
        lax.psum_scatter(
            taps_acc.astype(jnp.bfloat16), "dp", scatter_dimension=1, tiled=True
        ).astype(jnp.float32),
        lax.psum_scatter(d_coef.astype(jnp.bfloat16), "dp", scatter_dimension=1, tiled=True).astype(
            jnp.float32
        ),
        lax.psum_scatter(d_rate.astype(jnp.bfloat16), "dp", scatter_dimension=1, tiled=True).astype(
            jnp.float32
        ),
    )
    shares = (
        lax.psum_scatter(
            grad_gain_one.astype(jnp.bfloat16), "dp", scatter_dimension=0, tiled=True
        ).astype(jnp.float32),
        lax.psum_scatter(
            grad_query.astype(jnp.bfloat16), "dp", scatter_dimension=0, tiled=True
        ).astype(jnp.float32),
        lax.psum_scatter(
            grad_key.astype(jnp.bfloat16), "dp", scatter_dimension=0, tiled=True
        ).astype(jnp.float32),
        lax.psum_scatter(
            grad_value.astype(jnp.bfloat16), "dp", scatter_dimension=0, tiled=True
        ).astype(jnp.float32),
        lax.psum_scatter(
            grad_out.astype(jnp.bfloat16), "dp", scatter_dimension=0, tiled=True
        ).astype(jnp.float32),
        lax.psum_scatter(
            grad_gain_two.astype(jnp.bfloat16), "dp", scatter_dimension=0, tiled=True
        ).astype(jnp.float32),
        lax.psum_scatter(
            grad_up.astype(jnp.bfloat16), "dp", scatter_dimension=0, tiled=True
        ).astype(jnp.float32),
        lax.psum_scatter(
            grad_down.astype(jnp.bfloat16), "dp", scatter_dimension=0, tiled=True
        ).astype(jnp.float32),
    )
    totals = (
        lax.psum(shares[0].astype(jnp.bfloat16), "seq").astype(jnp.float32),
        lax.psum(shares[1].astype(jnp.bfloat16), "seq").astype(jnp.float32),
        lax.psum(shares[2].astype(jnp.bfloat16), "seq").astype(jnp.float32),
        lax.psum(shares[3].astype(jnp.bfloat16), "seq").astype(jnp.float32),
        lax.psum(shares[4].astype(jnp.bfloat16), "seq").astype(jnp.float32),
        lax.psum(shares[5].astype(jnp.bfloat16), "seq").astype(jnp.float32),
        lax.psum(shares[6].astype(jnp.bfloat16), "seq").astype(jnp.float32),
        lax.psum(shares[7].astype(jnp.bfloat16), "seq").astype(jnp.float32),
    )
    out_rows = jnp.concatenate(out_list, axis=0)
    dx_rows = jnp.concatenate(dx_list, axis=0)
    return (
        out_rows,
        dx_rows,
        totals[0],
        totals[1],
        totals[2],
        totals[3],
        totals[4],
        totals[5],
        totals[6],
        totals[7],
        taps_part,
        coef_part,
        rate_part,
    )


def add_low(a, b):
    return (a.astype(F32) + b.astype(F32)).astype(BF16)


def swap(value, axis_name, bit):
    count = lax.axis_size(axis_name)
    return lax.ppermute(value, axis_name, [(i, i ^ bit) for i in range(count)])


def halve(value, axis, bit):
    index = [slice(None)] * value.ndim
    index[axis] = 1
    given = swap(value[tuple(index)], "dp", bit)
    index[axis] = 0
    return add_low(value[tuple(index)], given)


def reduce_shares(send, keep, cut):
    joined = add_low(keep, swap(send, "dp", 1))
    axis, low = cut
    cuts = [slice(None)] * joined.ndim
    results = []
    for first in (True, False):
        cuts[axis] = slice(0, low) if first else slice(low, None)
        part = joined[tuple(cuts)]
        if first:
            part = halve(part, 0, 2)
            part = halve(part, 0, 4)
            part = halve(part, 0, 8)
        else:
            part = halve(part, 1, 4)
            part = halve(part, 1, 8)
            part = halve(part, 0, 2)
        part = part.astype(F32) + swap(part, "seq", 1).astype(F32)
        results.append(part)
    return jnp.concatenate(results, axis=axis - 3)


def reduce_small(value, place):
    count = value.shape[0]
    order = jnp.bitwise_xor(lax.iota(jnp.int32, count), place)
    value = jnp.take(value, order, axis=0)
    bit = count // 2
    while bit >= 1:
        value = value[:bit] + swap(value[bit:], "dp", bit)
        bit //= 2
    return value[0]


def whole_row(own, given, side):
    return jnp.where(
        side == 0, jnp.concatenate([own, given], axis=0), jnp.concatenate([given, own], axis=0)
    )


def exchange_rows(rows, side):
    own = lax.dynamic_index_in_dim(rows, side, 0, keepdims=False)
    other = lax.dynamic_index_in_dim(rows, 1 - side, 0, keepdims=False)
    return whole_row(own, swap(other, "seq", 1), side)


def return_rows(row, side):
    half = row.shape[0] // 2
    own = lax.dynamic_slice_in_dim(row, side * half, half, 0)
    other = lax.dynamic_slice_in_dim(row, (1 - side) * half, half, 0)
    given = swap(other, "seq", 1)
    return jnp.where(side == 0, jnp.stack([own, given]), jnp.stack([given, own]))


def split_rows(
    tokens, lengths, gain_one, w_query, w_key, w_value, w_out, gain_two, w_up, w_down,
    shift_taps, diag_coef, diag_rate, cotangent,
):
    side = lax.axis_index("seq")
    mine = lax.axis_index("dp")
    devices = lax.axis_size("dp")
    width = tokens.shape[2]
    length = tokens.shape[1] * 2
    channels, states = diag_coef.shape
    tile = 256
    tables = transform_tables()
    place = jnp.reshape(mine, (1,)).astype(jnp.int32)
    live = lax.dynamic_slice_in_dim(lengths, side, 1, 0)
    x = exchange_rows(tokens, side)
    packed = jnp.stack([diag_coef.T, diag_rate.T, shift_taps.T])
    packed_other = swap(packed, "seq", 1)
    packed_all = jnp.where(
        side == 0,
        jnp.concatenate([packed, packed_other], axis=2),
        jnp.concatenate([packed_other, packed], axis=2),
    )
    coef, rate, taps = packed_all[0], packed_all[1], packed_all[2]
    cot = exchange_rows(cotangent, side)
    kern, tapspec = spectra_call(coef, rate, taps, tables[0], length, tile)
    row_one = gain_one[None, :]
    row_two = gain_two[None, :]
    a_one, q, k, v, shifted, mixed, state, gated, hidden, a_two = mixer_call(
        live, x, row_one, w_query, w_key, w_value, w_out, row_two, kern, tapspec, tables, tile
    )
    out_row, d_pre, down_send, down_keep = ffn_call(live, place, a_two, cot, hidden, w_up, w_down)
    out = return_rows(out_row, side)
    share = w_down.shape[0] // devices
    down = reduce_shares(down_send[:, :, :, None], down_keep[:, :, :, None], (4, 112))
    d_hidden, d_mixer, d_gain_two, up_send, up_keep = ffn_back_call(
        live, place, a_two, d_pre, w_up, cot, hidden, row_two
    )
    up = reduce_shares(up_send, up_keep, (3, 2))
    d_query, d_state, gate_send, gate_keep = gate_back_call(place, d_mixer, w_out, state, q, gated, a_one)
    gate = reduce_shares(gate_send, gate_keep, (3, 1))
    d_row, d_gain_one, d_taps, kv_send, kv_keep, kern_send, kern_keep = mixer_back_call(
        live, place, d_state, d_query, mixed, shifted, k, v, a_one, w_query, w_key, w_value, kern, tapspec, tables,
        x, row_one, d_hidden, states, tile,
    )
    d_tokens = return_rows(d_row, side)
    d_kern = reduce_shares(kern_send, kern_keep, (4, 32))[0]
    kv = reduce_shares(kv_send, kv_keep, (3, 1))

    d_kern_half = lax.dynamic_slice_in_dim(d_kern, side * channels, channels, 1)
    steps = (mine * d_kern.shape[0] + lax.iota(jnp.int32, d_kern.shape[0])).astype(F32)
    decay = jnp.exp(-diag_rate.T[None] * steps[:, None, None]) * d_kern_half[:, None, :]
    coef_part = jnp.sum(decay, axis=0)
    rate_part = -diag_coef.T * jnp.sum(decay * steps[:, None, None], axis=0)
    each = states // devices
    pair = jnp.concatenate(
        [coef_part.reshape(devices, each, channels), rate_part.reshape(devices, each, channels)], axis=1
    )
    pair = reduce_small(pair, mine)

    gain_each = width // devices
    gains = jnp.concatenate([d_gain_one.reshape(devices, 1, gain_each), d_gain_two.reshape(devices, 1, gain_each)], axis=2)
    gains = jnp.pad(gains, ((0, 0), (0, 0), (0, width - 2 * gain_each)))
    small = jnp.concatenate([d_taps.reshape(devices, each, width), gains], axis=1)
    small = reduce_small(small, mine)
    small = small + swap(small, "seq", 1)
    taps_part = lax.dynamic_slice_in_dim(small[:each], side * channels, channels, 1)
    up_share = jnp.transpose(up, (1, 0, 2)).reshape(up.shape[1], -1)
    return (
        out,
        d_tokens,
        small[each, :gain_each],
        gate[1],
        kv[0],
        kv[1],
        gate[0],
        small[each, gain_each : 2 * gain_each],
        up_share,
        down.reshape(share, width),
        taps_part.T,
        pair[:each].T,
        pair[each:].T,
    )


def solution(mesh):
    in_specs = (
        P("dp", "seq", None),
        P("dp"),
        P(),
        P(),
        P(),
        P(),
        P(),
        P(),
        P(),
        P(),
        P("seq", None),
        P("seq", None),
        P("seq", None),
        P("dp", "seq", None),
    )
    out_specs = (
        P("dp", "seq", None),
        P("dp", "seq", None),
        P("dp"),
        P("dp", None),
        P("dp", None),
        P("dp", None),
        P("dp", None),
        P("dp"),
        P("dp", None),
        P("dp", None),
        P("seq", "dp"),
        P("seq", "dp"),
        P("seq", "dp"),
    )

    def per_device(*args):
        tokens, shift_taps = args[0], args[10]
        rows, positions, width = tokens.shape
        fits = (
            mesh.shape["seq"] == rows == 2
            and mesh.shape["dp"] == 16
            and positions * 2 % BLOCK == 0
            and width % 256 == 0
            and shift_taps.shape[1] <= BLOCK
        )
        return split_rows(*args) if fits else split_channels(*args)

    return jax.shard_map(
        per_device, mesh=mesh, in_specs=in_specs, out_specs=out_specs, check_vma=False
    )
```

```python
import functools
import math

import jax
import jax.numpy as jnp
import numpy as np
from jax import lax
from jax.experimental import pallas as pl
from jax.experimental.pallas import tpu as pltpu
from jax.sharding import PartitionSpec as P

BLOCK = 256
CHUNK = 16
LANES = 128
EPS = 1e-05
F32 = jnp.float32
BF16 = jnp.bfloat16
VMEM_BYTES = 60 * 1024 * 1024


def dot(a, b):
    return lax.dot_general(a, b, (((1,), (0,)), ((), ())), preferred_element_type=F32)


def dot_nt(a, b):
    return lax.dot_general(a, b, (((1,), (1,)), ((), ())), preferred_element_type=F32)


def dot_tn(a, b):
    return lax.dot_general(a, b, (((0,), (0,)), ((), ())), preferred_element_type=F32)


def params():
    return pltpu.CompilerParams(vmem_limit_bytes=VMEM_BYTES)


def cost(flops, byte_count):
    return pl.CostEstimate(flops=int(flops), bytes_accessed=int(byte_count), transcendentals=0)


def transform_tables():
    freq = np.concatenate([np.arange(0, BLOCK, 2), np.arange(1, BLOCK, 2)]).astype(np.float64)
    time = np.arange(BLOCK, dtype=np.float64)
    angle = (2.0 * math.pi / (2 * BLOCK)) * (freq[:, None] + 0.5) * time[None, :]
    table = np.concatenate([np.cos(angle), -np.sin(angle)], axis=0)
    return jnp.asarray(table, dtype=BF16), jnp.asarray(table.T.copy(), dtype=BF16)


def norm_stats(rows):
    center = rows - jnp.mean(rows, axis=-1, keepdims=True)
    spread = jnp.mean(center * center, axis=-1, keepdims=True)
    inv = lax.rsqrt(spread + EPS)
    return center * inv, inv


def norm_pull(grad, normed, inv, gain):
    scaled = grad * gain
    mean_one = jnp.mean(scaled, axis=-1, keepdims=True)
    mean_two = jnp.mean(scaled * normed, axis=-1, keepdims=True)
    return (scaled - mean_one - normed * mean_two) * inv


def live_rows(length, first, count):
    rows = lax.broadcasted_iota(jnp.int32, (count, 1), 0) + first
    return (rows < length).astype(F32)


def spectral_loop(channels, body):
    half = BLOCK // 2
    for parity in range(2):
        sign = 1.0 if parity == 0 else -1.0
        for lane in range(channels // LANES):
            lanes = slice(lane * LANES, (lane + 1) * LANES)

            def step(index, carry, sign=sign, lanes=lanes, parity=parity):
                low = pl.multiple_of(parity * half + index * CHUNK, CHUNK)
                body(sign, pl.ds(low, CHUNK), pl.ds(low + BLOCK, CHUNK), lanes)
                return carry

            lax.fori_loop(0, half // CHUNK, step, 0)


def multiply(ar, ai, br, bi):
    return ar * br - ai * bi, ar * bi + ai * br


def multiply_conj(ar, ai, br, bi):
    return ar * br + ai * bi, ar * bi - ai * br


def spectra_body(coef_ref, rate_ref, taps_ref, table_ref, kern_out, taps_out, near, far, taps_time, spec):
    states, channels = coef_ref.shape
    blocks = kern_out.shape[0]
    length = blocks * BLOCK
    step_count = 32
    groups = length // step_count
    together = 8
    near_time = lax.broadcasted_iota(jnp.int32, (step_count, 1), 0).astype(F32)
    far_time = lax.broadcasted_iota(jnp.int32, (groups, 1), 0).astype(F32) * step_count

    def fill(n, carry):
        rate = rate_ref[pl.ds(n, 1), :]
        near[n] = jnp.exp(-rate * near_time)
        steps = coef_ref[pl.ds(n, 1), :] * jnp.exp(-rate * far_time)
        for g in range(groups // together):
            far[g, n] = steps[g * together : (g + 1) * together, :]
        return carry

    lax.fori_loop(0, states, fill, 0)
    for lane in range(channels // LANES):
        lanes = slice(lane * LANES, (lane + 1) * LANES)

        def group_step(g, carry, lanes=lanes):
            def add(n, sums):
                near_n = near[n, :, lanes]
                return tuple(
                    sums[i] + far[g, n, i : i + 1, lanes] * near_n for i in range(together)
                )

            zeros = tuple(jnp.zeros((step_count, LANES), F32) for _ in range(together))
            sums = lax.fori_loop(0, states, add, zeros, unroll=4)
            for i in range(together):
                place = pl.multiple_of((g * together + i) * step_count, step_count)
                taps_time[pl.ds(place, step_count), lanes] = sums[i].astype(BF16)
            return carry

        lax.fori_loop(0, groups // together, group_step, 0)
    for j in range(blocks):
        spec[j] = dot(table_ref[...], taps_time[j * BLOCK : (j + 1) * BLOCK, :])
    scale = 1.0 / BLOCK

    def combine(sign, re, im, lanes):
        for j in range(blocks):
            out_re = spec[j, re, lanes]
            out_im = spec[j, im, lanes]
            if j > 0:
                out_re = out_re - sign * spec[j - 1, im, lanes]
                out_im = out_im + sign * spec[j - 1, re, lanes]
            kern_out[j, re, lanes] = (out_re * scale).astype(BF16)
            kern_out[j, im, lanes] = (out_im * scale).astype(BF16)

    spectral_loop(channels, combine)
    taps_out[...] = dot(table_ref[:, : taps_ref.shape[0]], taps_ref[...].astype(BF16)) * scale


def spectra_call(coef, rate, taps, table, length, tile):
    states, channels = coef.shape
    blocks = length // BLOCK
    column = lambda j: (0, j)
    return pl.pallas_call(
        spectra_body,
        grid=(channels // tile,),
        in_specs=[
            pl.BlockSpec((states, tile), column),
            pl.BlockSpec((states, tile), column),
            pl.BlockSpec((taps.shape[0], tile), column),
            pl.BlockSpec(table.shape, lambda j: (0, 0)),
        ],
        out_specs=[
            pl.BlockSpec((blocks, 2 * BLOCK, tile), lambda j: (0, 0, j)),
            pl.BlockSpec((2 * BLOCK, tile), column),
        ],
        out_shape=[
            jax.ShapeDtypeStruct((blocks, 2 * BLOCK, channels), BF16),
            jax.ShapeDtypeStruct((2 * BLOCK, channels), F32),
        ],
        scratch_shapes=[
            pltpu.VMEM((states, 32, tile), F32),
            pltpu.VMEM((length // 256, states, 8, tile), F32),
            pltpu.VMEM((length, tile), BF16),
            pltpu.VMEM((blocks, 2 * BLOCK, tile), F32),
        ],
        compiler_params=params(),
        cost_estimate=cost(6e9, 20e6),
        name="spectra",
    )(coef, rate, taps, table)


def mixer_body(
    length_ref, x_ref, gain_one_ref, wq_ref, wk_ref, wv_ref, wout_ref, gain_two_ref, kern_ref, tapspec_ref,
    table_ref, back_ref,
    a_one_ref, q_ref, k_ref, v_ref, shifted_ref, mixed_ref, state_ref, gated_ref, hidden_ref, a_two_ref,
    total, spec, prod,
):
    j = pl.program_id(0)
    length, width = x_ref.shape
    tile = q_ref.shape[1]
    blocks = length // BLOCK
    live = length_ref[0]

    @pl.when(j == 0)
    def _():
        for b in range(blocks):
            rows = slice(b * BLOCK, (b + 1) * BLOCK)
            normed, _ = norm_stats(x_ref[rows, :].astype(F32))
            a_one_ref[rows, :] = (normed * gain_one_ref[...]).astype(BF16)
        total[...] = jnp.zeros_like(total)

    for b in range(blocks):
        rows = slice(b * BLOCK, (b + 1) * BLOCK)
        mask = live_rows(live, b * BLOCK, BLOCK)
        a_rows = a_one_ref[rows, :]
        k_ref[rows, :] = (dot(a_rows, wk_ref[...]) * mask).astype(BF16)
        v_ref[rows, :] = (dot(a_rows, wv_ref[...]) * mask).astype(BF16)
        q_ref[rows, :] = dot(a_rows, wq_ref[...]).astype(BF16)
        spec[b] = dot(table_ref[...], k_ref[rows, :])

    def shift_product(sign, re, im, lanes):
        tr = tapspec_ref[re, lanes]
        ti = tapspec_ref[im, lanes]
        before = None
        for b in range(blocks):
            xr = spec[b, re, lanes]
            xi = spec[b, im, lanes]
            if b == 0:
                sr, si = xr, xi
            else:
                sr, si = xr - sign * before[1], xi + sign * before[0]
            before = (xr, xi)
            yr, yi = multiply(sr, si, tr, ti)
            prod[b, re, lanes] = yr.astype(BF16)
            prod[b, im, lanes] = yi.astype(BF16)

    spectral_loop(tile, shift_product)
    for b in range(blocks):
        rows = slice(b * BLOCK, (b + 1) * BLOCK)
        shifted = dot(back_ref[...], prod[b])
        shifted_ref[rows, :] = shifted.astype(BF16)
        mixed_ref[rows, :] = (shifted * v_ref[rows, :].astype(F32)).astype(BF16)
        spec[b] = dot(table_ref[...], mixed_ref[rows, :])

    def state_product(sign, re, im, lanes):
        x = [(spec[b, re, lanes], spec[b, im, lanes]) for b in range(blocks)]
        h = [(kern_ref[b, re, lanes].astype(F32), kern_ref[b, im, lanes].astype(F32)) for b in range(blocks)]
        for i in range(blocks):
            yr, yi = multiply(*x[i], *h[0])
            for d in range(1, i + 1):
                pr, pi = multiply(*x[i - d], *h[d])
                yr, yi = yr + pr, yi + pi
            prod[i, re, lanes] = yr.astype(BF16)
            prod[i, im, lanes] = yi.astype(BF16)

    spectral_loop(tile, state_product)
    for b in range(blocks):
        rows = slice(b * BLOCK, (b + 1) * BLOCK)
        state = dot(back_ref[...], prod[b]).astype(BF16)
        state_ref[rows, :] = state
        gated_ref[rows, :] = (q_ref[rows, :].astype(F32) * state.astype(F32)).astype(BF16)
        total[rows, :] += dot(gated_ref[rows, :], wout_ref[...])

    @pl.when(j == pl.num_programs(0) - 1)
    def _():
        for b in range(blocks):
            rows = slice(b * BLOCK, (b + 1) * BLOCK)
            mask = live_rows(live, b * BLOCK, BLOCK)
            hidden = x_ref[rows, :].astype(F32) + mask * total[rows, :]
            hidden_ref[rows, :] = hidden
            normed, _ = norm_stats(hidden)
            a_two_ref[rows, :] = (normed * gain_two_ref[...]).astype(BF16)


def mixer_call(live, x, gain_one, wq, wk, wv, wout, gain_two, kern, tapspec, tables, tile):
    length, width = x.shape
    blocks = length // BLOCK
    table, back = tables
    whole = lambda j, n: (0, 0)
    column = lambda j, n: (0, j)
    rows_full = pl.BlockSpec((length, width), whole)
    rows_tile = pl.BlockSpec((length, tile), column)
    gain_spec = pl.BlockSpec((1, width), whole)
    low = jax.ShapeDtypeStruct((length, width), BF16)
    return pl.pallas_call(
        mixer_body,
        grid_spec=pltpu.PrefetchScalarGridSpec(
            num_scalar_prefetch=1,
            grid=(width // tile,),
            in_specs=[
                rows_full,
                gain_spec,
                pl.BlockSpec((width, tile), column),
                pl.BlockSpec((width, tile), column),
                pl.BlockSpec((width, tile), column),
                pl.BlockSpec((tile, width), lambda j, n: (j, 0)),
                gain_spec,
                pl.BlockSpec((blocks, 2 * BLOCK, tile), lambda j, n: (0, 0, j)),
                pl.BlockSpec((2 * BLOCK, tile), column),
                pl.BlockSpec(table.shape, whole),
                pl.BlockSpec(back.shape, whole),
            ],
            out_specs=[rows_full] + [rows_tile] * 7 + [rows_full] * 2,
            scratch_shapes=[
                pltpu.VMEM((length, width), F32),
                pltpu.VMEM((blocks, 2 * BLOCK, tile), F32),
                pltpu.VMEM((blocks, 2 * BLOCK, tile), BF16),
            ],
        ),
        out_shape=[low] * 8 + [jax.ShapeDtypeStruct((length, width), F32), low],
        compiler_params=params(),
        cost_estimate=cost(10e9, 30e6),
        name="mixer_forward",
    )(live, x, gain_one, wq, wk, wv, wout, gain_two, kern, tapspec, table, back)


def gelu_pair(x):
    bell = jnp.exp(x * x * -0.5)
    size = jnp.abs(x)
    t = 1.0 / (1.0 + (0.3275911 / math.sqrt(2.0)) * size)
    poly = t * (
        0.5 * 0.254829592
        + t * (0.5 * -0.284496736 + t * (0.5 * 1.421413741 + t * (0.5 * -1.453152027 + t * (0.5 * 1.061405429))))
    )
    tail = poly * bell
    phi = jnp.where(x >= 0.0, 1.0 - tail, tail)
    return x * phi, phi + x * bell * (1.0 / math.sqrt(2.0 * math.pi))


def bit_of(index, bit):
    return lax.rem(index // bit, 2)


def partner(axis, bit):
    index = lax.axis_index(axis)
    return {axis: index + bit * (1 - 2 * bit_of(index, bit))}


CORE, MIDDLE, NEAR, FAR, SIDE = ("dp", 1), ("dp", 2), ("dp", 4), ("dp", 8), ("seq", 1)


def greet(partners):
    barrier = pltpu.get_barrier_semaphore()
    for axis, bit in partners:
        pl.semaphore_signal(barrier, inc=1, device_id=partner(axis, bit), device_id_type=pl.DeviceIdType.MESH)
    pl.semaphore_wait(barrier, len(partners))


def transfer(source, target, sems, to):
    return pltpu.make_async_remote_copy(
        src_ref=source,
        dst_ref=target,
        send_sem=sems.at[0],
        recv_sem=sems.at[1],
        device_id=partner(*to),
        device_id_type=pl.DeviceIdType.MESH,
    )


def add_into(target, other):
    target[...] = target[...] + other[...]


def owner_bits(mine, relative):
    total = 0
    for bit, differs in relative.items():
        own = bit_of(mine, bit)
        total = total + bit * (1 - own if differs else own)
    return total


def share_all(grad, send, keep, rows, share):
    mine = lax.axis_index("dp")
    for core, ref in ((0, keep), (1, send)):
        for x in range(2):
            for near in range(2):
                for far in range(2):
                    owner = owner_bits(mine, {1: core, 2: x, 4: near, 8: far})
                    low = pl.multiple_of(owner * share, 8)
                    ref[x, near, far, rows, :] = grad[pl.ds(low, share), :].astype(BF16)


class Sum:
    def __init__(self, send, keep, chain, sems, outer, start=0):
        self.send, self.keep, self.chain, self.sems = send, keep, chain, sems
        self.outer, self.start = outer, start

    def given(self, step, half):
        ref = self.chain[step]
        if step == 3:
            return ref
        if self.outer and step in (0, 1):
            return ref.at[:, half]
        return ref.at[half]

    def copy(self, step):
        order = (CORE, NEAR, FAR, MIDDLE, SIDE) if self.outer else (CORE, MIDDLE, NEAR, FAR, SIDE)
        source = self.send if step == self.start else self.given(step - 1, 1)
        return transfer(source, self.chain[step], self.sems.at[step], order[step])

    def begin(self):
        self.copy(self.start).start()

    def add(self, step):
        self.copy(step).wait()
        kept = self.keep if step == self.start else self.given(step - 1, 0)
        add_into(self.chain[step], kept)

    def advance(self, step):
        self.add(step)
        self.copy(step + 1).start()

    def finish(self):
        self.copy(4).wait()
        return self.chain[3][...].astype(F32) + self.chain[4][...].astype(F32)


class Gather:
    def __init__(self, z, source, first, chain, sems):
        self.z, self.source, self.first, self.chain, self.sems = z, source, first, chain, sems
        mine = lax.axis_index("dp")
        self.near = bit_of(mine, 4) == bit_of(z, 1)
        self.far = bit_of(mine, 8) == bit_of(z, 2)

    def copy(self, step):
        if step == self.first:
            source = self.source if step else self.source.at[1]
        else:
            source = self.chain[step - 1]
        return transfer(source, self.chain[step], self.sems.at[step], (MIDDLE, NEAR, FAR, SIDE)[step])

    def both(self):
        return jnp.logical_and(self.near, self.far)

    def step_x(self):
        self.copy(0).wait()
        add_into(self.chain[0], self.source.at[0])

    def send_near(self):
        @pl.when(jnp.logical_not(self.near))
        def _():
            self.copy(1).start()

    def step_near(self):
        kept = self.source if self.first == 1 else self.chain[0]

        @pl.when(jnp.logical_not(self.near))
        def _():
            self.copy(1).wait_send()

        @pl.when(self.near)
        def _():
            self.copy(1).wait_recv()
            add_into(self.chain[1], kept)

        @pl.when(jnp.logical_and(self.near, jnp.logical_not(self.far)))
        def _():
            self.copy(2).start()

    def step_far(self):
        @pl.when(jnp.logical_and(self.near, jnp.logical_not(self.far)))
        def _():
            self.copy(2).wait_send()

        @pl.when(self.both())
        def _():
            self.copy(2).wait_recv()
            add_into(self.chain[2], self.chain[1])
            self.copy(3).start()

    def finish(self, out):
        @pl.when(self.both())
        def _():
            self.copy(3).wait()
            out[...] = self.chain[2][...].astype(F32) + self.chain[3][...].astype(F32)


def ffn_body(
    length_ref, a_two_ref, cot_ref, hidden_ref, gain_ref, up_ref, down_ref,
    out_ref, d_hidden_ref, d_mixer_ref, gain_grad_ref, up_out, down_out, up_two, up_three, down_two, down_three,
    total, back, act, d_pre, d_down, grad,
    up_send, up_keep, up_r0, up_r1, up_r2, up_r3, up_r4, up_sems,
    down_send, down_keep, down_r0, down_r1, down_r2, down_r3, down_r4, down_sems, down_core_sems,
):
    j = pl.program_id(0)
    last = pl.num_programs(0) - 1
    length, width = a_two_ref.shape
    tile = up_ref.shape[1]
    live = length_ref[0]
    rows_count = 256
    share_up, share_down = width // 16, tile // 4

    def early(t):
        return min(t, 1) if isinstance(t, int) else t

    def up_sum(t):
        r1 = up_r1.at[min(t, 2) if isinstance(t, int) else t]
        chain = [up_r0.at[t], r1, up_r2.at[early(t)], up_r3.at[early(t)], up_r4.at[early(t)]]
        return Sum(up_send, up_keep, chain, up_sems.at[t], True)

    def down_core(t):
        return transfer(down_send, down_r0.at[t], down_core_sems.at[t], CORE)

    def down_sum(t):
        chain = [down_r1.at[t], down_r2.at[early(t)], down_r3.at[early(t)], down_r4.at[early(t)]]
        return Gather(t, down_r0.at[t], 0, chain, down_sems.at[t])

    @pl.when(j == 0)
    def _():
        greet((CORE, MIDDLE, NEAR, FAR, SIDE))
        for low in range(0, length, rows_count):
            rows = slice(low, low + rows_count)
            d_down[rows, :] = (cot_ref[rows, :].astype(F32) * live_rows(live, low, rows_count)).astype(BF16)
        total[...] = jnp.zeros_like(total)
        back[...] = jnp.zeros_like(back)
        down_out[...] = jnp.zeros_like(down_out)

    def chunk(low):
        rows = slice(low, low + rows_count)
        pre = dot(a_two_ref[rows, :], up_ref[...])
        d_act = dot_nt(d_down[rows, :], down_ref[...])
        value, slope = gelu_pair(pre)
        act[rows, :] = value.astype(BF16)
        d_pre[rows, :] = (d_act * slope).astype(BF16)
        total[rows, :] += dot(act[rows, :], down_ref[...])
        back[rows, :] += dot_nt(d_pre[rows, :], up_ref[...])

    def join_core(t):
        up_sum(t).add(0)
        down_core(t).wait()
        add_into(down_r0.at[t], down_keep)

    chunk(0)

    @pl.when(j >= 1)
    def _():
        join_core(j - 1)
        up_sum(j - 1).copy(1).start()
        down_sum(j - 1).copy(0).start()

    @pl.when(j >= 2)
    def _():
        up_sum(j - 2).advance(2)
        down_sum(j - 2).step_near()

    chunk(rows_count)

    @pl.when(j >= 2)
    def _():
        up_sum(j - 2).advance(3)

    chunk(2 * rows_count)

    @pl.when(j >= 2)
    def _():
        down_sum(j - 2).step_far()

    chunk(3 * rows_count)

    @pl.when(jnp.logical_and(j >= 1, j < last))
    def _():
        up_sum(j - 1).advance(1)
        down_sum(j - 1).step_x()
        down_sum(j - 1).send_near()

    @pl.when(j == last)
    def _():
        up_sum(2).add(1)
        down_sum(2).step_x()
        up_two[...] = up_r1[2]
        down_two[...] = down_r1[2]

    @pl.when(j >= 2)
    def _():
        up_out[j - 2] = up_sum(j - 2).finish()
        down_sum(j - 2).finish(down_out)

    grad[...] = dot_tn(act[...], d_down[...])
    mine = lax.axis_index("dp")
    for core, ref in ((0, down_keep), (1, down_send)):
        for x in range(2):
            low = pl.multiple_of(owner_bits(mine, {1: core, 2: x}) * share_down, 8)
            ref[x] = grad[pl.ds(low, share_down), :].astype(BF16)
    down_core(j).start()
    grad[...] = dot_tn(a_two_ref[...], d_pre[...])
    share_all(grad, up_send, up_keep, slice(None), share_up)
    up_sum(j).begin()

    @pl.when(j == last)
    def _():
        gain_sum = jnp.zeros((1, width), F32)
        for low in range(0, length, rows_count):
            rows = slice(low, low + rows_count)
            mask = live_rows(live, low, rows_count)
            hidden = hidden_ref[rows, :]
            out_ref[rows, :] = (hidden + mask * total[rows, :]).astype(BF16)
            normed, inv = norm_stats(hidden)
            grad_in = back[rows, :]
            gain_sum = gain_sum + jnp.sum(grad_in * normed, axis=0, keepdims=True)
            d_hidden = cot_ref[rows, :].astype(F32) + norm_pull(grad_in, normed, inv, gain_ref[...])
            d_hidden_ref[rows, :] = d_hidden
            d_mixer_ref[rows, :] = (mask * d_hidden).astype(BF16)
        gain_grad_ref[...] = gain_sum
        join_core(3)
        up_three[...] = up_r0[3]
        down_three[...] = down_r0[3]


def once(shape, index=None):
    zeros = (0,) * len(shape)
    return pl.BlockSpec(shape, index or (lambda *_: zeros), pipeline_mode=pl.Buffered(1))


def ffn_call(live, a_two, cot, hidden, gain, up, down):
    length, width = a_two.shape
    hidden_units = up.shape[1]
    tile = hidden_units // 4
    su, sd = width // 16, tile // 4
    rows_full = once((length, width))
    low = lambda *shape: jax.ShapeDtypeStruct(shape, BF16)
    full = lambda *shape: jax.ShapeDtypeStruct(shape, F32)
    vmem = lambda *shape: pltpu.VMEM(shape, BF16)
    out_shape = [
        low(length, width),
        full(length, width),
        low(length, width),
        full(1, width),
        full(2, su, tile),
        full(sd, width),
        low(2, 2, su, tile),
        low(2, 2, 2, su, tile),
        low(sd, width),
        low(2, sd, width),
    ]
    return pl.pallas_call(
        ffn_body,
        grid=(4,),
        in_specs=[
            pl.BlockSpec(memory_space=pltpu.SMEM),
            rows_full,
            rows_full,
            rows_full,
            once((1, width)),
            pl.BlockSpec((width, tile), lambda j: (0, j)),
            pl.BlockSpec((tile, width), lambda j: (j, 0)),
        ],
        out_specs=[once(s.shape) for s in out_shape],
        out_shape=out_shape,
        scratch_shapes=[
            pltpu.VMEM((length, width), F32),
            pltpu.VMEM((length, width), F32),
            vmem(length, tile),
            vmem(length, tile),
            vmem(length, width),
            pltpu.VMEM((tile, width), F32),
            vmem(2, 2, 2, su, tile),
            vmem(2, 2, 2, su, tile),
            vmem(4, 2, 2, 2, su, tile),
            vmem(3, 2, 2, su, tile),
            vmem(2, 2, su, tile),
            vmem(2, su, tile),
            vmem(2, su, tile),
            pltpu.SemaphoreType.DMA((4, 5, 2)),
            vmem(2, sd, width),
            vmem(2, sd, width),
            vmem(4, 2, sd, width),
            vmem(3, sd, width),
            vmem(2, sd, width),
            vmem(2, sd, width),
            vmem(2, sd, width),
            pltpu.SemaphoreType.DMA((4, 4, 2)),
            pltpu.SemaphoreType.DMA((4, 2)),
        ],
        compiler_params=pltpu.CompilerParams(vmem_limit_bytes=VMEM_BYTES, collective_id=1, has_side_effects=True),
        cost_estimate=cost(12 * length * width * hidden_units, 40e6),
        name="feed_forward",
    )(live, a_two, cot, hidden, gain, up, down)


def mixer_back_body(
    length_ref, out_row_ref, d_mixer_ref, wout_ref, state_ref, q_ref, gated_ref, a_one_ref,
    mixed_ref, shifted_ref, k_ref, v_ref, wq_ref, wk_ref, wv_ref, kern_ref, tapspec_ref, table_ref, back_ref,
    x_ref, gain_ref, d_hidden_ref, up_two_ref, up_three_ref, down_two_ref, down_three_ref, up_part_ref, down_part_ref,
    out_ref, d_tokens_ref, gain_grad_ref, d_taps_ref, up_ref, down_ref, gate_ref, kv_ref, d_kern_ref,
    total, spec_one, spec_two, prod, kern_prod, d_keys, d_values, d_query, d_state, grad, d_kern, d_x,
    up_two_r1, up_two_r2, up_two_r3, up_two_r4, up_three_r1, up_three_r2, up_three_r3, up_three_r4, up_sems,
    down_two_r, down_three_r, down_sems,
    gate_send, gate_keep, gate_r0, gate_r1, gate_r2, gate_r3, gate_r4, gate_sems,
    kv_send, kv_keep, kv_r0, kv_r1, kv_r2, kv_r3, kv_r4, kv_sems,
    out_sems, row_sems, own_sems,
):
    j = pl.program_id(0)
    tiles = pl.num_programs(0)
    length, width = a_one_ref.shape
    half = length // 2
    tile = k_ref.shape[1]
    blocks = length // BLOCK
    share = width // 16
    kern_share = length // 16
    live = length_ref[0]
    side = lax.axis_index("seq")
    columns = pl.ds(pl.multiple_of(j * tile, tile), tile)
    own_rows = pl.ds(pl.multiple_of(side * half, half), half)
    other_rows = pl.ds(pl.multiple_of((1 - side) * half, half), half)

    up_two = Sum(up_two_ref.at[:, 1], up_two_ref.at[:, 0], [None, None, up_two_r2, up_two_r3, up_two_r4], up_sems.at[0], True, 2)
    up_three = Sum(
        up_three_ref.at[:, 1], up_three_ref.at[:, 0], [None, up_three_r1, up_three_r2, up_three_r3, up_three_r4],
        up_sems.at[1], True, 1,
    )
    down_two = Gather(2, down_two_ref, 1, [None] + [down_two_r.at[i] for i in range(1, 4)], down_sems.at[0])
    down_three = Gather(3, down_three_ref, 0, [down_three_r.at[i] for i in range(4)], down_sems.at[1])
    gate = Sum(gate_send, gate_keep, [gate_r0, gate_r1, gate_r2, gate_r3, gate_r4], gate_sems, False)

    def kv(t):
        chain = [kv_r0.at[t], kv_r1.at[t], kv_r2.at[t], kv_r3.at[t], kv_r4.at[t]]
        return Sum(kv_send, kv_keep, chain, kv_sems.at[t], False)

    def kv_finish(t):
        value = kv(t).finish()
        place = slice(t * tile, (t + 1) * tile)
        kv_ref[0, :, place] = value[:share]
        kv_ref[1, :, place] = value[share : 2 * share]
        d_kern_ref[:, place] = value[2 * share :]

    def send_out():
        return transfer(out_row_ref.at[other_rows], out_ref.at[side], out_sems, SIDE)

    def keep_out():
        return pltpu.make_async_copy(out_row_ref.at[own_rows], out_ref.at[side], own_sems.at[0])

    def send_row():
        return transfer(d_x.at[0], d_tokens_ref.at[side], row_sems, SIDE)

    def keep_row():
        return pltpu.make_async_copy(d_x.at[1], d_tokens_ref.at[side], own_sems.at[1])

    @pl.when(j == 0)
    def _():
        greet((CORE, MIDDLE, NEAR, FAR, SIDE))
        up_three.begin()
        up_two.begin()
        down_three.copy(0).start()
        down_two.send_near()
        send_out().start()
        keep_out().start()
        total[:width, :] = dot_tn(gated_ref[...], d_mixer_ref[...])
        share_all(total, gate_send, gate_keep, slice(0, share), share)
        for b in range(blocks):
            rows = slice(b * BLOCK, (b + 1) * BLOCK)
            d_gated = dot_nt(d_mixer_ref[rows, :], wout_ref[...])
            low_query = (d_gated * state_ref[rows, :].astype(F32)).astype(BF16)
            low_state = (d_gated * q_ref[rows, :].astype(F32)).astype(BF16)
            d_query[rows, :] = low_query
            for t in range(width // tile):
                d_state[t, rows, :] = low_state[:, t * tile : (t + 1) * tile]
        total[:width, :] = dot_tn(a_one_ref[...], d_query[...])
        share_all(total, gate_send, gate_keep, slice(share, 2 * share), share)
        total[...] = jnp.zeros_like(total)
        gate.begin()
        up_three.advance(1)
        up_two.advance(2)
        down_three.step_x()
        down_three.send_near()
        down_two.step_near()

    for b in range(blocks):
        rows = slice(b * BLOCK, (b + 1) * BLOCK)
        spec_one[b] = dot(table_ref[...], d_state[j, rows, :])
        spec_two[b] = dot(table_ref[...], mixed_ref[rows, :])

    def state_product(sign, re, im, lanes):
        s = [(spec_one[b, re, lanes], spec_one[b, im, lanes]) for b in range(blocks)]
        h = [(kern_ref[b, re, lanes].astype(F32), kern_ref[b, im, lanes].astype(F32)) for b in range(blocks)]
        for b in range(blocks):
            yr, yi = multiply_conj(*h[0], *s[b])
            for i in range(b + 1, blocks):
                pr, pi = multiply_conj(*h[i - b], *s[i])
                yr, yi = yr + pr, yi + pi
            prod[b, re, lanes] = yr.astype(BF16)
            prod[b, im, lanes] = yi.astype(BF16)

    spectral_loop(tile, state_product)

    def kernel_product(sign, re, im, lanes):
        s = [(spec_one[b, re, lanes], spec_one[b, im, lanes]) for b in range(blocks)]
        x = [(spec_two[b, re, lanes], spec_two[b, im, lanes]) for b in range(blocks)]
        after = None
        for d in range(blocks - 1, -1, -1):
            yr, yi = multiply_conj(*x[0], *s[d])
            for i in range(d + 1, blocks):
                pr, pi = multiply_conj(*x[i - d], *s[i])
                yr, yi = yr + pr, yi + pi
            if after is None:
                hr, hi = yr, yi
            else:
                hr, hi = yr + sign * after[1], yi - sign * after[0]
            after = (yr, yi)
            kern_prod[d, re, lanes] = hr.astype(BF16)
            kern_prod[d, im, lanes] = hi.astype(BF16)

    spectral_loop(tile, kernel_product)

    @pl.when(j == 0)
    def _():
        gate.advance(0)
        up_three.advance(2)
        up_two.advance(3)
        down_three.step_near()
        down_two.step_far()

    @pl.when(j >= 1)
    def _():
        kv(j - 1).advance(0)

    @pl.when(j == 1)
    def _():
        gate.advance(3)
        up_ref[:, 2 * width : 3 * width] = up_two.finish()
        up_ref[:, 3 * width : 4 * width] = up_three.finish()

    @pl.when(j == 2)
    def _():
        kv_finish(0)

    for b in range(blocks):
        rows = slice(b * BLOCK, (b + 1) * BLOCK)
        mask = live_rows(live, b * BLOCK, BLOCK)
        d_mixed = dot(back_ref[...], prod[b]).astype(BF16).astype(F32)
        d_values[rows, :] = (mask * d_mixed * shifted_ref[rows, :].astype(F32)).astype(BF16)
        d_shifted = (d_mixed * v_ref[rows, :].astype(F32)).astype(BF16)
        spec_one[b] = dot(table_ref[...], d_shifted)
        spec_two[b] = dot(table_ref[...], k_ref[rows, :])
        d_kern[rows, :] = dot(back_ref[...], kern_prod[b]) * (1.0 / BLOCK)

    @pl.when(j == 0)
    def _():
        gate.advance(1)
        up_three.advance(3)
        down_three.step_far()

    @pl.when(j >= 1)
    def _():
        kv(j - 1).advance(1)

    @pl.when(j == 1)
    def _():
        for i in range(2):
            up_ref[:, i * width : (i + 1) * width] = up_part_ref[i]
        down_ref[...] = down_part_ref[...]
        down_two.finish(down_ref)
        down_three.finish(down_ref)
        send_out().wait()
        keep_out().wait()

    def shift_product(sign, re, im, lanes):
        tr = tapspec_ref[re, lanes]
        ti = tapspec_ref[im, lanes]
        s = [(spec_one[b, re, lanes], spec_one[b, im, lanes]) for b in range(blocks)]
        x = [(spec_two[b, re, lanes], spec_two[b, im, lanes]) for b in range(blocks)]
        u = [multiply_conj(tr, ti, *s[b]) for b in range(blocks)]
        sum_re, sum_im = multiply_conj(*x[0], *s[0])
        for b in range(blocks):
            yr, yi = u[b]
            if b < blocks - 1:
                yr, yi = yr + sign * u[b + 1][1], yi - sign * u[b + 1][0]
            prod[b, re, lanes] = yr.astype(BF16)
            prod[b, im, lanes] = yi.astype(BF16)
            if b > 0:
                wr = x[b][0] - sign * x[b - 1][1]
                wi = x[b][1] + sign * x[b - 1][0]
                pr, pi = multiply_conj(wr, wi, *s[b])
                sum_re, sum_im = sum_re + pr, sum_im + pi
        kern_prod[0, re, lanes] = sum_re.astype(BF16)
        kern_prod[0, im, lanes] = sum_im.astype(BF16)

    spectral_loop(tile, shift_product)
    for b in range(blocks):
        rows = slice(b * BLOCK, (b + 1) * BLOCK)
        mask = live_rows(live, b * BLOCK, BLOCK)
        d_keys[rows, :] = (mask * dot(back_ref[...], prod[b])).astype(BF16)
    taps = d_taps_ref.shape[0]
    d_taps_ref[:, columns] = dot(back_ref[:taps, :], kern_prod[0]) * (1.0 / BLOCK)

    @pl.when(j == 0)
    def _():
        gate.advance(2)

    @pl.when(j >= 1)
    def _():
        kv(j - 1).advance(2)

    @pl.when(j == 1)
    def _():
        value = gate.finish()
        gate_ref[0] = value[:share]
        gate_ref[1] = value[share:]

    def token_grad(rows):
        return (
            total[rows, :]
            + dot_nt(d_query[rows, columns], wq_ref[...])
            + dot_nt(d_keys[rows, :], wk_ref[...])
            + dot_nt(d_values[rows, :], wv_ref[...])
        )

    def key_value_grads():
        grad[...] = dot_tn(a_one_ref[...], d_keys[...])
        share_all(grad, kv_send, kv_keep, slice(0, share), share)
        grad[...] = dot_tn(a_one_ref[...], d_values[...])
        share_all(grad, kv_send, kv_keep, slice(share, 2 * share), share)
        share_all(d_kern, kv_send, kv_keep, slice(2 * share, 2 * share + kern_share), kern_share)
        kv(j).begin()

    @pl.when(j < tiles - 1)
    def _():
        key_value_grads()
        for b in range(blocks):
            rows = slice(b * BLOCK, (b + 1) * BLOCK)
            total[rows, :] = token_grad(rows)

    @pl.when(jnp.logical_and(j >= 1, j < tiles))
    def _():
        kv(j - 1).advance(3)

    @pl.when(j == tiles - 1)
    def _():
        def norm_rows(place, low, gain_sum):
            for b in range(half // BLOCK):
                rows = pl.ds(pl.multiple_of(low + b * BLOCK, BLOCK), BLOCK)
                normed, inv = norm_stats(x_ref[rows, :].astype(F32))
                grad_in = token_grad(rows)
                gain_sum = gain_sum + jnp.sum(grad_in * normed, axis=0, keepdims=True)
                pulled = d_hidden_ref[rows, :] + norm_pull(grad_in, normed, inv, gain_ref[...])
                d_x[place, b * BLOCK : (b + 1) * BLOCK, :] = pulled.astype(BF16)
            return gain_sum

        key_value_grads()
        gain_sum = norm_rows(0, (1 - side) * half, jnp.zeros((1, width), F32))
        send_row().start()
        kv(2).advance(0)
        gain_sum = norm_rows(1, side * half, gain_sum)
        keep_row().start()
        gain_grad_ref[...] = gain_sum
        kv(2).advance(1)
        kv_finish(1)
        kv(2).advance(2)
        kv(2).advance(3)
        kv_finish(2)
        keep_row().wait()
        send_row().wait()


def mixer_back_call(
    live, out_row, d_mixer, wout, state, q, gated, a_one, mixed, shifted, k, v, wq, wk, wv, kern, tapspec, tables,
    x, gain, d_hidden, ffn_sums, taps_count, tile,
):
    length, width = a_one.shape
    blocks = length // BLOCK
    half = length // 2
    table, back = tables
    share = width // 16
    part_rows = 2 * share + length // 16
    count = width // tile
    column = lambda j: (0, j)
    rows_full = once((length, width))
    rows_tile = pl.BlockSpec((length, tile), column)
    weight = pl.BlockSpec((width, tile), column)
    anywhere = pl.BlockSpec(memory_space=pl.ANY)
    low = lambda *shape: jax.ShapeDtypeStruct(shape, BF16)
    full = lambda *shape: jax.ShapeDtypeStruct(shape, F32)
    vmem = lambda *shape: pltpu.VMEM(shape, BF16)
    wide = lambda *shape: pltpu.VMEM(shape, F32)
    sems = lambda *shape: pltpu.SemaphoreType.DMA(shape)
    up_two, up_three, down_two, down_three, up_part, down_part = ffn_sums
    su, sd = up_two.shape[2], down_two.shape[0]
    out_shape = [
        low(2, half, width),
        low(2, half, width),
        full(1, width),
        full(taps_count, width),
        full(su, 4 * width),
        full(sd, width),
        full(2, share, width),
        full(2, share, width),
        full(length // 16, width),
    ]
    return pl.pallas_call(
        mixer_back_body,
        grid=(count,),
        in_specs=[pl.BlockSpec(memory_space=pltpu.SMEM), anywhere, rows_full, once(wout.shape)]
        + [rows_full] * 4
        + [rows_tile] * 4
        + [weight] * 3
        + [
            pl.BlockSpec((blocks, 2 * BLOCK, tile), lambda j: (0, 0, j)),
            pl.BlockSpec((2 * BLOCK, tile), column),
            once(table.shape),
            once(back.shape),
            rows_full,
            once((1, width)),
            rows_full,
        ]
        + [once(s.shape) for s in ffn_sums],
        out_specs=[anywhere, anywhere] + [once(s.shape) for s in out_shape[2:]],
        out_shape=out_shape,
        scratch_shapes=[
            wide(length, width),
            wide(blocks, 2 * BLOCK, tile),
            wide(blocks, 2 * BLOCK, tile),
            vmem(blocks, 2 * BLOCK, tile),
            vmem(blocks, 2 * BLOCK, tile),
            vmem(length, tile),
            vmem(length, tile),
            vmem(length, width),
            vmem(count, length, tile),
            wide(width, tile),
            wide(length, tile),
            vmem(2, half, width),
            vmem(16, LANES),
            vmem(2, su, width),
            vmem(su, width),
            vmem(su, width),
            vmem(2, 2, su, width),
            vmem(2, su, width),
            vmem(su, width),
            vmem(su, width),
            sems(2, 5, 2),
            vmem(4, sd, width),
            vmem(4, sd, width),
            sems(2, 4, 2),
            vmem(2, 2, 2, 2 * share, width),
            vmem(2, 2, 2, 2 * share, width),
            vmem(2, 2, 2, 2 * share, width),
            vmem(2, 2, 2 * share, width),
            vmem(2, 2 * share, width),
            vmem(2 * share, width),
            vmem(2 * share, width),
            sems(5, 2),
            vmem(2, 2, 2, part_rows, tile),
            vmem(2, 2, 2, part_rows, tile),
            vmem(count, 2, 2, 2, part_rows, tile),
            vmem(count, 2, 2, part_rows, tile),
            vmem(count, 2, part_rows, tile),
            vmem(count, part_rows, tile),
            vmem(count, part_rows, tile),
            sems(count, 5, 2),
            sems(2),
            sems(2),
            sems(2),
        ],
        compiler_params=pltpu.CompilerParams(
            vmem_limit_bytes=62 * 1024 * 1024, collective_id=2, has_side_effects=True
        ),
        cost_estimate=cost(26e9, 40e6),
        name="mixer_back",
    )(
        live, out_row, d_mixer, wout, state, q, gated, a_one, mixed, shifted, k, v, wq, wk, wv, kern, tapspec,
        table, back, x, gain, d_hidden, up_two, up_three, down_two, down_three, up_part, down_part,
    )


MICRO = 2


epsilon = 1e-05
highest = lax.Precision.HIGHEST


def layer_norm(rows, gain):
    center = rows - jnp.mean(rows, axis=-1, keepdims=True)
    spread = jnp.mean(center * center, axis=-1, keepdims=True)
    return center * lax.rsqrt(spread + epsilon) * gain


def exact_gelu(values):
    return jax.nn.gelu(values, approximate=False)


def project(rows, weight):
    return jnp.einsum("rtd,de->rte", rows, weight, preferred_element_type=jnp.float32)


def project_back(rows, weight):
    return jnp.einsum("rte,de->rtd", rows, weight, preferred_element_type=jnp.float32)


def weight_grad(left, right):
    return jnp.einsum("rtd,rte->de", left, right, preferred_element_type=jnp.float32)


def depth_conv(signal, kernel_taps):
    channels = signal.shape[2]
    return lax.conv_general_dilated(
        signal,
        kernel_taps,
        (1,),
        "VALID",
        dimension_numbers=("NWC", "WIO", "NWC"),
        feature_group_count=channels,
        precision=highest,
    )


def shift_conv(extended, taps, length):
    flipped = jnp.transpose(taps[:, ::-1])[:, None, :]
    return depth_conv(extended[:, 1:, :], flipped)[:, :length, :]


def shift_back(extended, taps, length):
    forward_taps = jnp.transpose(taps)[:, None, :]
    return depth_conv(extended, forward_taps)[:, :length, :]


def taps_grad(grad_rows, extended, width_taps):
    rows_count, span, channels = extended.shape
    left = jnp.transpose(extended, (2, 0, 1)).reshape(1, channels * rows_count, span)
    right = jnp.transpose(grad_rows, (2, 0, 1))
    result = lax.conv_general_dilated(
        left,
        right,
        (1,),
        "VALID",
        dimension_numbers=("NCW", "OIW", "NCW"),
        feature_group_count=channels,
        precision=highest,
    )
    return result[0][:, ::-1][:, :width_taps]


def diag_kernel(coef, rate, length):
    steps = lax.iota(jnp.float32, length)
    return jnp.sum(coef[:, :, None] * jnp.exp(-rate[:, :, None] * steps), axis=1)


def dft_tables(length):
    period = 2 * length
    time_index = lax.iota(jnp.int32, length)[:, None]
    freq_index = lax.iota(jnp.int32, length + 1)[None, :]
    phase_index = time_index * freq_index % period
    angles = phase_index.astype(jnp.float32) * (2.0 * math.pi / period)
    cos_table = jnp.cos(angles)
    sin_table = jnp.sin(angles)
    edges = (freq_index == 0) | (freq_index == length)
    weights = jnp.where(edges, 1.0, 2.0).astype(jnp.float32) / period
    return (cos_table, sin_table, cos_table * weights, sin_table * weights)


def spectrum(signal, cos_table, sin_table):
    real_part = jnp.einsum("rtc,tf->rfc", signal, cos_table, precision=highest)
    imag_part = -jnp.einsum("rtc,tf->rfc", signal, sin_table, precision=highest)
    return (real_part, imag_part)


def inverse(real_part, imag_part, cos_weighted, sin_weighted):
    first = jnp.einsum("rfc,tf->rtc", real_part, cos_weighted, precision=highest)
    second = jnp.einsum("rfc,tf->rtc", imag_part, sin_weighted, precision=highest)
    return first - second


def split_channels(
    tokens,
    lengths,
    gain_one,
    w_query,
    w_key,
    w_value,
    w_out,
    gain_two,
    w_up,
    w_down,
    shift_taps,
    diag_coef,
    diag_rate,
    cotangent,
):
    rows_dev, tok_len, model_width = tokens.shape
    length = tok_len * lax.axis_size("seq")
    width_taps = shift_taps.shape[1]
    first_pos = lax.axis_index("seq") * tok_len
    positions = first_pos + lax.iota(jnp.int32, tok_len)
    mask_all = (positions[None, :] < lengths[:, None]).astype(jnp.float32)[:, :, None]
    cos_table, sin_table, cos_weighted, sin_weighted = dft_tables(length)

    def kernel_of(coef_in, rate_in):
        return diag_kernel(coef_in, rate_in, length)

    kernel, kernel_pull = jax.vjp(kernel_of, diag_coef, diag_rate)
    kernel_real = jnp.einsum("ct,tf->fc", kernel, cos_table, precision=highest)
    kernel_imag = -jnp.einsum("ct,tf->fc", kernel, sin_table, precision=highest)
    taps_acc = jnp.zeros(shift_taps.shape, jnp.float32)
    spec_real_acc = jnp.zeros((length + 1, shift_taps.shape[0]), jnp.float32)
    spec_imag_acc = jnp.zeros((length + 1, shift_taps.shape[0]), jnp.float32)
    grad_gain_one = jnp.zeros(gain_one.shape, jnp.float32)
    grad_gain_two = jnp.zeros(gain_two.shape, jnp.float32)
    grad_query = jnp.zeros(w_query.shape, jnp.float32)
    grad_key = jnp.zeros(w_key.shape, jnp.float32)
    grad_value = jnp.zeros(w_value.shape, jnp.float32)
    grad_out = jnp.zeros(w_out.shape, jnp.float32)
    grad_up = jnp.zeros(w_up.shape, jnp.float32)
    grad_down = jnp.zeros(w_down.shape, jnp.float32)
    rows_mb = rows_dev // MICRO
    out_list = []
    dx_list = []
    for micro_step in range(MICRO):
        low_row = micro_step * rows_mb
        x_rows = tokens[low_row : low_row + rows_mb].astype(jnp.float32)
        live_mask = mask_all[low_row : low_row + rows_mb]
        grad_rows = cotangent[low_row : low_row + rows_mb].astype(jnp.float32)
        norm_one, norm_one_pull = jax.vjp(layer_norm, x_rows, gain_one)
        a_one = norm_one.astype(jnp.bfloat16)
        query_rows = project(a_one, w_query)
        key_rows = (project(a_one, w_key) * live_mask).astype(jnp.bfloat16)
        value_rows = (project(a_one, w_value) * live_mask).astype(jnp.bfloat16)
        keys_ch, values_ch = (
            lax.all_to_all(key_rows, "seq", split_axis=2, concat_axis=1, tiled=True),
            lax.all_to_all(value_rows, "seq", split_axis=2, concat_axis=1, tiled=True),
        )
        key_ext = jnp.pad(keys_ch.astype(jnp.float32), ((0, 0), (width_taps, 0), (0, 0)))
        shifted = shift_conv(key_ext, shift_taps, length)
        values_here = values_ch.astype(jnp.float32)
        mixed_ch = (shifted * values_here).astype(jnp.bfloat16)
        mixed_real, mixed_imag = spectrum(mixed_ch.astype(jnp.float32), cos_table, sin_table)
        state = inverse(
            mixed_real * kernel_real - mixed_imag * kernel_imag,
            mixed_real * kernel_imag + mixed_imag * kernel_real,
            cos_weighted,
            sin_weighted,
        )
        state_tok = lax.all_to_all(
            state.astype(jnp.bfloat16), "seq", split_axis=1, concat_axis=2, tiled=True
        )
        state_rows = state_tok.astype(jnp.float32)
        gated_rows = (query_rows * state_rows).astype(jnp.bfloat16)
        hidden = x_rows + live_mask * project(gated_rows, w_out)
        norm_two, norm_two_pull = jax.vjp(layer_norm, hidden, gain_two)
        a_two = norm_two.astype(jnp.bfloat16)
        pre_act = project(a_two, w_up)
        act_value, gelu_pull = jax.vjp(exact_gelu, pre_act)
        activation = act_value.astype(jnp.bfloat16)
        result = hidden + live_mask * project(activation, w_down)
        out_list.append(result.astype(jnp.bfloat16))
        d_down = (live_mask * grad_rows).astype(jnp.bfloat16)
        grad_down = grad_down + weight_grad(activation, d_down)
        d_act = project_back(d_down, w_down)
        d_pre = gelu_pull(d_act)[0].astype(jnp.bfloat16)
        grad_up = grad_up + weight_grad(a_two, d_pre)
        d_a_two = project_back(d_pre, w_up)
        d_hidden_norm, d_gain_two = norm_two_pull(d_a_two)
        grad_gain_two = grad_gain_two + d_gain_two
        d_hidden = grad_rows + d_hidden_norm
        d_mixer = (live_mask * d_hidden).astype(jnp.bfloat16)
        grad_out = grad_out + weight_grad(gated_rows, d_mixer)
        d_gated = project_back(d_mixer, w_out)
        d_query = (d_gated * state_rows).astype(jnp.bfloat16)
        d_state = (d_gated * query_rows).astype(jnp.bfloat16)
        d_state_ch = lax.all_to_all(d_state, "seq", split_axis=2, concat_axis=1, tiled=True)
        grad_real, grad_imag = spectrum(d_state_ch.astype(jnp.float32), cos_table, sin_table)
        d_mixed = inverse(
            kernel_real * grad_real + kernel_imag * grad_imag,
            kernel_real * grad_imag - kernel_imag * grad_real,
            cos_weighted,
            sin_weighted,
        )
        spec_real_acc = spec_real_acc + jnp.sum(
            mixed_real * grad_real + mixed_imag * grad_imag, axis=0
        )
        spec_imag_acc = spec_imag_acc + jnp.sum(
            mixed_real * grad_imag - mixed_imag * grad_real, axis=0
        )
        d_mixed_low = d_mixed.astype(jnp.bfloat16)
        d_mix_ch = d_mixed_low.astype(jnp.float32)
        d_shifted = d_mix_ch * values_here
        d_values_ch = (d_mix_ch * shifted).astype(jnp.bfloat16)
        grad_ext = jnp.pad(d_shifted, ((0, 0), (0, width_taps), (0, 0)))
        d_keys_ch = shift_back(grad_ext, shift_taps, length).astype(jnp.bfloat16)
        taps_acc = taps_acc + taps_grad(d_shifted, key_ext, width_taps)
        keys_back, values_back = (
            lax.all_to_all(d_keys_ch, "seq", split_axis=1, concat_axis=2, tiled=True),
            lax.all_to_all(d_values_ch, "seq", split_axis=1, concat_axis=2, tiled=True),
        )
        mask_low = live_mask.astype(jnp.bfloat16)
        d_keys = keys_back * mask_low
        d_values = values_back * mask_low
        grad_query = grad_query + weight_grad(a_one, d_query)
        grad_key = grad_key + weight_grad(a_one, d_keys)
        grad_value = grad_value + weight_grad(a_one, d_values)
        d_a_one = (
            project_back(d_query, w_query)
            + project_back(d_keys, w_key)
            + project_back(d_values, w_value)
        )
        d_x_norm, d_gain_one = norm_one_pull(d_a_one)
        grad_gain_one = grad_gain_one + d_gain_one
        dx_list.append((d_hidden + d_x_norm).astype(jnp.bfloat16))
    d_kernel = jnp.einsum("fc,tf->ct", spec_real_acc, cos_weighted, precision=highest) - jnp.einsum(
        "fc,tf->ct", spec_imag_acc, sin_weighted, precision=highest
    )
    d_coef, d_rate = kernel_pull(d_kernel)
    taps_part, coef_part, rate_part = (
        lax.psum_scatter(
            taps_acc.astype(jnp.bfloat16), "dp", scatter_dimension=1, tiled=True
        ).astype(jnp.float32),
        lax.psum_scatter(d_coef.astype(jnp.bfloat16), "dp", scatter_dimension=1, tiled=True).astype(
            jnp.float32
        ),
        lax.psum_scatter(d_rate.astype(jnp.bfloat16), "dp", scatter_dimension=1, tiled=True).astype(
            jnp.float32
        ),
    )
    shares = (
        lax.psum_scatter(
            grad_gain_one.astype(jnp.bfloat16), "dp", scatter_dimension=0, tiled=True
        ).astype(jnp.float32),
        lax.psum_scatter(
            grad_query.astype(jnp.bfloat16), "dp", scatter_dimension=0, tiled=True
        ).astype(jnp.float32),
        lax.psum_scatter(
            grad_key.astype(jnp.bfloat16), "dp", scatter_dimension=0, tiled=True
        ).astype(jnp.float32),
        lax.psum_scatter(
            grad_value.astype(jnp.bfloat16), "dp", scatter_dimension=0, tiled=True
        ).astype(jnp.float32),
        lax.psum_scatter(
            grad_out.astype(jnp.bfloat16), "dp", scatter_dimension=0, tiled=True
        ).astype(jnp.float32),
        lax.psum_scatter(
            grad_gain_two.astype(jnp.bfloat16), "dp", scatter_dimension=0, tiled=True
        ).astype(jnp.float32),
        lax.psum_scatter(
            grad_up.astype(jnp.bfloat16), "dp", scatter_dimension=0, tiled=True
        ).astype(jnp.float32),
        lax.psum_scatter(
            grad_down.astype(jnp.bfloat16), "dp", scatter_dimension=0, tiled=True
        ).astype(jnp.float32),
    )
    totals = (
        lax.psum(shares[0].astype(jnp.bfloat16), "seq").astype(jnp.float32),
        lax.psum(shares[1].astype(jnp.bfloat16), "seq").astype(jnp.float32),
        lax.psum(shares[2].astype(jnp.bfloat16), "seq").astype(jnp.float32),
        lax.psum(shares[3].astype(jnp.bfloat16), "seq").astype(jnp.float32),
        lax.psum(shares[4].astype(jnp.bfloat16), "seq").astype(jnp.float32),
        lax.psum(shares[5].astype(jnp.bfloat16), "seq").astype(jnp.float32),
        lax.psum(shares[6].astype(jnp.bfloat16), "seq").astype(jnp.float32),
        lax.psum(shares[7].astype(jnp.bfloat16), "seq").astype(jnp.float32),
    )
    out_rows = jnp.concatenate(out_list, axis=0)
    dx_rows = jnp.concatenate(dx_list, axis=0)
    return (
        out_rows,
        dx_rows,
        totals[0],
        totals[1],
        totals[2],
        totals[3],
        totals[4],
        totals[5],
        totals[6],
        totals[7],
        taps_part,
        coef_part,
        rate_part,
    )


def swap(value, axis_name, bit):
    count = lax.axis_size(axis_name)
    return lax.ppermute(value, axis_name, [(i, i ^ bit) for i in range(count)])


def reduce_small(value, place):
    count = value.shape[0]
    order = jnp.bitwise_xor(lax.iota(jnp.int32, count), place)
    value = jnp.take(value, order, axis=0)
    bit = count // 2
    while bit >= 1:
        value = value[:bit] + swap(value[bit:], "dp", bit)
        bit //= 2
    return value[0]


def whole_row(own, given, side):
    return jnp.where(
        side == 0, jnp.concatenate([own, given], axis=0), jnp.concatenate([given, own], axis=0)
    )


def exchange_rows(rows, side):
    own = lax.dynamic_index_in_dim(rows, side, 0, keepdims=False)
    other = lax.dynamic_index_in_dim(rows, 1 - side, 0, keepdims=False)
    return whole_row(own, swap(other, "seq", 1), side)


def split_rows(
    tokens, lengths, gain_one, w_query, w_key, w_value, w_out, gain_two, w_up, w_down,
    shift_taps, diag_coef, diag_rate, cotangent,
):
    side = lax.axis_index("seq")
    mine = lax.axis_index("dp")
    devices = lax.axis_size("dp")
    width = tokens.shape[2]
    length = tokens.shape[1] * 2
    channels, states = diag_coef.shape
    tile = 256
    tables = transform_tables()
    live = lax.dynamic_slice_in_dim(lengths, side, 1, 0)
    x = exchange_rows(tokens, side)
    packed = jnp.stack([diag_coef.T, diag_rate.T, shift_taps.T])
    packed_other = swap(packed, "seq", 1)
    packed_all = jnp.where(
        side == 0,
        jnp.concatenate([packed, packed_other], axis=2),
        jnp.concatenate([packed_other, packed], axis=2),
    )
    coef, rate, taps = packed_all[0], packed_all[1], packed_all[2]
    cot = exchange_rows(cotangent, side)
    kern, tapspec = spectra_call(coef, rate, taps, tables[0], length, tile)
    row_one = gain_one[None, :]
    row_two = gain_two[None, :]
    a_one, q, k, v, shifted, mixed, state, gated, hidden, a_two = mixer_call(
        live, x, row_one, w_query, w_key, w_value, w_out, row_two, kern, tapspec, tables, tile
    )
    out_row, d_hidden, d_mixer, d_gain_two, up_part, down_part, *parts = ffn_call(
        live, a_two, cot, hidden, row_two, w_up, w_down
    )
    out, d_tokens, d_gain_one, d_taps, up, down, gate, kv, d_kern = mixer_back_call(
        live, out_row, d_mixer, w_out, state, q, gated, a_one, mixed, shifted, k, v, w_query, w_key, w_value, kern,
        tapspec, tables, x, row_one, d_hidden, (*parts, up_part, down_part), states, tile,
    )

    d_kern_half = lax.dynamic_slice_in_dim(d_kern, side * channels, channels, 1)
    steps = (mine * d_kern.shape[0] + lax.iota(jnp.int32, d_kern.shape[0])).astype(F32)
    decay = jnp.exp(-diag_rate.T[None] * steps[:, None, None]) * d_kern_half[:, None, :]
    coef_part = jnp.sum(decay, axis=0)
    rate_part = -diag_coef.T * jnp.sum(decay * steps[:, None, None], axis=0)
    each = states // devices
    pair = jnp.concatenate(
        [coef_part.reshape(devices, each, channels), rate_part.reshape(devices, each, channels)], axis=1
    )
    pair = reduce_small(pair, mine)

    gain_each = width // devices
    gains = jnp.concatenate([d_gain_one.reshape(devices, 1, gain_each), d_gain_two.reshape(devices, 1, gain_each)], axis=2)
    gains = jnp.pad(gains, ((0, 0), (0, 0), (0, width - 2 * gain_each)))
    small = jnp.concatenate([d_taps.reshape(devices, each, width), gains], axis=1)
    small = reduce_small(small, mine)
    small = small + swap(small, "seq", 1)
    taps_part = lax.dynamic_slice_in_dim(small[:each], side * channels, channels, 1)
    return (
        out,
        d_tokens,
        small[each, :gain_each],
        gate[1],
        kv[0],
        kv[1],
        gate[0],
        small[each, gain_each : 2 * gain_each],
        up,
        down,
        taps_part.T,
        pair[:each].T,
        pair[each:].T,
    )


def solution(mesh):
    in_specs = (
        P("dp", "seq", None),
        P("dp"),
        P(),
        P(),
        P(),
        P(),
        P(),
        P(),
        P(),
        P(),
        P("seq", None),
        P("seq", None),
        P("seq", None),
        P("dp", "seq", None),
    )
    out_specs = (
        P("dp", "seq", None),
        P("dp", "seq", None),
        P("dp"),
        P("dp", None),
        P("dp", None),
        P("dp", None),
        P("dp", None),
        P("dp"),
        P("dp", None),
        P("dp", None),
        P("seq", "dp"),
        P("seq", "dp"),
        P("seq", "dp"),
    )

    def per_device(*args):
        tokens, shift_taps = args[0], args[10]
        rows, positions, width = tokens.shape
        fits = (
            mesh.shape["seq"] == rows == 2
            and mesh.shape["dp"] == 16
            and positions * 2 % BLOCK == 0
            and width % 256 == 0
            and shift_taps.shape[1] <= BLOCK
        )
        return split_rows(*args) if fits else split_channels(*args)

    return jax.shard_map(
        per_device, mesh=mesh, in_specs=in_specs, out_specs=out_specs, check_vma=False
    )
```

```python
import functools
import math

import jax
import jax.numpy as jnp
import numpy as np
from jax import lax
from jax.experimental import pallas as pl
from jax.experimental.pallas import tpu as pltpu
from jax.sharding import PartitionSpec as P

BLOCK = 256
CHUNK = 16
LANES = 128
EPS = 1e-05
F32 = jnp.float32
BF16 = jnp.bfloat16
VMEM_BYTES = 60 * 1024 * 1024


def dot(a, b):
    return lax.dot_general(a, b, (((1,), (0,)), ((), ())), preferred_element_type=F32)


def dot_nt(a, b):
    return lax.dot_general(a, b, (((1,), (1,)), ((), ())), preferred_element_type=F32)


def dot_tn(a, b):
    return lax.dot_general(a, b, (((0,), (0,)), ((), ())), preferred_element_type=F32)


def params():
    return pltpu.CompilerParams(vmem_limit_bytes=VMEM_BYTES)


def cost(flops, byte_count):
    return pl.CostEstimate(flops=int(flops), bytes_accessed=int(byte_count), transcendentals=0)


def transform_tables():
    freq = np.concatenate([np.arange(0, BLOCK, 2), np.arange(1, BLOCK, 2)]).astype(np.float64)
    time = np.arange(BLOCK, dtype=np.float64)
    angle = (2.0 * math.pi / (2 * BLOCK)) * (freq[:, None] + 0.5) * time[None, :]
    table = np.concatenate([np.cos(angle), -np.sin(angle)], axis=0)
    return jnp.asarray(table, dtype=BF16), jnp.asarray(table.T.copy(), dtype=BF16)


def norm_stats(rows):
    center = rows - jnp.mean(rows, axis=-1, keepdims=True)
    spread = jnp.mean(center * center, axis=-1, keepdims=True)
    inv = lax.rsqrt(spread + EPS)
    return center * inv, inv


def norm_pull(grad, normed, inv, gain):
    scaled = grad * gain
    mean_one = jnp.mean(scaled, axis=-1, keepdims=True)
    mean_two = jnp.mean(scaled * normed, axis=-1, keepdims=True)
    return (scaled - mean_one - normed * mean_two) * inv


def live_rows(length, first, count):
    rows = lax.broadcasted_iota(jnp.int32, (count, 1), 0) + first
    return (rows < length).astype(F32)


def spectral_loop(channels, body):
    half = BLOCK // 2
    for parity in range(2):
        sign = 1.0 if parity == 0 else -1.0
        for lane in range(channels // LANES):
            lanes = slice(lane * LANES, (lane + 1) * LANES)

            def step(index, carry, sign=sign, lanes=lanes, parity=parity):
                low = pl.multiple_of(parity * half + index * CHUNK, CHUNK)
                body(sign, pl.ds(low, CHUNK), pl.ds(low + BLOCK, CHUNK), lanes)
                return carry

            lax.fori_loop(0, half // CHUNK, step, 0)


def multiply(ar, ai, br, bi):
    return ar * br - ai * bi, ar * bi + ai * br


def multiply_conj(ar, ai, br, bi):
    return ar * br + ai * bi, ar * bi - ai * br


def gelu_pair(x):
    bell = jnp.exp(x * x * -0.5)
    size = jnp.abs(x)
    t = 1.0 / (1.0 + (0.3275911 / math.sqrt(2.0)) * size)
    poly = t * (
        0.5 * 0.254829592
        + t * (0.5 * -0.284496736 + t * (0.5 * 1.421413741 + t * (0.5 * -1.453152027 + t * (0.5 * 1.061405429))))
    )
    tail = poly * bell
    phi = jnp.where(x >= 0.0, 1.0 - tail, tail)
    return x * phi, phi + x * bell * (1.0 / math.sqrt(2.0 * math.pi))


def bit_of(index, bit):
    return lax.rem(index // bit, 2)


def partner(axis, bit):
    index = lax.axis_index(axis)
    return {axis: index + bit * (1 - 2 * bit_of(index, bit))}


UP, DOWN, GATE, KERN, KEY, VALUE, KV, OUT, ROW, COEF, TAPS, GAIN = range(12)
CORE, MIDDLE, NEAR, FAR, SIDE = ("dp", 1), ("dp", 2), ("dp", 4), ("dp", 8), ("seq", 1)


def greet(partners):
    barrier = pltpu.get_barrier_semaphore()
    for axis, bit in partners:
        pl.semaphore_signal(barrier, inc=1, device_id=partner(axis, bit), device_id_type=pl.DeviceIdType.MESH)
    pl.semaphore_wait(barrier, len(partners))


def transfer(source, target, sems, to):
    return pltpu.make_async_remote_copy(
        src_ref=source,
        dst_ref=target,
        send_sem=sems.at[0],
        recv_sem=sems.at[1],
        device_id=partner(*to),
        device_id_type=pl.DeviceIdType.MESH,
    )


def add_into(target, other):
    *lead, rows, _ = target.shape
    for place in np.ndindex(*lead):
        for low in range(0, rows, 48):
            piece = (*place, slice(low, min(low + 48, rows)))
            target[piece] = target[piece] + other[piece]


def places(mine, owners, bits):
    own = [bit_of(mine, bit) for bit in bits]
    return [
        tuple(1 - own[i] if (owner // bit) % 2 else own[i] for i, bit in enumerate(bits)) for owner in range(owners)
    ]


def spread(value, base, sideways=False):
    value = value.astype(BF16)
    share = value.shape[0] // 16
    half = value.shape[1] // 2
    side = lax.axis_index("seq")
    for owner, (core, *place) in enumerate(places(lax.axis_index("dp"), 16, (1, 2, 4, 8))):
        rows = value[owner * share : (owner + 1) * share]
        if sideways:
            base[(core, side, *place)] = rows[:, :half]
            base[(core, 1 - side, *place)] = rows[:, half:]
        else:
            base[(core, *place)] = rows


class Sum:
    def __init__(self, refs, sems, order, final=None, across=True):
        self.refs, self.sems, self.final = refs, sems, final
        self.outer, self.sideways = order in "zZ", order in "XZ"
        self.lead = 2 if self.sideways else 1
        self.last = self.lead + 3
        self.across = across

    def part(self, step, half):
        ref = self.refs[step]
        if step == self.last:
            return ref
        if self.outer and self.lead <= step < self.lead + 2:
            return ref.at[:, half]
        return ref.at[half]

    def copy(self, step):
        order = (NEAR, FAR, MIDDLE) if self.outer else (MIDDLE, NEAR, FAR)
        order = (CORE, *((SIDE,) if self.sideways else ()), *order, SIDE)
        return transfer(self.part(step, 1), self.refs[step + 1], self.sems.at[step], order[step])

    def start(self, step):
        self.copy(step).start()

    def wait(self, step):
        self.copy(step).wait()
        if step < self.last:
            add_into(self.refs[step + 1], self.part(step, 0))
            if step == self.last - 1 and not self.across:
                self.final(self.refs[step + 1][...])
        else:
            self.final(self.refs[step][...], self.refs[step + 1][...], self.sideways)


class Whole:
    def __init__(self, refs, lands, sems):
        self.refs, self.lands, self.sems = refs, lands, sems

    def copy(self, step):
        return transfer(self.refs.at[step], self.lands.at[step], self.sems.at[step], (CORE, MIDDLE, NEAR, FAR, SIDE)[step])

    def start(self, step):
        self.copy(step).start()

    def wait(self, step):
        self.copy(step).wait()
        self.refs[step + 1] = self.refs[step] + self.lands[step]


class Gather:
    def __init__(self, z, refs, sems, sideways, final=None):
        self.refs, self.sems, self.final, self.sideways = refs, sems, final, sideways
        self.lead = 3 if sideways else 2
        self.last = self.lead + 2
        mine = lax.axis_index("dp")
        near = bit_of(mine, 4) == z % 2
        far = bit_of(mine, 8) == z // 2
        both = jnp.logical_and(near, far)
        self.gives = (jnp.logical_not(near), jnp.logical_and(near, jnp.logical_not(far)), both)
        self.takes = (near, both, both)

    def part(self, step, half):
        return self.refs[step].at[half] if step < self.lead else self.refs[step]

    def copy(self, step):
        order = (CORE, *((SIDE,) if self.sideways else ()), MIDDLE, NEAR, FAR, SIDE)
        return transfer(self.part(step, 1), self.refs[step + 1], self.sems.at[step], order[step])

    def start(self, step):
        if step < self.lead:
            self.copy(step).start()
        else:

            @pl.when(self.gives[step - self.lead])
            def _():
                self.copy(step).start()

    def wait(self, step):
        if step < self.lead:
            self.copy(step).wait()
            add_into(self.refs[step + 1], self.part(step, 0))
            return

        @pl.when(self.gives[step - self.lead])
        def _():
            self.copy(step).wait_send()

        @pl.when(self.takes[step - self.lead])
        def _():
            self.copy(step).wait_recv()
            if step < self.last:
                add_into(self.refs[step + 1], self.part(step, 0))
            else:
                self.final(self.refs[step][...], self.refs[step + 1][...], self.sideways)


class Rows:
    def __init__(self, source, target, sems):
        self.copy = transfer(source, target, sems, SIDE)

    def start(self, _):
        self.copy.start()

    def wait(self, _):
        self.copy.wait()


def follow(sums, events):
    for name, index, exchange, begin in events:
        if begin:
            sums[name, index].start(exchange)
        else:
            sums[name, index].wait(exchange)


def put(target, low, own, given, sideways):
    if sideways:
        side = lax.axis_index("seq")
        half = own.shape[-1]
        target[:, pl.ds(pl.multiple_of(low + side * half, LANES), half)] = own.astype(F32)
        target[:, pl.ds(pl.multiple_of(low + (1 - side) * half, LANES), half)] = given.astype(F32)
    else:
        target[:, low : low + own.shape[-1]] = own.astype(F32) + given.astype(F32)


def base_shape(rows, columns, order):
    return (2, 2, 2, 2, 2, rows, columns // 2) if order in "XZ" else (2, 2, 2, 2, rows, columns)


def landings(rows, columns, order):
    *bits, rows, columns = base_shape(rows, columns, order)
    return [pltpu.VMEM((*bits[n + 1 :], rows, columns), BF16) for n in range(len(bits))] + [pltpu.VMEM((rows, columns), BF16)]


def gather_landings(rows, columns, sideways):
    bits = (2, 2) if sideways else (2,)
    columns = columns // 2 if sideways else columns
    return [pltpu.VMEM((*bits[n:], rows, columns), BF16) for n in range(len(bits) + 1)] + [
        pltpu.VMEM((rows, columns), BF16) for _ in range(3)
    ]


def once(shape):
    zeros = (0,) * len(shape)
    return pl.BlockSpec(shape, lambda *_: zeros, pipeline_mode=pl.Buffered(1))


def mixer_body(
    length_ref, tokens_hbm, cot_hbm, own_ref, taps_ref, gain_one_ref, gain_two_ref, wq_hbm, wk_hbm, wv_hbm, wout_hbm,
    table_ref, back_ref,
    x_hbm, cot_out, a_one_hbm, q_hbm, k_hbm, v_hbm, kern_hbm, tapspec_hbm, hidden_hbm, a_two_hbm,
    shifted_ref, mixed_ref, state_ref,
    x, a_one, q, k, v, total, a_two, wq, wk, wv, wout, kern, tapspec, taps, other, current, kern_time, near, far,
    spec, prod, in_sems, own_sems, out_sems, token_sems, cot_sems, other_sems, taps_sems, unit_sems,
):
    j = pl.program_id(0)
    steps = pl.num_programs(0)
    length, width = x.shape
    half = length // 2
    tile = shifted_ref.shape[1]
    blocks = length // BLOCK
    states, channels = own_ref.shape[1:]
    live = length_ref[0]
    side = lax.axis_index("seq")
    core = bit_of(lax.axis_index("dp"), 1)
    own_rows = pl.ds(pl.multiple_of(side * half, half), half)

    weights = [
        pltpu.make_async_copy(source, target, in_sems.at[i])
        for i, (source, target) in enumerate(((wq_hbm, wq), (wk_hbm, wk), (wv_hbm, wv), (wout_hbm, wout)))
    ]
    outs = [
        pltpu.make_async_copy(source, target, out_sems.at[i])
        for i, (source, target) in enumerate(
            (
                (x, x_hbm), (a_one, a_one_hbm), (q, q_hbm), (k, k_hbm), (v, v_hbm), (kern, kern_hbm),
                (tapspec, tapspec_hbm), (total, hidden_hbm), (a_two, a_two_hbm),
            )
        )
    ]
    own_x = pltpu.make_async_copy(tokens_hbm.at[side], x.at[own_rows], own_sems.at[0])
    own_cot = pltpu.make_async_copy(cot_hbm.at[side], cot_out.at[own_rows], own_sems.at[1])
    other_x = transfer(tokens_hbm.at[1 - side], x.at[own_rows], token_sems, SIDE)
    other_cot = transfer(cot_hbm.at[1 - side], cot_out.at[own_rows], cot_sems, SIDE)
    wanted = pl.ds(pl.multiple_of(core * LANES, LANES), 2 * LANES)
    other_params = transfer(own_ref.at[:, :, wanted], other, other_sems, SIDE)
    own_lanes = pl.ds(pl.multiple_of(side * channels, LANES), channels)
    other_taps = transfer(taps_ref, taps.at[:, own_lanes], taps_sems, SIDE)

    def unit_columns(number, of_core):
        tile_of = (2 * of_core, 1, 2 * of_core)[number]
        half_of = (side, side + of_core - 2 * side * of_core, 1 - side)[number]
        return pl.ds(pl.multiple_of(half_of * channels + tile_of * LANES, LANES), LANES)

    def unit_copy(number):
        columns = unit_columns(number, core)
        return transfer(kern_time.at[:, columns], kern_time.at[:, columns], unit_sems.at[number], CORE)

    def unit(number):
        if number == 0:
            for part in range(2):
                current[part] = own_ref[part, :, pl.ds(pl.multiple_of(core * 2 * LANES, LANES), LANES)]
        elif number == 1:

            @pl.when(core == 0)
            def _():
                for part in range(2):
                    current[part] = own_ref[part, :, LANES : 2 * LANES]

            @pl.when(core == 1)
            def _():
                other_params.wait()
                for part in range(2):
                    current[part] = other[part, :, :LANES]

        else:

            @pl.when(core == 0)
            def _():
                other_params.wait()
                for part in range(2):
                    current[part] = other[part, :, :LANES]

            @pl.when(core == 1)
            def _():
                for part in range(2):
                    current[part] = other[part, :, LANES:]

        columns = unit_columns(number, core)
        step_count, together = 32, 8
        groups = length // step_count
        near_time = lax.broadcasted_iota(jnp.int32, (step_count, 1), 0).astype(F32)
        far_time = lax.broadcasted_iota(jnp.int32, (groups, 1), 0).astype(F32) * step_count

        def fill(n, carry):
            rate = current[1, pl.ds(n, 1), :]
            near[n] = jnp.exp(-rate * near_time)
            far_n = current[0, pl.ds(n, 1), :] * jnp.exp(-rate * far_time)
            for g in range(groups // together):
                far[g, n] = far_n[g * together : (g + 1) * together, :]
            return carry

        lax.fori_loop(0, states, fill, 0)

        def group(g, carry):
            def add(n, sums):
                near_n = near[n]
                return tuple(sums[i] + far[g, n, i : i + 1, :] * near_n for i in range(together))

            zeros = tuple(jnp.zeros((step_count, LANES), F32) for _ in range(together))
            sums = lax.fori_loop(0, states, add, zeros, unroll=4)
            for i in range(together):
                place = pl.multiple_of((g * together + i) * step_count, step_count)
                kern_time[pl.ds(place, step_count), columns] = sums[i].astype(BF16)
            return carry

        lax.fori_loop(0, groups // together, group, 0)
        unit_copy(number).start()

    def project_rows(low):
        def block(b, carry):
            rows = pl.ds(pl.multiple_of(low + b * BLOCK, BLOCK), BLOCK)
            normed, _ = norm_stats(x[rows, :].astype(F32))
            a_rows = (normed * gain_one_ref[...]).astype(BF16)
            a_one[rows, :] = a_rows
            mask = live_rows(live, low + b * BLOCK, BLOCK)
            k[rows, :] = (dot(a_rows, wk[...]) * mask).astype(BF16)
            v[rows, :] = (dot(a_rows, wv[...]) * mask).astype(BF16)
            q[rows, :] = dot(a_rows, wq[...]).astype(BF16)
            return carry

        lax.fori_loop(0, half // BLOCK, block, 0)

    @pl.when(j == 0)
    def _():
        own_x.start()
        own_cot.start()
        for copy in weights:
            copy.start()
        greet((CORE, SIDE))
        other_params.start()
        other_taps.start()
        other_x.start()
        taps[:, own_lanes] = taps_ref[...]
        total[...] = jnp.zeros_like(total)
        unit(0)
        unit(1)
        unit(2)
        for copy in weights:
            copy.wait()
        own_x.wait()
        project_rows(side * half)
        other_taps.wait()
        for number in range(3):
            unit_copy(number).wait()

        def tile_spectra(t, carry):
            columns = pl.ds(pl.multiple_of(t * tile, tile), tile)
            for b in range(blocks):
                spec[b] = dot(table_ref[...], kern_time[b * BLOCK : (b + 1) * BLOCK, columns])

            def combine(sign, re, im, lanes):
                to = pl.ds(pl.multiple_of(t * tile + lanes.start, LANES), LANES)
                for b in range(blocks):
                    out_re = spec[b, re, lanes]
                    out_im = spec[b, im, lanes]
                    if b > 0:
                        out_re = out_re - sign * spec[b - 1, im, lanes]
                        out_im = out_im + sign * spec[b - 1, re, lanes]
                    kern[b, re, to] = (out_re * (1.0 / BLOCK)).astype(BF16)
                    kern[b, im, to] = (out_im * (1.0 / BLOCK)).astype(BF16)

            spectral_loop(tile, combine)
            tapspec[:, columns] = dot(table_ref[:, : taps.shape[0]], taps[:, columns]) * (1.0 / BLOCK)
            return carry

        lax.fori_loop(0, width // tile, tile_spectra, 0)
        outs[5].start()
        outs[6].start()
        other_x.wait()
        other_cot.start()
        outs[0].start()
        project_rows((1 - side) * half)
        for copy in outs[1:5]:
            copy.start()

    @pl.when(j > 0)
    def _():
        t = j - 1
        columns = pl.ds(pl.multiple_of(t * tile, tile), tile)
        for b in range(blocks):
            spec[b] = dot(table_ref[...], k[b * BLOCK : (b + 1) * BLOCK, columns])

        def shift_product(sign, re, im, lanes):
            at = pl.ds(pl.multiple_of(t * tile + lanes.start, LANES), LANES)
            tr = tapspec[re, at]
            ti = tapspec[im, at]
            before = None
            for b in range(blocks):
                xr = spec[b, re, lanes]
                xi = spec[b, im, lanes]
                if b == 0:
                    sr, si = xr, xi
                else:
                    sr, si = xr - sign * before[1], xi + sign * before[0]
                before = (xr, xi)
                yr, yi = multiply(sr, si, tr, ti)
                prod[b, re, lanes] = yr.astype(BF16)
                prod[b, im, lanes] = yi.astype(BF16)

        spectral_loop(tile, shift_product)
        for b in range(blocks):
            rows = slice(b * BLOCK, (b + 1) * BLOCK)
            shifted = dot(back_ref[...], prod[b])
            shifted_ref[rows, :] = shifted.astype(BF16)
            mixed_ref[rows, :] = (shifted * v[rows, columns].astype(F32)).astype(BF16)
            spec[b] = dot(table_ref[...], mixed_ref[rows, :])

        def state_product(sign, re, im, lanes):
            at = pl.ds(pl.multiple_of(t * tile + lanes.start, LANES), LANES)
            s = [(spec[b, re, lanes], spec[b, im, lanes]) for b in range(blocks)]
            h = [(kern[b, re, at].astype(F32), kern[b, im, at].astype(F32)) for b in range(blocks)]
            for i in range(blocks):
                yr, yi = multiply(*s[i], *h[0])
                for d in range(1, i + 1):
                    pr, pi = multiply(*s[i - d], *h[d])
                    yr, yi = yr + pr, yi + pi
                prod[i, re, lanes] = yr.astype(BF16)
                prod[i, im, lanes] = yi.astype(BF16)

        spectral_loop(tile, state_product)
        for b in range(blocks):
            rows = slice(b * BLOCK, (b + 1) * BLOCK)
            state = dot(back_ref[...], prod[b]).astype(BF16)
            state_ref[rows, :] = state
            gated = (q[rows, columns].astype(F32) * state.astype(F32)).astype(BF16)
            total[rows, :] += dot(gated, wout[columns, :])

    @pl.when(j == steps - 1)
    def _():
        def block(b, carry):
            rows = pl.ds(pl.multiple_of(b * BLOCK, BLOCK), BLOCK)
            mask = live_rows(live, b * BLOCK, BLOCK)
            hidden = x[rows, :].astype(F32) + mask * total[rows, :]
            total[rows, :] = hidden
            normed, _ = norm_stats(hidden)
            a_two[rows, :] = (normed * gain_two_ref[...]).astype(BF16)
            return carry

        lax.fori_loop(0, blocks, block, 0)
        outs[7].start()
        outs[8].start()
        for copy in outs:
            copy.wait()
        own_cot.wait()
        other_cot.wait()


def mixer_call(live, tokens, cot, own, taps, gain_one, gain_two, wq, wk, wv, wout, tables, tile):
    _, half, width = tokens.shape
    length = 2 * half
    blocks = length // BLOCK
    table, back = tables
    states, channels = taps.shape
    anywhere = pl.BlockSpec(memory_space=pl.ANY)
    rows_tile = pl.BlockSpec((length, tile), lambda j: (0, jnp.maximum(j - 1, 0)))
    low = lambda *shape: jax.ShapeDtypeStruct(shape, BF16)
    full = lambda *shape: jax.ShapeDtypeStruct(shape, F32)
    vmem = lambda *shape: pltpu.VMEM(shape, BF16)
    wide = lambda *shape: pltpu.VMEM(shape, F32)
    sems = lambda *shape: pltpu.SemaphoreType.DMA(shape)
    rows = low(length, width)
    return pl.pallas_call(
        mixer_body,
        grid=(1 + width // tile,),
        in_specs=[
            pl.BlockSpec(memory_space=pltpu.SMEM),
            anywhere,
            anywhere,
            once(own.shape),
            once(taps.shape),
            once((1, width)),
            once((1, width)),
            anywhere,
            anywhere,
            anywhere,
            anywhere,
            once(table.shape),
            once(back.shape),
        ],
        out_specs=[anywhere] * 10 + [rows_tile] * 3,
        out_shape=[
            rows, rows, rows, rows, rows, rows,
            low(blocks, 2 * BLOCK, width), full(2 * BLOCK, width), full(length, width), rows,
            rows, rows, rows,
        ],
        scratch_shapes=[
            vmem(length, width),
            vmem(length, width),
            vmem(length, width),
            vmem(length, width),
            vmem(length, width),
            wide(length, width),
            vmem(length, width),
            vmem(*wq.shape),
            vmem(*wk.shape),
            vmem(*wv.shape),
            vmem(*wout.shape),
            vmem(blocks, 2 * BLOCK, width),
            wide(2 * BLOCK, width),
            vmem(states, width),
            wide(2, states, 2 * LANES),
            wide(2, states, LANES),
            vmem(length, width),
            wide(states, 32, LANES),
            wide(length // 256, states, 8, LANES),
            wide(blocks, 2 * BLOCK, tile),
            vmem(blocks, 2 * BLOCK, tile),
            sems(4),
            sems(2),
            sems(9),
            sems(2),
            sems(2),
            sems(2),
            sems(2),
            sems(3, 2),
        ],
        compiler_params=pltpu.CompilerParams(vmem_limit_bytes=VMEM_BYTES, collective_id=3, has_side_effects=True),
        cost_estimate=cost(16e9, 40e6),
        name="mixer_forward",
    )(live, tokens, cot, own, taps, gain_one, gain_two, wq, wk, wv, wout, table, back)


ORDER = {UP: "zxxz", DOWN: "YYYY", GATE: "xx", KERN: "x", KV: "xX"}
FEED_PLAN = {
    (0, 4): ((DOWN, 0, 0, 1),),
    (0, 5): ((UP, 0, 0, 1),),
    (1, 1): ((DOWN, 0, 0, 0), (UP, 0, 0, 0), (DOWN, 0, 1, 1), (UP, 0, 1, 1)),
    (1, 4): ((DOWN, 1, 0, 1),),
    (1, 5): ((UP, 1, 0, 1),),
    (2, 1): ((DOWN, 1, 0, 0), (DOWN, 0, 1, 0), (UP, 0, 1, 0), (UP, 1, 0, 0), (DOWN, 1, 1, 1), (UP, 1, 1, 1), (UP, 0, 2, 1)),
    (2, 4): ((DOWN, 2, 0, 1),),
    (2, 5): ((UP, 2, 0, 1), (DOWN, 0, 2, 1)),
    (3, 1): ((DOWN, 2, 0, 0), (DOWN, 1, 1, 0), (UP, 1, 1, 0), (UP, 0, 2, 0), (UP, 2, 0, 0), (DOWN, 2, 1, 1), (UP, 2, 1, 1), (UP, 1, 2, 1)),
    (3, 3): ((DOWN, 0, 2, 0), (DOWN, 0, 3, 1)),
    (3, 4): ((DOWN, 3, 0, 1),),
    (3, 5): ((UP, 1, 2, 0), (UP, 3, 0, 1), (DOWN, 1, 2, 1)),
    (4, 1): ((UP, 1, 3, 1),),
    (4, 4): ((DOWN, 3, 0, 0), (DOWN, 2, 1, 0), (UP, 2, 1, 0)),
    (4, 5): ((DOWN, 0, 3, 0), (UP, 3, 0, 0), (GATE, 0, 0, 1), (UP, 0, 3, 1)),
    (4, 7): ((DOWN, 1, 2, 0), (GATE, 1, 0, 1)),
}
FEED_LEFT = (
    (DOWN, 3, 0, True),
    (UP, 3, 0, True),
    (DOWN, 2, 1, True),
    (DOWN, 1, 2, True),
    (UP, 2, 1, True),
    (DOWN, 0, 3, True),
    (UP, 1, 3, False),
    (GATE, 0, 0, False),
    (UP, 0, 3, False),
    (GATE, 1, 0, False),
)


def ffn_body(
    length_ref, a_two_ref, cot_ref, gain_ref, up_ref, down_ref, hidden_hbm, wout_hbm, state_hbm, q_hbm, a_one_hbm,
    out_hbm, d_hidden_hbm, d_query_hbm, d_state_hbm, gain_grad_ref, up_out, down_out, *rest,
):
    left = rest[: len(FEED_LEFT)]
    (
        total, back, act, d_pre, d_down, hidden, wout, state, q, a_one, in_sems, out_sems,
        up_flat, up_side, down_flat, down_side, gate_base, up_sems, down_sems, gate_sems, *lands,
    ) = rest[len(FEED_LEFT) :]
    j = pl.program_id(0)
    quarters = 4
    length, width = a_two_ref.shape
    tile = up_ref.shape[1]
    live = length_ref[0]
    rows_count = 256

    sums = {}
    lands = list(lands)
    up_bases, down_bases = (up_flat, up_side), (down_flat, down_side)

    def take(count):
        taken = lands[:count]
        del lands[:count]
        return taken

    for t in range(quarters):
        order, sideways = ORDER[UP][t], ORDER[DOWN][t] == "Y"

        def keep_up(own, given, sideways, t=t):
            put(up_out, t * tile, own, given, sideways)

        def keep_down(own, given, sideways):
            put(down_out, 0, own, given, sideways)

        refs = [up_bases[order in "XZ"]] + take(6 if order in "XZ" else 5)
        sums[UP, t] = Sum(refs, up_sems.at[t], order, keep_up)
        refs = [down_bases[sideways]] + take(6 if sideways else 5)
        sums[DOWN, t] = Gather(t, refs, down_sems.at[t], sideways, keep_down)
    for i in range(2):
        sums[GATE, i] = Sum([gate_base.at[i]] + take(5), gate_sems.at[i], ORDER[GATE][i])

    def run(step, number):
        follow(sums, FEED_PLAN.get((step, number), ()))

    def slot(step, number):
        if FEED_PLAN.get((step, number)):

            @pl.when(j == step)
            def _():
                run(step, number)

    def slots(number):
        for step in range(quarters):
            slot(step, number)

    late = [
        pltpu.make_async_copy(source, target, in_sems.at[i])
        for i, (source, target) in enumerate(
            ((hidden_hbm, hidden), (q_hbm, q), (state_hbm, state), (wout_hbm, wout), (a_one_hbm, a_one))
        )
    ]

    @pl.when(j == 0)
    def _():
        for copy in late:
            copy.start()
        greet((CORE, MIDDLE, NEAR, FAR, SIDE))
        for low in range(0, length, rows_count):
            rows = slice(low, low + rows_count)
            d_down[rows, :] = (cot_ref[rows, :].astype(F32) * live_rows(live, low, rows_count)).astype(BF16)
        total[...] = jnp.zeros_like(total)
        back[...] = jnp.zeros_like(back)
        down_out[...] = jnp.zeros_like(down_out)
        up_out[...] = jnp.zeros_like(up_out)

    def chunk(low):
        rows = pl.ds(low, rows_count)
        pre = dot(a_two_ref[rows, :], up_ref[...])
        d_act = dot_nt(d_down[rows, :], down_ref[...])
        value, slope = gelu_pair(pre)
        act[rows, :] = value.astype(BF16)
        d_pre[rows, :] = (d_act * slope).astype(BF16)
        total[rows, :] += dot(act[rows, :], down_ref[...])
        back[rows, :] += dot_nt(d_pre[rows, :], up_ref[...])

    @pl.when(j < quarters)
    def _():
        def step(part, carry):
            chunk(pl.multiple_of(part * rows_count, rows_count))
            for t in range(1, quarters):
                for number in range(4):
                    if FEED_PLAN.get((t, number)):
                        pl.when(jnp.logical_and(j == t, part == number))(functools.partial(run, t, number))
            return carry

        lax.fori_loop(0, 4, step, 0)

    share = tile // 4
    for sideways in (False, True):
        steps = [t for t in range(quarters) if (ORDER[DOWN][t] == "Y") == sideways]

        @pl.when(functools.reduce(jnp.logical_or, [j == t for t in steps], False))
        def _(sideways=sideways):
            value = dot_tn(act[...], d_down[...]).astype(BF16)
            side = lax.axis_index("seq")
            for owner, (core, x) in enumerate(places(lax.axis_index("dp"), 4, (1, 2))):
                rows = value[owner * share : (owner + 1) * share]
                if sideways:
                    down_side[core, side, x] = rows[:, : width // 2]
                    down_side[core, 1 - side, x] = rows[:, width // 2 :]
                else:
                    down_flat[core, x] = rows

    slots(4)

    for sideways in (False, True):
        steps = [t for t in range(quarters) if (ORDER[UP][t] in "XZ") == sideways]

        @pl.when(functools.reduce(jnp.logical_or, [j == t for t in steps], False))
        def _(sideways=sideways):
            spread(dot_tn(a_two_ref[...], d_pre[...]), up_bases[sideways], sideways)

    slots(5)

    def send(source, target, number):
        return pltpu.make_async_copy(source, target, out_sems.at[number])

    @pl.when(j == quarters)
    def _():
        run(4, 0)
        late[0].wait()
        late[1].wait()
        late[2].wait()
        gain_sum = jnp.zeros((1, width), F32)
        for low in range(0, length, rows_count):
            rows = slice(low, low + rows_count)
            mask = live_rows(live, low, rows_count)
            before = hidden[rows, :]
            d_pre[rows, :] = (before + mask * total[rows, :]).astype(BF16)
            normed, inv = norm_stats(before)
            grad_in = back[rows, :]
            gain_sum = gain_sum + jnp.sum(grad_in * normed, axis=0, keepdims=True)
            d_hidden = cot_ref[rows, :].astype(F32) + norm_pull(grad_in, normed, inv, gain_ref[...])
            back[rows, :] = d_hidden
            d_down[rows, :] = (mask * d_hidden).astype(BF16)
            gated = q[rows, :].astype(F32) * state[rows, :].astype(F32)
            act[rows, :] = gated.astype(BF16)
            run(4, 1 + low // rows_count)
        gain_grad_ref[...] = gain_sum
        copies = [send(d_pre, out_hbm, 0), send(back, d_hidden_hbm, 1)]
        for copy in copies:
            copy.start()
        spread(dot_tn(act[...], d_down[...]), gate_base.at[0])
        run(4, 5)
        late[3].wait()
        late[4].wait()
        for low in range(0, length, rows_count):
            rows = slice(low, low + rows_count)
            d_gated = dot_nt(d_down[rows, :], wout[...])
            total[rows, :] = d_gated
            act[rows, :] = (d_gated * state[rows, :].astype(F32)).astype(BF16)
        copies.append(send(act, d_query_hbm, 2))
        copies[2].start()
        run(4, 6)
        spread(dot_tn(a_one[...], act[...]), gate_base.at[1])
        run(4, 7)
        for low in range(0, length, rows_count):
            rows = slice(low, low + rows_count)
            d_down[rows, :] = (total[rows, :] * q[rows, :].astype(F32)).astype(BF16)
        copies.append(send(d_down, d_state_hbm, 3))
        copies[3].start()
        run(4, 8)
        for i, (name, index, exchange, waited) in enumerate(FEED_LEFT):
            if not waited:
                sums[name, index].wait(exchange)
            copies.append(send(sums[name, index].refs[exchange + 1], left[i], 4 + i))
            copies[-1].start()
        for copy in copies:
            copy.wait()


def ffn_call(live, a_two, cot, hidden, gain, up, down, wout, state, q, a_one):
    length, width = a_two.shape
    hidden_units = up.shape[1]
    tile = hidden_units // 4
    su, sd = width // 16, tile // 4
    rows_full = once((length, width))
    anywhere = pl.BlockSpec(memory_space=pl.ANY)
    low = lambda *shape: jax.ShapeDtypeStruct(shape, BF16)
    full = lambda *shape: jax.ShapeDtypeStruct(shape, F32)
    vmem = lambda *shape: pltpu.VMEM(shape, BF16)
    wide = lambda *shape: pltpu.VMEM(shape, F32)
    sems = lambda *shape: pltpu.SemaphoreType.DMA(shape)
    shape_of = {}
    for t in range(4):
        shape_of[UP, t] = landings(su, tile, ORDER[UP][t])
        shape_of[DOWN, t] = gather_landings(sd, width, ORDER[DOWN][t] == "Y")
    for i in range(2):
        shape_of[GATE, i] = landings(su, width, ORDER[GATE][i])
    left = [low(*shape_of[name, index][exchange].shape) for name, index, exchange, _ in FEED_LEFT]
    for name, index, exchange, _ in FEED_LEFT:
        shapes = shape_of[name, index]
        shapes[exchange + 1 :] = [vmem(16, LANES)] * (len(shapes) - exchange - 1)
    lands = [shape for shapes in shape_of.values() for shape in shapes]
    return pl.pallas_call(
        ffn_body,
        grid=(5,),
        in_specs=[
            pl.BlockSpec(memory_space=pltpu.SMEM),
            rows_full,
            rows_full,
            once((1, width)),
            pl.BlockSpec((width, tile), lambda j: (0, jnp.minimum(j, 3))),
            pl.BlockSpec((tile, width), lambda j: (jnp.minimum(j, 3), 0)),
        ]
        + [anywhere] * 5,
        out_specs=[anywhere] * 4 + [once((1, width)), once((su, hidden_units)), once((sd, width))] + [anywhere] * len(left),
        out_shape=[
            low(length, width),
            full(length, width),
            low(length, width),
            low(length, width),
            full(1, width),
            full(su, hidden_units),
            full(sd, width),
            *left,
        ],
        scratch_shapes=[
            wide(length, width),
            wide(length, width),
            vmem(length, tile),
            vmem(length, tile),
            vmem(length, width),
            wide(length, width),
            vmem(*wout.shape),
            vmem(length, width),
            vmem(length, width),
            vmem(length, width),
            sems(5),
            sems(4 + len(left)),
            vmem(*base_shape(su, tile, "x")) if set(ORDER[UP]) & set("xz") else vmem(16, LANES),
            vmem(*base_shape(su, tile, "X")) if set(ORDER[UP]) & set("XZ") else vmem(16, LANES),
            vmem(2, 2, sd, width) if "n" in ORDER[DOWN] else vmem(16, LANES),
            vmem(2, 2, 2, sd, width // 2) if "Y" in ORDER[DOWN] else vmem(16, LANES),
            vmem(2, *base_shape(su, width, "x")),
            sems(4, 6, 2),
            sems(4, 6, 2),
            sems(2, 5, 2),
            *lands,
        ],
        compiler_params=pltpu.CompilerParams(vmem_limit_bytes=62 * 1024 * 1024, collective_id=1, has_side_effects=True),
        cost_estimate=cost(12 * length * width * hidden_units, 40e6),
        name="feed_forward",
    )(live, a_two, cot, gain, up, down, hidden, wout, state, q, a_one)


BACK_PLAN = {
    (0, 0): ((OUT, 0, 0, 1), (OUT, 1, 0, 1), (UP, 3, 1, 1), (GATE, 0, 1, 1), (GATE, 1, 1, 1), (DOWN, 1, 3, 1), (DOWN, 0, 4, 1)),
    (1, 1): ((UP, 2, 2, 1),),
    (2, 1): ((DOWN, 1, 3, 0),),
    (2, 2): ((DOWN, 0, 4, 0),),
    (2, 3): ((KERN, 0, 0, 1),),
    (3, 2): ((DOWN, 2, 2, 1), (DOWN, 1, 4, 1)),
    (3, 4): ((UP, 3, 1, 0), (GATE, 0, 1, 0), (GATE, 1, 1, 0), (UP, 2, 2, 0), (KERN, 0, 0, 0), (KERN, 0, 1, 1), (UP, 3, 2, 1)),
    (3, 5): ((DOWN, 3, 1, 1), (VALUE, 0, 0, 1), (KEY, 0, 0, 1), (GATE, 0, 2, 1), (DOWN, 0, 5, 1)),
    (4, 2): ((OUT, 0, 0, 0), (OUT, 1, 0, 0), (DOWN, 2, 2, 0), (DOWN, 1, 4, 0)),
    (4, 3): ((VALUE, 0, 0, 0), (KEY, 0, 0, 0), (VALUE, 0, 1, 1), (KEY, 0, 1, 1)),
    (4, 4): ((DOWN, 2, 3, 1), (GATE, 1, 2, 1)),
    (4, 5): ((DOWN, 0, 5, 0), (VALUE, 1, 0, 1), (KEY, 1, 0, 1)),
    (5, 1): ((GATE, 0, 2, 0), (UP, 3, 2, 0), (UP, 3, 3, 1), (DOWN, 1, 5, 1)),
    (5, 2): ((UP, 1, 4, 1),),
    (5, 3): ((VALUE, 1, 0, 0), (KEY, 1, 0, 0), (VALUE, 0, 1, 0), (KEY, 0, 1, 0), (VALUE, 1, 1, 1), (KEY, 1, 1, 1), (VALUE, 0, 2, 1)),
    (5, 4): ((KERN, 0, 1, 0), (DOWN, 3, 1, 0), (KERN, 0, 2, 1), (KEY, 0, 2, 1), (UP, 0, 4, 1)),
    (5, 5): ((UP, 3, 3, 0), (DOWN, 3, 2, 1), (VALUE, 2, 0, 1), (TAPS, 0, 0, 1), (KEY, 2, 0, 1)),
    (5, 7): ((UP, 1, 4, 0), (DOWN, 2, 3, 0), (GATE, 1, 2, 0), (DOWN, 2, 4, 1), (ROW, 0, 0, 1)),
    (5, 8): ((DOWN, 1, 5, 0), (ROW, 1, 0, 1)),
    (5, 9): ((VALUE, 0, 2, 0), (VALUE, 2, 0, 0), (TAPS, 0, 0, 0), (KEY, 2, 0, 0), (TAPS, 0, 1, 1)),
    (5, 10): ((KEY, 0, 2, 0), (VALUE, 1, 1, 0), (KEY, 1, 1, 0), (UP, 0, 4, 0), (KEY, 2, 1, 1)),
    (5, 11): ((GAIN, 0, 0, 1),),
}
BACK_LEFT = (
    (KEY, 1, 2, 1),
    (DOWN, 3, 2, 0),
    (VALUE, 1, 2, 1),
    (GAIN, 0, 0, 0),
    (DOWN, 3, 3, 1),
    (UP, 2, 3, 1),
    (GAIN, 0, 1, 1),
    (KERN, 0, 2, 0),
    (TAPS, 0, 1, 0),
    (DOWN, 2, 4, 0),
    (KEY, 1, 2, 0),
    (KERN, 0, 3, 1),
    (KEY, 2, 1, 0),
    (VALUE, 1, 2, 0),
    (GAIN, 0, 1, 0),
    (TAPS, 0, 2, 1),
    (UP, 2, 3, 0),
    (KEY, 2, 2, 1),
    (GATE, 0, 3, 1),
    (DOWN, 3, 3, 0),
    (VALUE, 2, 1, 1),
    (DOWN, 3, 4, 1),
    (TAPS, 0, 2, 0),
    (DOWN, 2, 5, 1),
    (KERN, 0, 3, 0),
    (GATE, 1, 3, 1),
    (ROW, 0, 0, 0),
    (KERN, 0, 4, 1),
    (KEY, 2, 2, 0),
    (ROW, 1, 0, 0),
    (UP, 3, 4, 1),
    (UP, 2, 4, 1),
    (VALUE, 2, 1, 0),
    (GATE, 0, 3, 0),
    (VALUE, 2, 2, 1),
    (GAIN, 0, 2, 1),
    (VALUE, 0, 3, 1),
    (DOWN, 2, 5, 0),
    (KERN, 0, 4, 0),
    (COEF, 0, 0, 1),
    (GATE, 0, 4, 1),
    (VALUE, 1, 3, 1),
    (TAPS, 0, 3, 1),
    (VALUE, 2, 2, 0),
    (VALUE, 2, 3, 1),
    (KEY, 0, 3, 1),
    (GATE, 1, 3, 0),
    (GATE, 1, 4, 1),
    (COEF, 0, 0, 0),
    (GAIN, 0, 2, 0),
    (COEF, 0, 1, 1),
    (GAIN, 0, 3, 1),
    (UP, 3, 4, 0),
    (UP, 2, 4, 0),
    (KEY, 1, 3, 1),
    (VALUE, 0, 3, 0),
    (DOWN, 3, 4, 0),
    (DOWN, 3, 5, 1),
    (VALUE, 1, 3, 0),
    (GATE, 0, 4, 0),
    (KEY, 2, 3, 1),
    (VALUE, 0, 4, 1),
    (VALUE, 2, 3, 0),
    (TAPS, 0, 3, 0),
    (TAPS, 0, 4, 1),
    (VALUE, 1, 4, 1),
    (GATE, 1, 4, 0),
    (COEF, 0, 1, 0),
    (KEY, 0, 3, 0),
    (COEF, 0, 2, 1),
    (KEY, 0, 4, 1),
    (VALUE, 2, 4, 1),
    (GAIN, 0, 3, 0),
    (GAIN, 0, 4, 1),
    (KEY, 1, 3, 0),
    (KEY, 1, 4, 1),
    (TAPS, 0, 4, 0),
    (VALUE, 0, 4, 0),
    (VALUE, 0, 5, 1),
    (DOWN, 3, 5, 0),
    (KEY, 0, 4, 0),
    (KEY, 2, 3, 0),
    (KEY, 2, 4, 1),
    (COEF, 0, 2, 0),
    (VALUE, 1, 4, 0),
    (COEF, 0, 3, 1),
    (VALUE, 1, 5, 1),
    (VALUE, 2, 4, 0),
    (VALUE, 2, 5, 1),
    (GAIN, 0, 4, 0),
    (KEY, 1, 4, 0),
    (VALUE, 0, 5, 0),
    (KEY, 2, 4, 0),
    (VALUE, 1, 5, 0),
    (VALUE, 2, 5, 0),
    (COEF, 0, 3, 0),
)


def mixer_back_body(
    length_ref, out_row_ref, d_state_ref, d_query_ref, mixed_ref, shifted_ref, k_ref, v_ref,
    wq_ref, wk_ref, wv_ref, kern_ref, tapspec_ref, table_ref, back_ref, gain_ref, gain_two_grad_ref,
    coef_ref, rate_ref, up_part_ref, down_part_ref, *rest,
):
    left = rest[: len(FEED_LEFT)]
    (
        a_one_hbm, x_hbm, d_hidden_hbm,
        out_ref, d_tokens_ref, gains_out, taps_out, coef_out, rate_out, up_ref, down_ref, gate_out, kv_out,
        total, spec_one, spec_two, prod, shift_prod, d_keys, d_values, d_x, a_one, x, d_hidden, d_taps, d_kern,
        gain_refs, gain_lands, gain_sems, taps_base, taps_sems, coef_base, coef_sems,
        kern_base, key_base, value_base, left_sems, kern_sems, kv_sems, out_sems, row_sems, own_sems, in_sems, *lands,
    ) = rest[len(FEED_LEFT) :]
    j = pl.program_id(0)
    length, width = a_one.shape
    half = length // 2
    tile = k_ref.shape[1]
    tiles = width // tile
    blocks = length // BLOCK
    live = length_ref[0]
    side = lax.axis_index("seq")
    own_rows = pl.ds(pl.multiple_of(side * half, half), half)

    sums = {}
    lands = list(lands)
    kv_bases = (key_base, value_base)

    def take(count):
        taken = lands[:count]
        del lands[:count]
        return taken

    for i, (name, index, exchange, _) in enumerate(FEED_LEFT):

        def keep(own, given, sideways, name=name, index=index):
            if name == UP:
                put(up_ref, index * width, own, given, sideways)
            elif name == DOWN:
                put(down_ref, 0, own, given, sideways)
            else:
                put(gate_out.at[index], 0, own, given, sideways)

        order = ORDER[name][index]
        refs = [None] * (exchange + 1) + [left[i]] + take((5 if order in "XZY" else 4) - exchange)
        if name == DOWN:
            sums[name, index] = Gather(index, refs, left_sems.at[i], order == "Y", keep)
        else:
            sums[name, index] = Sum(refs, left_sems.at[i], order, keep)

    states, channels = rate_ref.shape
    each = states // 16

    def keep_kern(own, given, sideways):
        put(d_kern, 0, own, given, sideways)
        steps = d_kern.shape[0]
        first = lax.convert_element_type(lax.axis_index("dp") * steps, F32)
        for low in range(0, channels, LANES):
            lanes = slice(low, low + LANES)
            rate = rate_ref[:, lanes]
            from_lane = pl.ds(pl.multiple_of(side * channels + low, LANES), LANES)

            def group(g, sums, rate=rate, from_lane=from_lane):
                coef_sum, rate_sum = sums
                rows = d_kern[pl.ds(pl.multiple_of(g * 8, 8), 8), from_lane]
                for i in range(8):
                    time = first + lax.convert_element_type(g * 8 + i, F32)
                    term = jnp.exp(rate * -time) * rows[i : i + 1]
                    coef_sum = coef_sum + term
                    rate_sum = rate_sum + term * time
                return coef_sum, rate_sum

            zeros = jnp.zeros((states, LANES), F32)
            coef_sum, rate_sum = lax.fori_loop(0, steps // 8, group, (zeros, zeros))
            rate_sum = -coef_ref[:, lanes] * rate_sum
            for owner, place in enumerate(places(lax.axis_index("dp"), 16, (1, 2, 4, 8))):
                rows = slice(owner * each, (owner + 1) * each)
                coef_base[(*place, slice(0, each), lanes)] = coef_sum[rows]
                coef_base[(*place, slice(each, 2 * each), lanes)] = rate_sum[rows]

    def keep_coef(value):
        flat = jnp.transpose(value)
        coef_out[...] = flat[:, :each]
        rate_out[...] = flat[:, each:]

    def keep_taps(own, given, sideways):
        both = jnp.concatenate([own + given] * 2, axis=0)
        flat = jnp.where(side == 0, both[:, :channels], both[:, channels:])
        taps_out[...] = jnp.transpose(flat)[:, :each]

    sums[COEF, 0] = Sum([coef_base] + take(4), coef_sems, "x", keep_coef, across=False)
    sums[TAPS, 0] = Sum([taps_base] + take(5), taps_sems, "x", keep_taps)
    sums[GAIN, 0] = Whole(gain_refs, gain_lands, gain_sems)

    for i in range(2):
        piece = pl.ds(i * (half // 2), half // 2)
        other = pl.ds(pl.multiple_of((1 - side) * half + i * (half // 2), half // 2), half // 2)
        sums[OUT, i] = Rows(out_row_ref.at[other], out_ref.at[side, piece], out_sems.at[i])
        sums[ROW, i] = Rows(d_x.at[0, piece], d_tokens_ref.at[side, piece], row_sems.at[i])
    kern_sideways = ORDER[KERN] in "XZ"
    sums[KERN, 0] = Sum([kern_base] + take(6 if kern_sideways else 5), kern_sems, ORDER[KERN], keep_kern)
    for t in range(tiles):
        for i, name in enumerate((KEY, VALUE)):

            def keep_kv(own, given, sideways, t=t, i=i):
                put(kv_out.at[i], t * tile, own, given, sideways)

            order = ORDER[KV][i]
            refs = [kv_bases[i].at[t]] + take(6 if order in "XZ" else 5)
            sums[name, t] = Sum(refs, kv_sems.at[t, i], order, keep_kv)

    def events(step, number):
        follow(sums, BACK_PLAN.get((step, number), ()))

    def slots(first, last, number):
        for step in range(first, last):
            if BACK_PLAN.get((step, number)):
                pl.when(j == step)(functools.partial(events, step, number))

    def keep_out():
        return pltpu.make_async_copy(out_row_ref.at[own_rows], out_ref.at[side], own_sems.at[0])

    def keep_row():
        return pltpu.make_async_copy(d_x.at[1], d_tokens_ref.at[side], own_sems.at[1])

    late = [
        pltpu.make_async_copy(source, target, in_sems.at[i])
        for i, (source, target) in enumerate(((a_one_hbm, a_one), (x_hbm, x), (d_hidden_hbm, d_hidden)))
    ]

    @pl.when(j == 0)
    def _():
        greet((CORE, MIDDLE, NEAR, FAR, SIDE))
        events(0, 0)
        keep_out().start()
        for copy in late:
            copy.start()
        up_ref[...] = up_part_ref[...]
        down_ref[...] = down_part_ref[...]

    def kernel_product(sign, re, im, lanes):
        s = [(spec_one[b, re, lanes], spec_one[b, im, lanes]) for b in range(blocks)]
        x = [(spec_two[b, re, lanes], spec_two[b, im, lanes]) for b in range(blocks)]
        after = None
        for d in range(blocks - 1, -1, -1):
            yr, yi = multiply_conj(*x[0], *s[d])
            for i in range(d + 1, blocks):
                pr, pi = multiply_conj(*x[i - d], *s[i])
                yr, yi = yr + pr, yi + pi
            if after is None:
                hr, hi = yr, yi
            else:
                hr, hi = yr + sign * after[1], yi - sign * after[0]
            after = (yr, yi)
            prod[d, re, lanes] = hr.astype(BF16)
            prod[d, im, lanes] = hi.astype(BF16)

    @pl.when(j < tiles)
    def _():
        for b in range(blocks):
            rows = slice(b * BLOCK, (b + 1) * BLOCK)
            spec_one[b] = dot(table_ref[...], d_state_ref[rows, :])
            spec_two[b] = dot(table_ref[...], mixed_ref[rows, :])

    slots(0, tiles, 1)

    @pl.when(j < tiles)
    def _():
        spectral_loop(tile, kernel_product)

    slots(0, tiles, 2)

    @pl.when(j < tiles)
    def _():
        parts = [dot(back_ref[...], prod[b]) * (1.0 / BLOCK) for b in range(blocks)]
        kern_parts = jnp.concatenate(parts, axis=0)
        if kern_sideways:
            columns = pl.ds(pl.multiple_of(j * (tile // 2), tile // 2), tile // 2)
        else:
            columns = pl.ds(pl.multiple_of(j * tile, tile), tile)
        spread(kern_parts, kern_base.at[..., columns], kern_sideways)

    @pl.when(j == tiles - 1)
    def _():
        total[...] = jnp.zeros_like(total)
        late[0].wait()

    slots(0, tiles, 3)

    def state_product(sign, re, im, lanes):
        s = [(spec_one[b, re, lanes], spec_one[b, im, lanes]) for b in range(blocks)]
        h = [(kern_ref[b, re, lanes].astype(F32), kern_ref[b, im, lanes].astype(F32)) for b in range(blocks)]
        for b in range(blocks):
            yr, yi = multiply_conj(*h[0], *s[b])
            for i in range(b + 1, blocks):
                pr, pi = multiply_conj(*h[i - b], *s[i])
                yr, yi = yr + pr, yi + pi
            prod[b, re, lanes] = yr.astype(BF16)
            prod[b, im, lanes] = yi.astype(BF16)

    @pl.when(j >= tiles)
    def _():
        for b in range(blocks):
            spec_one[b] = dot(table_ref[...], d_state_ref[b * BLOCK : (b + 1) * BLOCK, :])

    slots(tiles, 2 * tiles, 1)

    @pl.when(j >= tiles)
    def _():
        spectral_loop(tile, state_product)

    slots(tiles, 2 * tiles, 2)

    @pl.when(j >= tiles)
    def _():
        for b in range(blocks):
            rows = slice(b * BLOCK, (b + 1) * BLOCK)
            mask = live_rows(live, b * BLOCK, BLOCK)
            d_mixed = dot(back_ref[...], prod[b]).astype(BF16).astype(F32)
            d_values[rows, :] = (mask * d_mixed * shifted_ref[rows, :].astype(F32)).astype(BF16)
            d_shifted = (d_mixed * v_ref[rows, :].astype(F32)).astype(BF16)
            spec_one[b] = dot(table_ref[...], d_shifted)
            spec_two[b] = dot(table_ref[...], k_ref[rows, :])

    slots(tiles, 2 * tiles, 3)

    def shift_product(sign, re, im, lanes):
        tr = tapspec_ref[re, lanes]
        ti = tapspec_ref[im, lanes]
        s = [(spec_one[b, re, lanes], spec_one[b, im, lanes]) for b in range(blocks)]
        x = [(spec_two[b, re, lanes], spec_two[b, im, lanes]) for b in range(blocks)]
        u = [multiply_conj(tr, ti, *s[b]) for b in range(blocks)]
        sum_re, sum_im = multiply_conj(*x[0], *s[0])
        for b in range(blocks):
            yr, yi = u[b]
            if b < blocks - 1:
                yr, yi = yr + sign * u[b + 1][1], yi - sign * u[b + 1][0]
            prod[b, re, lanes] = yr.astype(BF16)
            prod[b, im, lanes] = yi.astype(BF16)
            if b > 0:
                wr = x[b][0] - sign * x[b - 1][1]
                wi = x[b][1] + sign * x[b - 1][0]
                pr, pi = multiply_conj(wr, wi, *s[b])
                sum_re, sum_im = sum_re + pr, sum_im + pi
        shift_prod[re, lanes] = sum_re.astype(BF16)
        shift_prod[im, lanes] = sum_im.astype(BF16)

    def token_grad(rows):
        return (
            total[rows, :]
            + dot_nt(d_query_ref[rows, :], wq_ref[...])
            + dot_nt(d_keys[rows, :], wk_ref[...])
            + dot_nt(d_values[rows, :], wv_ref[...])
        )

    @pl.when(j >= tiles)
    def _():
        spectral_loop(tile, shift_product)

    slots(tiles, 2 * tiles, 4)

    @pl.when(j >= tiles)
    def _():
        for b in range(blocks):
            rows = slice(b * BLOCK, (b + 1) * BLOCK)
            mask = live_rows(live, b * BLOCK, BLOCK)
            d_keys[rows, :] = (mask * dot(back_ref[...], prod[b])).astype(BF16)
        taps = d_taps.shape[0]
        columns = pl.ds(pl.multiple_of((j - tiles) * tile, tile), tile)
        d_taps[:, columns] = dot(back_ref[:taps, :], shift_prod[...]) * (1.0 / BLOCK)
        spread(dot_tn(a_one[...], d_keys[...]), key_base.at[j - tiles], ORDER[KV][0] in "XZ")
        spread(dot_tn(a_one[...], d_values[...]), value_base.at[j - tiles], ORDER[KV][1] in "XZ")

    @pl.when(j == 2 * tiles - 1)
    def _():
        for owner, place in enumerate(places(lax.axis_index("dp"), 16, (1, 2, 4, 8))):
            taps_base[place] = d_taps[owner * each : (owner + 1) * each, :]

    slots(tiles, 2 * tiles, 5)

    @pl.when(jnp.logical_and(j >= tiles, j < 2 * tiles - 1))
    def _():
        for b in range(blocks):
            rows = slice(b * BLOCK, (b + 1) * BLOCK)
            total[rows, :] = token_grad(rows)

    slots(tiles, 2 * tiles, 6)

    @pl.when(j == 2 * tiles - 1)
    def _():
        late[1].wait()
        late[2].wait()
        gain_sum = jnp.zeros((1, width), F32)
        count = half // BLOCK
        for b in range(2 * count):
            low = (1 - side if b < count else side) * half + (b % count) * BLOCK
            rows = pl.ds(pl.multiple_of(low, BLOCK), BLOCK)
            normed, inv = norm_stats(x[rows, :].astype(F32))
            grad_in = token_grad(rows)
            gain_sum = gain_sum + jnp.sum(grad_in * normed, axis=0, keepdims=True)
            pulled = d_hidden[rows, :] + norm_pull(grad_in, normed, inv, gain_ref[...])
            d_x[b // count, (b % count) * BLOCK : (b % count + 1) * BLOCK, :] = pulled.astype(BF16)
            events(2 * tiles - 1, 7 + b)
        keep_row().start()
        gain_refs[0] = jnp.concatenate([gain_sum, gain_two_grad_ref[...], jnp.zeros((6, width), F32)], axis=0)
        events(2 * tiles - 1, 11)
        follow(sums, BACK_LEFT)
        gains_out[...] = gain_refs[5]
        keep_out().wait()
        keep_row().wait()


def mixer_back_call(
    live, out_row, a_one, d_state, d_query, mixed, shifted, k, v, wq, wk, wv, kern, tapspec, tables, x, gain, d_hidden,
    d_gain_two, coef, rate, begun, taps_count, tile,
):
    length, width = a_one.shape
    blocks = length // BLOCK
    half = length // 2
    table, back = tables
    share = width // 16
    ks = length // 16
    count = width // tile
    both = lambda j: (0, lax.rem(j, count))
    first = lambda j: (0, jnp.minimum(j, count - 1))
    second = lambda j: (0, jnp.maximum(j - count, 0))
    rows_second = pl.BlockSpec((length, tile), second)
    weight = pl.BlockSpec((width, tile), second)
    anywhere = pl.BlockSpec(memory_space=pl.ANY)
    low = lambda *shape: jax.ShapeDtypeStruct(shape, BF16)
    full = lambda *shape: jax.ShapeDtypeStruct(shape, F32)
    vmem = lambda *shape: pltpu.VMEM(shape, BF16)
    wide = lambda *shape: pltpu.VMEM(shape, F32)
    sems = lambda *shape: pltpu.SemaphoreType.DMA(shape)
    up_part, down_part, left = begun
    states, channels = rate.shape
    each = states // 16
    lands = []
    for name, index, exchange, _ in FEED_LEFT:
        order = ORDER[name][index]
        if name == DOWN:
            lands += gather_landings(*down_part.shape, order == "Y")[exchange + 1 :]
        else:
            lands += landings(share, width, order)[exchange + 1 :]
    bits = [(2, 2, 2), (2, 2), (2,), (), ()]
    lands += [wide(*bits[n], 2 * each, channels) for n in range(4)]
    lands += [wide(*bits[n], each, width) for n in range(5)]
    lands += landings(ks, width, ORDER[KERN])
    for t in range(count):
        lands += landings(share, tile, ORDER[KV][0]) + landings(share, tile, ORDER[KV][1])
    out_shape = [
        low(2, half, width),
        low(2, half, width),
        full(8, width),
        full(channels, each),
        full(channels, each),
        full(channels, each),
        full(*up_part.shape),
        full(*down_part.shape),
        full(2, share, width),
        full(2, share, width),
    ]
    return pl.pallas_call(
        mixer_back_body,
        grid=(2 * count,),
        in_specs=[pl.BlockSpec(memory_space=pltpu.SMEM), anywhere]
        + [pl.BlockSpec((length, tile), both), rows_second, pl.BlockSpec((length, tile), first)]
        + [rows_second] * 3
        + [weight] * 3
        + [
            pl.BlockSpec((blocks, 2 * BLOCK, tile), lambda j: (0, 0, jnp.maximum(j - count, 0))),
            pl.BlockSpec((2 * BLOCK, tile), second),
            once(table.shape),
            once(back.shape),
            once((1, width)),
            once((1, width)),
            once(coef.shape),
            once(rate.shape),
            once(up_part.shape),
            once(down_part.shape),
        ]
        + [once(s.shape) for s in left]
        + [anywhere] * 3,
        out_specs=[anywhere, anywhere] + [once(s.shape) for s in out_shape[2:]],
        out_shape=out_shape,
        scratch_shapes=[
            wide(length, width),
            wide(blocks, 2 * BLOCK, tile),
            wide(blocks, 2 * BLOCK, tile),
            vmem(blocks, 2 * BLOCK, tile),
            vmem(2 * BLOCK, tile),
            vmem(length, tile),
            vmem(length, tile),
            vmem(2, half, width),
            vmem(length, width),
            vmem(length, width),
            wide(length, width),
            wide(taps_count, width),
            wide(ks, width),
            wide(6, 8, width),
            wide(5, 8, width),
            sems(5, 2),
            wide(2, 2, 2, 2, each, width),
            sems(5, 2),
            wide(2, 2, 2, 2, 2 * each, channels),
            sems(4, 2),
            vmem(*base_shape(ks, width, ORDER[KERN])),
            vmem(count, *base_shape(share, tile, ORDER[KV][0])),
            vmem(count, *base_shape(share, tile, ORDER[KV][1])),
            sems(len(left), 6, 2),
            sems(6, 2),
            sems(count, 2, 6, 2),
            sems(2, 2),
            sems(2, 2),
            sems(2),
            sems(3),
            *lands,
        ],
        compiler_params=pltpu.CompilerParams(
            vmem_limit_bytes=62 * 1024 * 1024, collective_id=2, has_side_effects=True
        ),
        cost_estimate=cost(26e9, 40e6),
        name="mixer_back",
    )(
        live, out_row, d_state, d_query, mixed, shifted, k, v, wq, wk, wv, kern, tapspec, table, back, gain,
        d_gain_two, coef, rate, up_part, down_part, *left, a_one, x, d_hidden,
    )


MICRO = 2


epsilon = 1e-05
highest = lax.Precision.HIGHEST


def layer_norm(rows, gain):
    center = rows - jnp.mean(rows, axis=-1, keepdims=True)
    spread = jnp.mean(center * center, axis=-1, keepdims=True)
    return center * lax.rsqrt(spread + epsilon) * gain


def exact_gelu(values):
    return jax.nn.gelu(values, approximate=False)


def project(rows, weight):
    return jnp.einsum("rtd,de->rte", rows, weight, preferred_element_type=jnp.float32)


def project_back(rows, weight):
    return jnp.einsum("rte,de->rtd", rows, weight, preferred_element_type=jnp.float32)


def weight_grad(left, right):
    return jnp.einsum("rtd,rte->de", left, right, preferred_element_type=jnp.float32)


def depth_conv(signal, kernel_taps):
    channels = signal.shape[2]
    return lax.conv_general_dilated(
        signal,
        kernel_taps,
        (1,),
        "VALID",
        dimension_numbers=("NWC", "WIO", "NWC"),
        feature_group_count=channels,
        precision=highest,
    )


def shift_conv(extended, taps, length):
    flipped = jnp.transpose(taps[:, ::-1])[:, None, :]
    return depth_conv(extended[:, 1:, :], flipped)[:, :length, :]


def shift_back(extended, taps, length):
    forward_taps = jnp.transpose(taps)[:, None, :]
    return depth_conv(extended, forward_taps)[:, :length, :]


def taps_grad(grad_rows, extended, width_taps):
    rows_count, span, channels = extended.shape
    left = jnp.transpose(extended, (2, 0, 1)).reshape(1, channels * rows_count, span)
    right = jnp.transpose(grad_rows, (2, 0, 1))
    result = lax.conv_general_dilated(
        left,
        right,
        (1,),
        "VALID",
        dimension_numbers=("NCW", "OIW", "NCW"),
        feature_group_count=channels,
        precision=highest,
    )
    return result[0][:, ::-1][:, :width_taps]


def diag_kernel(coef, rate, length):
    steps = lax.iota(jnp.float32, length)
    return jnp.sum(coef[:, :, None] * jnp.exp(-rate[:, :, None] * steps), axis=1)


def dft_tables(length):
    period = 2 * length
    time_index = lax.iota(jnp.int32, length)[:, None]
    freq_index = lax.iota(jnp.int32, length + 1)[None, :]
    phase_index = time_index * freq_index % period
    angles = phase_index.astype(jnp.float32) * (2.0 * math.pi / period)
    cos_table = jnp.cos(angles)
    sin_table = jnp.sin(angles)
    edges = (freq_index == 0) | (freq_index == length)
    weights = jnp.where(edges, 1.0, 2.0).astype(jnp.float32) / period
    return (cos_table, sin_table, cos_table * weights, sin_table * weights)


def spectrum(signal, cos_table, sin_table):
    real_part = jnp.einsum("rtc,tf->rfc", signal, cos_table, precision=highest)
    imag_part = -jnp.einsum("rtc,tf->rfc", signal, sin_table, precision=highest)
    return (real_part, imag_part)


def inverse(real_part, imag_part, cos_weighted, sin_weighted):
    first = jnp.einsum("rfc,tf->rtc", real_part, cos_weighted, precision=highest)
    second = jnp.einsum("rfc,tf->rtc", imag_part, sin_weighted, precision=highest)
    return first - second


def split_channels(
    tokens,
    lengths,
    gain_one,
    w_query,
    w_key,
    w_value,
    w_out,
    gain_two,
    w_up,
    w_down,
    shift_taps,
    diag_coef,
    diag_rate,
    cotangent,
):
    rows_dev, tok_len, model_width = tokens.shape
    length = tok_len * lax.axis_size("seq")
    width_taps = shift_taps.shape[1]
    first_pos = lax.axis_index("seq") * tok_len
    positions = first_pos + lax.iota(jnp.int32, tok_len)
    mask_all = (positions[None, :] < lengths[:, None]).astype(jnp.float32)[:, :, None]
    cos_table, sin_table, cos_weighted, sin_weighted = dft_tables(length)

    def kernel_of(coef_in, rate_in):
        return diag_kernel(coef_in, rate_in, length)

    kernel, kernel_pull = jax.vjp(kernel_of, diag_coef, diag_rate)
    kernel_real = jnp.einsum("ct,tf->fc", kernel, cos_table, precision=highest)
    kernel_imag = -jnp.einsum("ct,tf->fc", kernel, sin_table, precision=highest)
    taps_acc = jnp.zeros(shift_taps.shape, jnp.float32)
    spec_real_acc = jnp.zeros((length + 1, shift_taps.shape[0]), jnp.float32)
    spec_imag_acc = jnp.zeros((length + 1, shift_taps.shape[0]), jnp.float32)
    grad_gain_one = jnp.zeros(gain_one.shape, jnp.float32)
    grad_gain_two = jnp.zeros(gain_two.shape, jnp.float32)
    grad_query = jnp.zeros(w_query.shape, jnp.float32)
    grad_key = jnp.zeros(w_key.shape, jnp.float32)
    grad_value = jnp.zeros(w_value.shape, jnp.float32)
    grad_out = jnp.zeros(w_out.shape, jnp.float32)
    grad_up = jnp.zeros(w_up.shape, jnp.float32)
    grad_down = jnp.zeros(w_down.shape, jnp.float32)
    rows_mb = rows_dev // MICRO
    out_list = []
    dx_list = []
    for micro_step in range(MICRO):
        low_row = micro_step * rows_mb
        x_rows = tokens[low_row : low_row + rows_mb].astype(jnp.float32)
        live_mask = mask_all[low_row : low_row + rows_mb]
        grad_rows = cotangent[low_row : low_row + rows_mb].astype(jnp.float32)
        norm_one, norm_one_pull = jax.vjp(layer_norm, x_rows, gain_one)
        a_one = norm_one.astype(jnp.bfloat16)
        query_rows = project(a_one, w_query)
        key_rows = (project(a_one, w_key) * live_mask).astype(jnp.bfloat16)
        value_rows = (project(a_one, w_value) * live_mask).astype(jnp.bfloat16)
        keys_ch, values_ch = (
            lax.all_to_all(key_rows, "seq", split_axis=2, concat_axis=1, tiled=True),
            lax.all_to_all(value_rows, "seq", split_axis=2, concat_axis=1, tiled=True),
        )
        key_ext = jnp.pad(keys_ch.astype(jnp.float32), ((0, 0), (width_taps, 0), (0, 0)))
        shifted = shift_conv(key_ext, shift_taps, length)
        values_here = values_ch.astype(jnp.float32)
        mixed_ch = (shifted * values_here).astype(jnp.bfloat16)
        mixed_real, mixed_imag = spectrum(mixed_ch.astype(jnp.float32), cos_table, sin_table)
        state = inverse(
            mixed_real * kernel_real - mixed_imag * kernel_imag,
            mixed_real * kernel_imag + mixed_imag * kernel_real,
            cos_weighted,
            sin_weighted,
        )
        state_tok = lax.all_to_all(
            state.astype(jnp.bfloat16), "seq", split_axis=1, concat_axis=2, tiled=True
        )
        state_rows = state_tok.astype(jnp.float32)
        gated_rows = (query_rows * state_rows).astype(jnp.bfloat16)
        hidden = x_rows + live_mask * project(gated_rows, w_out)
        norm_two, norm_two_pull = jax.vjp(layer_norm, hidden, gain_two)
        a_two = norm_two.astype(jnp.bfloat16)
        pre_act = project(a_two, w_up)
        act_value, gelu_pull = jax.vjp(exact_gelu, pre_act)
        activation = act_value.astype(jnp.bfloat16)
        result = hidden + live_mask * project(activation, w_down)
        out_list.append(result.astype(jnp.bfloat16))
        d_down = (live_mask * grad_rows).astype(jnp.bfloat16)
        grad_down = grad_down + weight_grad(activation, d_down)
        d_act = project_back(d_down, w_down)
        d_pre = gelu_pull(d_act)[0].astype(jnp.bfloat16)
        grad_up = grad_up + weight_grad(a_two, d_pre)
        d_a_two = project_back(d_pre, w_up)
        d_hidden_norm, d_gain_two = norm_two_pull(d_a_two)
        grad_gain_two = grad_gain_two + d_gain_two
        d_hidden = grad_rows + d_hidden_norm
        d_mixer = (live_mask * d_hidden).astype(jnp.bfloat16)
        grad_out = grad_out + weight_grad(gated_rows, d_mixer)
        d_gated = project_back(d_mixer, w_out)
        d_query = (d_gated * state_rows).astype(jnp.bfloat16)
        d_state = (d_gated * query_rows).astype(jnp.bfloat16)
        d_state_ch = lax.all_to_all(d_state, "seq", split_axis=2, concat_axis=1, tiled=True)
        grad_real, grad_imag = spectrum(d_state_ch.astype(jnp.float32), cos_table, sin_table)
        d_mixed = inverse(
            kernel_real * grad_real + kernel_imag * grad_imag,
            kernel_real * grad_imag - kernel_imag * grad_real,
            cos_weighted,
            sin_weighted,
        )
        spec_real_acc = spec_real_acc + jnp.sum(
            mixed_real * grad_real + mixed_imag * grad_imag, axis=0
        )
        spec_imag_acc = spec_imag_acc + jnp.sum(
            mixed_real * grad_imag - mixed_imag * grad_real, axis=0
        )
        d_mixed_low = d_mixed.astype(jnp.bfloat16)
        d_mix_ch = d_mixed_low.astype(jnp.float32)
        d_shifted = d_mix_ch * values_here
        d_values_ch = (d_mix_ch * shifted).astype(jnp.bfloat16)
        grad_ext = jnp.pad(d_shifted, ((0, 0), (0, width_taps), (0, 0)))
        d_keys_ch = shift_back(grad_ext, shift_taps, length).astype(jnp.bfloat16)
        taps_acc = taps_acc + taps_grad(d_shifted, key_ext, width_taps)
        keys_back, values_back = (
            lax.all_to_all(d_keys_ch, "seq", split_axis=1, concat_axis=2, tiled=True),
            lax.all_to_all(d_values_ch, "seq", split_axis=1, concat_axis=2, tiled=True),
        )
        mask_low = live_mask.astype(jnp.bfloat16)
        d_keys = keys_back * mask_low
        d_values = values_back * mask_low
        grad_query = grad_query + weight_grad(a_one, d_query)
        grad_key = grad_key + weight_grad(a_one, d_keys)
        grad_value = grad_value + weight_grad(a_one, d_values)
        d_a_one = (
            project_back(d_query, w_query)
            + project_back(d_keys, w_key)
            + project_back(d_values, w_value)
        )
        d_x_norm, d_gain_one = norm_one_pull(d_a_one)
        grad_gain_one = grad_gain_one + d_gain_one
        dx_list.append((d_hidden + d_x_norm).astype(jnp.bfloat16))
    d_kernel = jnp.einsum("fc,tf->ct", spec_real_acc, cos_weighted, precision=highest) - jnp.einsum(
        "fc,tf->ct", spec_imag_acc, sin_weighted, precision=highest
    )
    d_coef, d_rate = kernel_pull(d_kernel)
    taps_part, coef_part, rate_part = (
        lax.psum_scatter(
            taps_acc.astype(jnp.bfloat16), "dp", scatter_dimension=1, tiled=True
        ).astype(jnp.float32),
        lax.psum_scatter(d_coef.astype(jnp.bfloat16), "dp", scatter_dimension=1, tiled=True).astype(
            jnp.float32
        ),
        lax.psum_scatter(d_rate.astype(jnp.bfloat16), "dp", scatter_dimension=1, tiled=True).astype(
            jnp.float32
        ),
    )
    shares = (
        lax.psum_scatter(
            grad_gain_one.astype(jnp.bfloat16), "dp", scatter_dimension=0, tiled=True
        ).astype(jnp.float32),
        lax.psum_scatter(
            grad_query.astype(jnp.bfloat16), "dp", scatter_dimension=0, tiled=True
        ).astype(jnp.float32),
        lax.psum_scatter(
            grad_key.astype(jnp.bfloat16), "dp", scatter_dimension=0, tiled=True
        ).astype(jnp.float32),
        lax.psum_scatter(
            grad_value.astype(jnp.bfloat16), "dp", scatter_dimension=0, tiled=True
        ).astype(jnp.float32),
        lax.psum_scatter(
            grad_out.astype(jnp.bfloat16), "dp", scatter_dimension=0, tiled=True
        ).astype(jnp.float32),
        lax.psum_scatter(
            grad_gain_two.astype(jnp.bfloat16), "dp", scatter_dimension=0, tiled=True
        ).astype(jnp.float32),
        lax.psum_scatter(
            grad_up.astype(jnp.bfloat16), "dp", scatter_dimension=0, tiled=True
        ).astype(jnp.float32),
        lax.psum_scatter(
            grad_down.astype(jnp.bfloat16), "dp", scatter_dimension=0, tiled=True
        ).astype(jnp.float32),
    )
    totals = (
        lax.psum(shares[0].astype(jnp.bfloat16), "seq").astype(jnp.float32),
        lax.psum(shares[1].astype(jnp.bfloat16), "seq").astype(jnp.float32),
        lax.psum(shares[2].astype(jnp.bfloat16), "seq").astype(jnp.float32),
        lax.psum(shares[3].astype(jnp.bfloat16), "seq").astype(jnp.float32),
        lax.psum(shares[4].astype(jnp.bfloat16), "seq").astype(jnp.float32),
        lax.psum(shares[5].astype(jnp.bfloat16), "seq").astype(jnp.float32),
        lax.psum(shares[6].astype(jnp.bfloat16), "seq").astype(jnp.float32),
        lax.psum(shares[7].astype(jnp.bfloat16), "seq").astype(jnp.float32),
    )
    out_rows = jnp.concatenate(out_list, axis=0)
    dx_rows = jnp.concatenate(dx_list, axis=0)
    return (
        out_rows,
        dx_rows,
        totals[0],
        totals[1],
        totals[2],
        totals[3],
        totals[4],
        totals[5],
        totals[6],
        totals[7],
        taps_part,
        coef_part,
        rate_part,
    )


def split_rows(
    tokens, lengths, gain_one, w_query, w_key, w_value, w_out, gain_two, w_up, w_down,
    shift_taps, diag_coef, diag_rate, cotangent,
):
    side = lax.axis_index("seq")
    mine = lax.axis_index("dp")
    devices = lax.axis_size("dp")
    width = tokens.shape[2]
    length = tokens.shape[1] * 2
    channels, states = diag_coef.shape
    tile = 256
    tables = transform_tables()
    live = lax.dynamic_slice_in_dim(lengths, side, 1, 0)
    packed = jnp.stack([diag_coef.T, diag_rate.T])
    row_one = gain_one[None, :]
    row_two = gain_two[None, :]
    x, cot, a_one, q, k, v, kern, tapspec, hidden, a_two, shifted, mixed, state = mixer_call(
        live, tokens, cotangent, packed, shift_taps.T.astype(BF16), row_one, row_two, w_query, w_key, w_value, w_out,
        tables, tile,
    )
    out_row, d_hidden, d_query, d_state, d_gain_two, up_part, down_part, *left = ffn_call(
        live, a_two, cot, hidden, row_two, w_up, w_down, w_out, state, q, a_one
    )
    out, d_tokens, gains, taps_grad, coef_grad, rate_grad, up, down, gate, kv = mixer_back_call(
        live, out_row, a_one, d_state, d_query, mixed, shifted, k, v, w_query, w_key, w_value, kern, tapspec, tables, x,
        row_one, d_hidden, d_gain_two, packed[0], packed[1], (up_part, down_part, left), states, tile,
    )
    gain_each = width // devices
    gains = lax.dynamic_slice_in_dim(gains, mine * gain_each, gain_each, 1)
    return (
        out,
        d_tokens,
        gains[0],
        gate[1],
        kv[0],
        kv[1],
        gate[0],
        gains[1],
        up,
        down,
        taps_grad,
        coef_grad,
        rate_grad,
    )


def solution(mesh):
    in_specs = (
        P("dp", "seq", None),
        P("dp"),
        P(),
        P(),
        P(),
        P(),
        P(),
        P(),
        P(),
        P(),
        P("seq", None),
        P("seq", None),
        P("seq", None),
        P("dp", "seq", None),
    )
    out_specs = (
        P("dp", "seq", None),
        P("dp", "seq", None),
        P("dp"),
        P("dp", None),
        P("dp", None),
        P("dp", None),
        P("dp", None),
        P("dp"),
        P("dp", None),
        P("dp", None),
        P("seq", "dp"),
        P("seq", "dp"),
        P("seq", "dp"),
    )

    def per_device(*args):
        tokens, shift_taps = args[0], args[10]
        rows, positions, width = tokens.shape
        fits = (
            mesh.shape["seq"] == rows == 2
            and mesh.shape["dp"] == 16
            and positions * 2 % BLOCK == 0
            and width % 256 == 0
            and shift_taps.shape[1] <= BLOCK
        )
        return split_rows(*args) if fits else split_channels(*args)

    return jax.shard_map(
        per_device, mesh=mesh, in_specs=in_specs, out_specs=out_specs, check_vma=False
    )
```

```python
import functools
import math

import jax
import jax.numpy as jnp
import numpy as np
from jax import lax
from jax.experimental import pallas as pl
from jax.experimental.pallas import tpu as pltpu
from jax.sharding import PartitionSpec as P

BLOCK = 256
CHUNK = 16
LANES = 128
EPS = 1e-05
F32 = jnp.float32
BF16 = jnp.bfloat16
VMEM_BYTES = 60 * 1024 * 1024


def dot(a, b):
    return lax.dot_general(a, b, (((1,), (0,)), ((), ())), preferred_element_type=F32)


def dot_nt(a, b):
    return lax.dot_general(a, b, (((1,), (1,)), ((), ())), preferred_element_type=F32)


def dot_tn(a, b):
    return lax.dot_general(a, b, (((0,), (0,)), ((), ())), preferred_element_type=F32)


def params():
    return pltpu.CompilerParams(vmem_limit_bytes=VMEM_BYTES)


def cost(flops, byte_count):
    return pl.CostEstimate(flops=int(flops), bytes_accessed=int(byte_count), transcendentals=0)


def transform_tables():
    freq = np.concatenate([np.arange(0, BLOCK, 2), np.arange(1, BLOCK, 2)]).astype(np.float64)
    time = np.arange(BLOCK, dtype=np.float64)
    angle = (2.0 * math.pi / (2 * BLOCK)) * (freq[:, None] + 0.5) * time[None, :]
    table = np.concatenate([np.cos(angle), -np.sin(angle)], axis=0)
    return jnp.asarray(table, dtype=BF16), jnp.asarray(table.T.copy(), dtype=BF16)


def norm_stats(rows):
    center = rows - jnp.mean(rows, axis=-1, keepdims=True)
    spread = jnp.mean(center * center, axis=-1, keepdims=True)
    inv = lax.rsqrt(spread + EPS)
    return center * inv, inv


def norm_pull(grad, normed, inv, gain):
    scaled = grad * gain
    mean_one = jnp.mean(scaled, axis=-1, keepdims=True)
    mean_two = jnp.mean(scaled * normed, axis=-1, keepdims=True)
    return (scaled - mean_one - normed * mean_two) * inv


def live_rows(length, first, count):
    rows = lax.broadcasted_iota(jnp.int32, (count, 1), 0) + first
    return (rows < length).astype(F32)


def spectral_loop(channels, body):
    half = BLOCK // 2
    for parity in range(2):
        sign = 1.0 if parity == 0 else -1.0

        def step(index, carry, sign=sign, parity=parity):
            low = pl.multiple_of(parity * half + index * CHUNK, CHUNK)
            body(sign, pl.ds(low, CHUNK), pl.ds(low + BLOCK, CHUNK), slice(0, channels))
            return carry

        lax.fori_loop(0, half // CHUNK, step, 0)


def multiply(ar, ai, br, bi):
    return ar * br - ai * bi, ar * bi + ai * br


def multiply_conj(ar, ai, br, bi):
    return ar * br + ai * bi, ar * bi - ai * br


def gelu_pair(x):
    bell = jnp.exp(x * x * -0.5)
    size = jnp.abs(x)
    t = 1.0 / (1.0 + (0.3275911 / math.sqrt(2.0)) * size)
    poly = t * (
        0.5 * 0.254829592
        + t * (0.5 * -0.284496736 + t * (0.5 * 1.421413741 + t * (0.5 * -1.453152027 + t * (0.5 * 1.061405429))))
    )
    tail = poly * bell
    phi = jnp.where(x >= 0.0, 1.0 - tail, tail)
    return x * phi, phi + x * bell * (1.0 / math.sqrt(2.0 * math.pi))


def bit_of(index, bit):
    return lax.rem(index // bit, 2)


def partner(axis, bit):
    index = lax.axis_index(axis)
    return {axis: index + bit * (1 - 2 * bit_of(index, bit))}


UP, DOWN, GATE, KERN, KEY, VALUE, KV, OUT, ROW, COEF, TAPS = range(11)
CORE, MIDDLE, NEAR, FAR, SIDE = ("dp", 1), ("dp", 2), ("dp", 4), ("dp", 8), ("seq", 1)


def greet(partners):
    barrier = pltpu.get_barrier_semaphore()
    for axis, bit in partners:
        pl.semaphore_signal(barrier, inc=1, device_id=partner(axis, bit), device_id_type=pl.DeviceIdType.MESH)
    pl.semaphore_wait(barrier, len(partners))


def transfer(source, target, sems, to):
    return pltpu.make_async_remote_copy(
        src_ref=source,
        dst_ref=target,
        send_sem=sems.at[0],
        recv_sem=sems.at[1],
        device_id=partner(*to),
        device_id_type=pl.DeviceIdType.MESH,
    )


def add_into(target, other):
    *lead, rows, _ = target.shape
    for place in np.ndindex(*lead):
        for low in range(0, rows, 48):
            piece = (*place, slice(low, min(low + 48, rows)))
            target[piece] = target[piece] + other[piece]


def places(mine, owners, bits):
    own = [bit_of(mine, bit) for bit in bits]
    return [
        tuple(1 - own[i] if (owner // bit) % 2 else own[i] for i, bit in enumerate(bits)) for owner in range(owners)
    ]


def spread(value, base, sideways=False):
    value = value.astype(BF16)
    share = value.shape[0] // 16
    half = value.shape[1] // 2
    side = lax.axis_index("seq")
    for owner, (core, *place) in enumerate(places(lax.axis_index("dp"), 16, (1, 2, 4, 8))):
        rows = value[owner * share : (owner + 1) * share]
        if sideways:
            base[(core, side, *place)] = rows[:, :half]
            base[(core, 1 - side, *place)] = rows[:, half:]
        else:
            base[(core, *place)] = rows


AXES = {"c": CORE, "x": MIDDLE, "n": NEAR, "f": FAR, "y": SIDE}


class Sum:
    def __init__(self, refs, sems, order, final=None, across=True):
        self.refs, self.sems, self.final, self.across = refs, sems, final, across
        self.order = "c" + order
        self.sideways = "y" in order
        self.last = len(self.order)

    def part(self, step, half):
        ref = self.refs[step]
        if step == self.last:
            return ref
        left = [axis for axis in "cyxnf" if axis in self.order[step:]]
        return ref.at[(slice(None),) * left.index(self.order[step]) + (half,)]

    def copy(self, step):
        axis = AXES[(self.order + "y")[step]]
        return transfer(self.part(step, 1), self.refs[step + 1], self.sems.at[step], axis)

    def start(self, step):
        self.copy(step).start()

    def wait(self, step):
        self.copy(step).wait()
        if step < self.last:
            add_into(self.refs[step + 1], self.part(step, 0))
            if step == self.last - 1 and not self.across:
                self.final(self.refs[step + 1][...])
        else:
            self.final(self.refs[step][...], self.refs[step + 1][...], self.sideways)


class Gather:
    def __init__(self, z, refs, sems, order, final=None):
        self.refs, self.sems, self.final = refs, sems, final
        self.order = "c" + order
        self.sideways = "y" in order
        self.lead = len(self.order)
        self.last = self.lead + 2
        mine = lax.axis_index("dp")
        near = bit_of(mine, 4) == z % 2
        far = bit_of(mine, 8) == z // 2
        both = jnp.logical_and(near, far)
        self.gives = (jnp.logical_not(near), jnp.logical_and(near, jnp.logical_not(far)), both)
        self.takes = (near, both, both)

    def part(self, step, half):
        ref = self.refs[step]
        if step >= self.lead:
            return ref
        left = [axis for axis in "cyx" if axis in self.order[step:]]
        return ref.at[(slice(None),) * left.index(self.order[step]) + (half,)]

    def copy(self, step):
        axis = AXES[(self.order + "nfy")[step]]
        return transfer(self.part(step, 1), self.refs[step + 1], self.sems.at[step], axis)

    def start(self, step):
        if step < self.lead:
            self.copy(step).start()
        else:

            @pl.when(self.gives[step - self.lead])
            def _():
                self.copy(step).start()

    def wait(self, step):
        if step < self.lead:
            self.copy(step).wait()
            add_into(self.refs[step + 1], self.part(step, 0))
            return

        @pl.when(self.gives[step - self.lead])
        def _():
            self.copy(step).wait_send()

        @pl.when(self.takes[step - self.lead])
        def _():
            self.copy(step).wait_recv()
            if step < self.last:
                add_into(self.refs[step + 1], self.part(step, 0))
            else:
                self.final(self.refs[step][...], self.refs[step + 1][...], self.sideways)


class Rows:
    def __init__(self, source, target, sems):
        self.copy = transfer(source, target, sems, SIDE)

    def start(self, _):
        self.copy.start()

    def wait(self, _):
        self.copy.wait()


def follow(sums, events):
    for name, index, exchange, begin in events:
        if begin:
            sums[name, index].start(exchange)
        else:
            sums[name, index].wait(exchange)


def put(target, low, own, given, sideways):
    if sideways:
        side = lax.axis_index("seq")
        half = own.shape[-1]
        target[:, pl.ds(pl.multiple_of(low + side * half, LANES), half)] = own.astype(F32)
        target[:, pl.ds(pl.multiple_of(low + (1 - side) * half, LANES), half)] = given.astype(F32)
    else:
        target[:, low : low + own.shape[-1]] = own.astype(F32) + given.astype(F32)


def base_shape(rows, columns, order):
    return (2, 2, 2, 2, 2, rows, columns // 2) if "y" in order else (2, 2, 2, 2, rows, columns)


def landings(rows, columns, order):
    *bits, rows, columns = base_shape(rows, columns, order)
    return [pltpu.VMEM((*bits[n + 1 :], rows, columns), BF16) for n in range(len(bits))] + [pltpu.VMEM((rows, columns), BF16)]


def gather_landings(rows, columns, order):
    columns = columns // 2 if "y" in order else columns
    return [pltpu.VMEM((*(2,) * (len(order) - n), rows, columns), BF16) for n in range(len(order) + 1)] + [
        pltpu.VMEM((rows, columns), BF16) for _ in range(3)
    ]


def row_of(ref):
    return ref[...].reshape(1, ref.shape[0])


def once(shape):
    zeros = (0,) * len(shape)
    return pl.BlockSpec(shape, lambda *_: zeros, pipeline_mode=pl.Buffered(1))


def mixer_body(
    lengths_ref, tokens_hbm, cot_hbm, coef_ref, rate_ref, taps_ref, gain_one_ref, gain_two_ref, wq_hbm, wk_hbm, wv_hbm, wout_hbm,
    table_ref, back_ref,
    x_hbm, cot_out, a_one_hbm, q_hbm, k_hbm, v_hbm, kern_hbm, tapspec_hbm, hidden_hbm, a_two_hbm,
    shifted_ref, mixed_ref, state_ref,
    x, a_one, q, k, v, total, a_two, wq, wk, wv, wout, kern, tapspec, taps, other, current, kern_time, near, far,
    spec, prod, in_sems, own_sems, out_sems, token_sems, cot_sems, other_sems, taps_sems, unit_sems,
):
    j = pl.program_id(0)
    steps = pl.num_programs(0)
    length, width = x.shape
    half = length // 2
    tile = shifted_ref.shape[1]
    blocks = length // BLOCK
    states, channels = coef_ref.shape
    side = lax.axis_index("seq")
    live = lengths_ref[side]
    core = bit_of(lax.axis_index("dp"), 1)
    own_rows = pl.ds(pl.multiple_of(side * half, half), half)

    weights = [
        pltpu.make_async_copy(source, target, in_sems.at[i])
        for i, (source, target) in enumerate(((wq_hbm, wq), (wk_hbm, wk), (wv_hbm, wv), (wout_hbm, wout)))
    ]
    outs = [
        pltpu.make_async_copy(source, target, out_sems.at[i])
        for i, (source, target) in enumerate(
            (
                (x, x_hbm), (a_one, a_one_hbm), (q, q_hbm), (k, k_hbm), (v, v_hbm), (kern, kern_hbm),
                (tapspec, tapspec_hbm),
            )
        )
    ]
    own_x = pltpu.make_async_copy(tokens_hbm.at[side], x.at[own_rows], own_sems.at[0])
    own_cot = pltpu.make_async_copy(cot_hbm.at[side], cot_out.at[own_rows], own_sems.at[1])
    other_x = [
        transfer(
            tokens_hbm.at[1 - side, pl.ds(i * BLOCK, BLOCK)],
            x.at[pl.ds(pl.multiple_of(side * half + i * BLOCK, BLOCK), BLOCK)],
            token_sems.at[i],
            SIDE,
        )
        for i in range(half // BLOCK)
    ]
    other_cot = transfer(cot_hbm.at[1 - side], cot_out.at[own_rows], cot_sems, SIDE)
    wanted = pl.ds(pl.multiple_of(core * LANES, LANES), 2 * LANES)
    params = (coef_ref, rate_ref)
    other_params = [transfer(params[i].at[:, wanted], other.at[i], other_sems.at[i], SIDE) for i in range(2)]
    own_lanes = pl.ds(pl.multiple_of(side * channels, LANES), channels)
    other_taps = transfer(taps.at[:, own_lanes], taps.at[:, own_lanes], taps_sems, SIDE)

    def unit_columns(number, of_core):
        tile_of = (2 * of_core, 1, 2 * of_core)[number]
        half_of = (side, side + of_core - 2 * side * of_core, 1 - side)[number]
        return pl.ds(pl.multiple_of(half_of * channels + tile_of * LANES, LANES), LANES)

    def unit_copy(number):
        columns = unit_columns(number, core)
        return transfer(kern_time.at[:, columns], kern_time.at[:, columns], unit_sems.at[number], CORE)

    def unit(number):
        if number == 0:
            for part in range(2):
                current[part] = params[part][:, pl.ds(pl.multiple_of(core * 2 * LANES, LANES), LANES)]
        elif number == 1:

            @pl.when(core == 0)
            def _():
                for part in range(2):
                    current[part] = params[part][:, LANES : 2 * LANES]

            @pl.when(core == 1)
            def _():
                for part in range(2):
                    other_params[part].wait()
                    current[part] = other[part, :, :LANES]

        else:

            @pl.when(core == 0)
            def _():
                for part in range(2):
                    other_params[part].wait()
                    current[part] = other[part, :, :LANES]

            @pl.when(core == 1)
            def _():
                for part in range(2):
                    current[part] = other[part, :, LANES:]

        columns = unit_columns(number, core)
        step_count, together = 32, 8
        groups = length // step_count
        near_time = lax.broadcasted_iota(jnp.int32, (step_count, 1), 0).astype(F32)
        far_time = lax.broadcasted_iota(jnp.int32, (groups, 1), 0).astype(F32) * step_count

        def fill(n, carry):
            rate = current[1, pl.ds(n, 1), :]
            near[n] = jnp.exp(-rate * near_time)
            far_n = current[0, pl.ds(n, 1), :] * jnp.exp(-rate * far_time)
            for g in range(groups // together):
                far[g, n] = far_n[g * together : (g + 1) * together, :]
            return carry

        lax.fori_loop(0, states, fill, 0)

        def group(g, carry):
            def add(n, sums):
                near_n = near[n]
                return tuple(sums[i] + far[g, n, i : i + 1, :] * near_n for i in range(together))

            zeros = tuple(jnp.zeros((step_count, LANES), F32) for _ in range(together))
            sums = lax.fori_loop(0, states, add, zeros, unroll=4)
            for i in range(together):
                place = pl.multiple_of((g * together + i) * step_count, step_count)
                kern_time[pl.ds(place, step_count), columns] = sums[i].astype(BF16)
            return carry

        lax.fori_loop(0, groups // together, group, 0)
        unit_copy(number).start()

    def project_block(low):
        rows = pl.ds(pl.multiple_of(low, BLOCK), BLOCK)
        normed, _ = norm_stats(x[rows, :].astype(F32))
        a_rows = (normed * row_of(gain_one_ref)).astype(BF16)
        a_one[rows, :] = a_rows
        mask = live_rows(live, low, BLOCK)
        k[rows, :] = (dot(a_rows, wk[...]) * mask).astype(BF16)
        v[rows, :] = (dot(a_rows, wv[...]) * mask).astype(BF16)
        q[rows, :] = dot(a_rows, wq[...]).astype(BF16)

    @pl.when(j == 0)
    def _():
        own_x.start()
        own_cot.start()
        for copy in weights:
            copy.start()
        greet((CORE, SIDE))
        for copy in other_params:
            copy.start()
        for copy in other_x:
            copy.start()
        taps[:, own_lanes] = taps_ref[...].astype(BF16)
        other_taps.start()
        total[...] = jnp.zeros_like(total)
        unit(0)
        unit(1)
        unit(2)
        for copy in weights:
            copy.wait()
        own_x.wait()

        def own_block(b, carry):
            project_block(side * half + b * BLOCK)
            return carry

        lax.fori_loop(0, half // BLOCK, own_block, 0)
        other_taps.wait()
        for number in range(3):
            unit_copy(number).wait()

        def tile_spectra(t, carry):
            columns = pl.ds(pl.multiple_of(t * tile, tile), tile)
            for b in range(blocks):
                spec[b] = dot(table_ref[...], kern_time[b * BLOCK : (b + 1) * BLOCK, columns])

            def combine(sign, re, im, lanes):
                to = pl.ds(pl.multiple_of(t * tile + lanes.start, LANES), lanes.stop - lanes.start)
                for b in range(blocks):
                    out_re = spec[b, re, lanes]
                    out_im = spec[b, im, lanes]
                    if b > 0:
                        out_re = out_re - sign * spec[b - 1, im, lanes]
                        out_im = out_im + sign * spec[b - 1, re, lanes]
                    kern[b, re, to] = (out_re * (1.0 / BLOCK)).astype(BF16)
                    kern[b, im, to] = (out_im * (1.0 / BLOCK)).astype(BF16)

            spectral_loop(tile, combine)
            tapspec[:, columns] = dot(table_ref[:, : taps.shape[0]], taps[:, columns]) * (1.0 / BLOCK)
            return carry

        lax.fori_loop(0, width // tile, tile_spectra, 0)
        outs[5].start()
        outs[6].start()
        other_cot.start()
        for i, copy in enumerate(other_x):
            copy.wait()
            if i == len(other_x) - 1:
                outs[0].start()
            project_block((1 - side) * half + i * BLOCK)
        for copy in outs[1:5]:
            copy.start()

    @pl.when(j > 0)
    def _():
        t = j - 1
        columns = pl.ds(pl.multiple_of(t * tile, tile), tile)
        for b in range(blocks):
            spec[b] = dot(table_ref[...], k[b * BLOCK : (b + 1) * BLOCK, columns])

        def shift_product(sign, re, im, lanes):
            at = pl.ds(pl.multiple_of(t * tile + lanes.start, LANES), lanes.stop - lanes.start)
            tr = tapspec[re, at]
            ti = tapspec[im, at]
            before = None
            for b in range(blocks):
                xr = spec[b, re, lanes]
                xi = spec[b, im, lanes]
                if b == 0:
                    sr, si = xr, xi
                else:
                    sr, si = xr - sign * before[1], xi + sign * before[0]
                before = (xr, xi)
                yr, yi = multiply(sr, si, tr, ti)
                prod[b, re, lanes] = yr.astype(BF16)
                prod[b, im, lanes] = yi.astype(BF16)

        spectral_loop(tile, shift_product)
        for b in range(blocks):
            rows = slice(b * BLOCK, (b + 1) * BLOCK)
            shifted = dot(back_ref[...], prod[b])
            shifted_ref[rows, :] = shifted.astype(BF16)
            mixed_ref[rows, :] = (shifted * v[rows, columns].astype(F32)).astype(BF16)
            spec[b] = dot(table_ref[...], mixed_ref[rows, :])

        def state_product(sign, re, im, lanes):
            at = pl.ds(pl.multiple_of(t * tile + lanes.start, LANES), lanes.stop - lanes.start)
            s = [(spec[b, re, lanes], spec[b, im, lanes]) for b in range(blocks)]
            h = [(kern[b, re, at].astype(F32), kern[b, im, at].astype(F32)) for b in range(blocks)]
            for i in range(blocks):
                yr, yi = multiply(*s[i], *h[0])
                for d in range(1, i + 1):
                    pr, pi = multiply(*s[i - d], *h[d])
                    yr, yi = yr + pr, yi + pi
                prod[i, re, lanes] = yr.astype(BF16)
                prod[i, im, lanes] = yi.astype(BF16)

        spectral_loop(tile, state_product)
        for b in range(blocks):
            rows = slice(b * BLOCK, (b + 1) * BLOCK)
            state = dot(back_ref[...], prod[b]).astype(BF16)
            state_ref[rows, :] = state
            gated = (q[rows, columns].astype(F32) * state.astype(F32)).astype(BF16)
            total[rows, :] += dot(gated, wout[columns, :])

    @pl.when(j == steps - 1)
    def _():
        def last_copies(b):
            rows = pl.ds(pl.multiple_of(b * BLOCK, BLOCK), BLOCK)
            return [
                pltpu.make_async_copy(total.at[rows], hidden_hbm.at[rows], out_sems.at[7 + b]),
                pltpu.make_async_copy(a_two.at[rows], a_two_hbm.at[rows], out_sems.at[7 + blocks + b]),
            ]

        def block(b, carry):
            rows = pl.ds(pl.multiple_of(b * BLOCK, BLOCK), BLOCK)
            mask = live_rows(live, b * BLOCK, BLOCK)
            hidden = x[rows, :].astype(F32) + mask * total[rows, :]
            total[rows, :] = hidden
            normed, _ = norm_stats(hidden)
            a_two[rows, :] = (normed * row_of(gain_two_ref)).astype(BF16)
            for copy in last_copies(b):
                copy.start()
            return carry

        lax.fori_loop(0, blocks, block, 0)
        for b in range(blocks):
            for copy in last_copies(b):
                copy.wait()
        for copy in outs:
            copy.wait()
        own_cot.wait()
        other_cot.wait()


def mixer_call(lengths, tokens, cot, coef, rate, taps, gain_one, gain_two, wq, wk, wv, wout, tables, tile):
    _, half, width = tokens.shape
    length = 2 * half
    blocks = length // BLOCK
    table, back = tables
    states, channels = taps.shape
    anywhere = pl.BlockSpec(memory_space=pl.ANY)
    rows_tile = pl.BlockSpec((length, tile), lambda j: (0, jnp.maximum(j - 1, 0)))
    low = lambda *shape: jax.ShapeDtypeStruct(shape, BF16)
    full = lambda *shape: jax.ShapeDtypeStruct(shape, F32)
    vmem = lambda *shape: pltpu.VMEM(shape, BF16)
    wide = lambda *shape: pltpu.VMEM(shape, F32)
    sems = lambda *shape: pltpu.SemaphoreType.DMA(shape)
    rows = low(length, width)
    return pl.pallas_call(
        mixer_body,
        grid=(1 + width // tile,),
        in_specs=[
            pl.BlockSpec(memory_space=pltpu.SMEM),
            anywhere,
            anywhere,
            once(coef.shape),
            once(rate.shape),
            once(taps.shape),
            once((width,)),
            once((width,)),
            anywhere,
            anywhere,
            anywhere,
            anywhere,
            once(table.shape),
            once(back.shape),
        ],
        out_specs=[anywhere] * 10 + [rows_tile] * 3,
        out_shape=[
            rows, rows, rows, rows, rows, rows,
            low(blocks, 2 * BLOCK, width), full(2 * BLOCK, width), full(length, width), rows,
            rows, rows, rows,
        ],
        scratch_shapes=[
            vmem(length, width),
            vmem(length, width),
            vmem(length, width),
            vmem(length, width),
            vmem(length, width),
            wide(length, width),
            vmem(length, width),
            vmem(*wq.shape),
            vmem(*wk.shape),
            vmem(*wv.shape),
            vmem(*wout.shape),
            vmem(blocks, 2 * BLOCK, width),
            wide(2 * BLOCK, width),
            vmem(states, width),
            wide(2, states, 2 * LANES),
            wide(2, states, LANES),
            vmem(length, width),
            wide(states, 32, LANES),
            wide(length // 256, states, 8, LANES),
            wide(blocks, 2 * BLOCK, tile),
            vmem(blocks, 2 * BLOCK, tile),
            sems(4),
            sems(2),
            sems(7 + 2 * blocks),
            sems(half // BLOCK, 2),
            sems(2),
            sems(2, 2),
            sems(2),
            sems(3, 2),
        ],
        compiler_params=pltpu.CompilerParams(vmem_limit_bytes=VMEM_BYTES, collective_id=3, has_side_effects=True),
        cost_estimate=cost(16e9, 40e6),
        name="mixer_forward",
    )(lengths, tokens, cot, coef, rate, taps, gain_one, gain_two, wq, wk, wv, wout, table, back)


ORDER = {UP: ["ynfx", "ynfx", "ynfx", "yxnf"], DOWN: ["xy", "xy", "xy", "yx"], GATE: ["xfn", "xnf"], KERN: "xnf", KV: [["nxf"], ["xnf", "nxf"], ["nxf", "xfn"]]}
FEED_PLAN = {
    (0, 4): ((DOWN, 0, 0, 1),),
    (0, 5): ((UP, 0, 0, 1),),
    (1, 1): ((DOWN, 0, 0, 0), (UP, 0, 0, 0), (UP, 0, 1, 1), (DOWN, 0, 1, 1)),
    (1, 4): ((DOWN, 1, 0, 1),),
    (1, 5): ((UP, 1, 0, 1),),
    (2, 1): ((DOWN, 1, 0, 0), (UP, 0, 1, 0), (DOWN, 0, 1, 0), (UP, 1, 0, 0), (UP, 1, 1, 1), (DOWN, 1, 1, 1), (UP, 0, 2, 1), (DOWN, 0, 2, 1)),
    (2, 4): ((DOWN, 2, 0, 1),),
    (2, 5): ((UP, 0, 2, 0), (UP, 2, 0, 1), (UP, 0, 3, 1)),
    (3, 1): ((DOWN, 2, 0, 0), (DOWN, 1, 1, 0), (DOWN, 0, 2, 0), (UP, 2, 0, 0), (UP, 2, 1, 1), (DOWN, 2, 1, 1), (DOWN, 1, 2, 1), (DOWN, 0, 3, 1)),
    (3, 3): ((UP, 1, 1, 0), (UP, 0, 3, 0), (UP, 1, 2, 1), (UP, 0, 4, 1)),
    (3, 4): ((DOWN, 3, 0, 1),),
    (3, 5): ((DOWN, 0, 3, 0), (UP, 3, 0, 1), (DOWN, 0, 4, 1)),
    (4, 3): ((UP, 0, 4, 0), (UP, 0, 5, 1)),
    (4, 4): ((DOWN, 3, 0, 0), (DOWN, 1, 2, 0), (DOWN, 1, 3, 1)),
    (4, 5): ((DOWN, 2, 1, 0), (UP, 3, 0, 0), (UP, 1, 2, 0), (GATE, 0, 0, 1), (DOWN, 2, 2, 1)),
    (4, 7): ((GATE, 1, 0, 1),),
    (4, 8): ((UP, 0, 5, 0),),
}
FEED_LEFT = (
    (UP, 3, 0, True),
    (DOWN, 3, 0, True),
    (UP, 1, 2, True),
    (UP, 2, 1, False),
    (DOWN, 0, 4, False),
    (GATE, 0, 0, False),
    (DOWN, 1, 3, False),
    (GATE, 1, 0, False),
    (DOWN, 2, 2, False),
)


def ffn_body(
    lengths_ref, a_two_ref, cot_ref, gain_ref, up_ref, down_ref, hidden_hbm, wout_hbm, state_hbm, q_hbm, a_one_hbm,
    out_hbm, d_hidden_hbm, d_query_hbm, d_state_hbm, gain_grad_ref, up_out, down_out, *rest,
):
    left = rest[: len(FEED_LEFT)]
    (
        total, back, act, d_pre, d_down, hidden, wout, state, q, a_one, in_sems, out_sems,
        up_flat, up_side, down_flat, down_side, gate_base, up_sems, down_sems, gate_sems, *lands,
    ) = rest[len(FEED_LEFT) :]
    j = pl.program_id(0)
    quarters = 4
    length, width = a_two_ref.shape
    tile = up_ref.shape[1]
    live = lengths_ref[lax.axis_index("seq")]
    rows_count = 256

    sums = {}
    lands = list(lands)
    up_bases, down_bases = (up_flat, up_side), (down_flat, down_side)

    def take(count):
        taken = lands[:count]
        del lands[:count]
        return taken

    for t in range(quarters):
        order, gather = ORDER[UP][t], ORDER[DOWN][t]

        def keep_up(own, given, sideways, t=t):
            put(up_out, t * tile, own, given, sideways)

        def keep_down(own, given, sideways):
            put(down_out, 0, own, given, sideways)

        refs = [up_bases["y" in order]] + take(len(order) + 2)
        sums[UP, t] = Sum(refs, up_sems.at[t], order, keep_up)
        refs = [down_bases["y" in gather]] + take(len(gather) + 4)
        sums[DOWN, t] = Gather(t, refs, down_sems.at[t], gather, keep_down)
    for i in range(2):
        sums[GATE, i] = Sum([gate_base.at[i]] + take(5), gate_sems.at[i], ORDER[GATE][i])

    def run(step, number):
        follow(sums, FEED_PLAN.get((step, number), ()))

    def slot(step, number):
        if FEED_PLAN.get((step, number)):

            @pl.when(j == step)
            def _():
                run(step, number)

    def slots(number):
        for step in range(quarters):
            slot(step, number)

    late = [
        pltpu.make_async_copy(source, target, in_sems.at[i])
        for i, (source, target) in enumerate(
            ((hidden_hbm, hidden), (q_hbm, q), (state_hbm, state), (wout_hbm, wout), (a_one_hbm, a_one))
        )
    ]

    @pl.when(j == 0)
    def _():
        for copy in late:
            copy.start()
        greet((CORE, MIDDLE, NEAR, FAR, SIDE))
        for low in range(0, length, rows_count):
            rows = slice(low, low + rows_count)
            d_down[rows, :] = (cot_ref[rows, :].astype(F32) * live_rows(live, low, rows_count)).astype(BF16)
        total[...] = jnp.zeros_like(total)
        back[...] = jnp.zeros_like(back)
        down_out[...] = jnp.zeros_like(down_out)
        up_out[...] = jnp.zeros_like(up_out)

    def chunk(low):
        rows = pl.ds(low, rows_count)
        pre = dot(a_two_ref[rows, :], up_ref[...])
        d_act = dot_nt(d_down[rows, :], down_ref[...])
        value, slope = gelu_pair(pre)
        act[rows, :] = value.astype(BF16)
        d_pre[rows, :] = (d_act * slope).astype(BF16)
        total[rows, :] += dot(act[rows, :], down_ref[...])
        back[rows, :] += dot_nt(d_pre[rows, :], up_ref[...])

    @pl.when(j < quarters)
    def _():
        def step(part, carry):
            chunk(pl.multiple_of(part * rows_count, rows_count))
            for t in range(1, quarters):
                for number in range(4):
                    if FEED_PLAN.get((t, number)):
                        pl.when(jnp.logical_and(j == t, part == number))(functools.partial(run, t, number))
            return carry

        lax.fori_loop(0, 4, step, 0)

    share = tile // 4
    for sideways in (False, True):
        steps = [t for t in range(quarters) if ("y" in ORDER[DOWN][t]) == sideways]

        @pl.when(functools.reduce(jnp.logical_or, [j == t for t in steps], False))
        def _(sideways=sideways):
            value = dot_tn(act[...], d_down[...]).astype(BF16)
            side = lax.axis_index("seq")
            for owner, (core, x) in enumerate(places(lax.axis_index("dp"), 4, (1, 2))):
                rows = value[owner * share : (owner + 1) * share]
                if sideways:
                    down_side[core, side, x] = rows[:, : width // 2]
                    down_side[core, 1 - side, x] = rows[:, width // 2 :]
                else:
                    down_flat[core, x] = rows

    slots(4)

    for sideways in (False, True):
        steps = [t for t in range(quarters) if ("y" in ORDER[UP][t]) == sideways]

        @pl.when(functools.reduce(jnp.logical_or, [j == t for t in steps], False))
        def _(sideways=sideways):
            spread(dot_tn(a_two_ref[...], d_pre[...]), up_bases[sideways], sideways)

    slots(5)

    def send(source, target, number):
        return pltpu.make_async_copy(source, target, out_sems.at[number])

    @pl.when(j == quarters)
    def _():
        run(4, 0)
        late[0].wait()
        late[1].wait()
        late[2].wait()
        gain_sum = jnp.zeros((1, width), F32)
        for low in range(0, length, rows_count):
            rows = slice(low, low + rows_count)
            mask = live_rows(live, low, rows_count)
            before = hidden[rows, :]
            d_pre[rows, :] = (before + mask * total[rows, :]).astype(BF16)
            normed, inv = norm_stats(before)
            grad_in = back[rows, :]
            gain_sum = gain_sum + jnp.sum(grad_in * normed, axis=0, keepdims=True)
            d_hidden = cot_ref[rows, :].astype(F32) + norm_pull(grad_in, normed, inv, row_of(gain_ref))
            back[rows, :] = d_hidden
            d_down[rows, :] = (mask * d_hidden).astype(BF16)
            gated = q[rows, :].astype(F32) * state[rows, :].astype(F32)
            act[rows, :] = gated.astype(BF16)
            run(4, 1 + low // rows_count)
        gain_grad_ref[...] = gain_sum
        copies = [send(d_pre, out_hbm, 0), send(back, d_hidden_hbm, 1)]
        for copy in copies:
            copy.start()
        spread(dot_tn(act[...], d_down[...]), gate_base.at[0])
        run(4, 5)
        late[3].wait()
        late[4].wait()
        for low in range(0, length, rows_count):
            rows = slice(low, low + rows_count)
            d_gated = dot_nt(d_down[rows, :], wout[...])
            total[rows, :] = d_gated
            act[rows, :] = (d_gated * state[rows, :].astype(F32)).astype(BF16)
        copies.append(send(act, d_query_hbm, 2))
        copies[2].start()
        run(4, 6)
        spread(dot_tn(a_one[...], act[...]), gate_base.at[1])
        run(4, 7)
        for low in range(0, length, rows_count):
            rows = slice(low, low + rows_count)
            d_down[rows, :] = (total[rows, :] * q[rows, :].astype(F32)).astype(BF16)
        copies.append(send(d_down, d_state_hbm, 3))
        copies[3].start()
        run(4, 8)
        for i, (name, index, exchange, waited) in enumerate(FEED_LEFT):
            if not waited:
                sums[name, index].wait(exchange)
            copies.append(send(sums[name, index].refs[exchange + 1], left[i], 4 + i))
            copies[-1].start()
        for copy in copies:
            copy.wait()


def ffn_call(lengths, a_two, cot, hidden, gain, up, down, wout, state, q, a_one):
    length, width = a_two.shape
    hidden_units = up.shape[1]
    tile = hidden_units // 4
    su, sd = width // 16, tile // 4
    rows_full = once((length, width))
    anywhere = pl.BlockSpec(memory_space=pl.ANY)
    low = lambda *shape: jax.ShapeDtypeStruct(shape, BF16)
    full = lambda *shape: jax.ShapeDtypeStruct(shape, F32)
    vmem = lambda *shape: pltpu.VMEM(shape, BF16)
    wide = lambda *shape: pltpu.VMEM(shape, F32)
    sems = lambda *shape: pltpu.SemaphoreType.DMA(shape)
    shape_of = {}
    for t in range(4):
        shape_of[UP, t] = landings(su, tile, ORDER[UP][t])
        shape_of[DOWN, t] = gather_landings(sd, width, ORDER[DOWN][t])
    for i in range(2):
        shape_of[GATE, i] = landings(su, width, ORDER[GATE][i])
    left = [low(*shape_of[name, index][exchange].shape) for name, index, exchange, _ in FEED_LEFT]
    for name, index, exchange, _ in FEED_LEFT:
        shapes = shape_of[name, index]
        shapes[exchange + 1 :] = [vmem(16, LANES)] * (len(shapes) - exchange - 1)
    lands = [shape for shapes in shape_of.values() for shape in shapes]
    return pl.pallas_call(
        ffn_body,
        grid=(5,),
        in_specs=[
            pl.BlockSpec(memory_space=pltpu.SMEM),
            rows_full,
            rows_full,
            once((width,)),
            pl.BlockSpec((width, tile), lambda j: (0, jnp.minimum(j, 3))),
            pl.BlockSpec((tile, width), lambda j: (jnp.minimum(j, 3), 0)),
        ]
        + [anywhere] * 5,
        out_specs=[anywhere] * 4 + [once((1, width)), once((su, hidden_units)), once((sd, width))] + [anywhere] * len(left),
        out_shape=[
            low(length, width),
            full(length, width),
            low(length, width),
            low(length, width),
            full(1, width),
            full(su, hidden_units),
            full(sd, width),
            *left,
        ],
        scratch_shapes=[
            wide(length, width),
            wide(length, width),
            vmem(length, tile),
            vmem(length, tile),
            vmem(length, width),
            wide(length, width),
            vmem(*wout.shape),
            vmem(length, width),
            vmem(length, width),
            vmem(length, width),
            sems(5),
            sems(4 + len(left)),
            vmem(*base_shape(su, tile, "")) if any("y" not in order for order in ORDER[UP]) else vmem(16, LANES),
            vmem(*base_shape(su, tile, "y")) if any("y" in order for order in ORDER[UP]) else vmem(16, LANES),
            vmem(2, 2, sd, width) if any("y" not in order for order in ORDER[DOWN]) else vmem(16, LANES),
            vmem(2, 2, 2, sd, width // 2) if any("y" in order for order in ORDER[DOWN]) else vmem(16, LANES),
            vmem(2, *base_shape(su, width, "")),
            sems(4, 6, 2),
            sems(4, 6, 2),
            sems(2, 5, 2),
            *lands,
        ],
        compiler_params=pltpu.CompilerParams(vmem_limit_bytes=62 * 1024 * 1024, collective_id=1, has_side_effects=True),
        cost_estimate=cost(12 * length * width * hidden_units, 40e6),
        name="feed_forward",
    )(lengths, a_two, cot, gain, up, down, hidden, wout, state, q, a_one)


BACK_PLAN = {
    (0, 0): ((GATE, 0, 1, 1), (GATE, 1, 1, 1), (OUT, 0, 0, 1), (OUT, 1, 0, 1), (UP, 2, 2, 1), (UP, 1, 3, 1)),
    (0, 1): ((DOWN, 2, 3, 1),),
    (1, 1): ((DOWN, 1, 4, 1),),
    (1, 2): ((UP, 1, 3, 0),),
    (2, 1): ((UP, 2, 2, 0), (UP, 2, 3, 1)),
    (2, 3): ((KERN, 0, 0, 1),),
    (3, 1): ((DOWN, 2, 3, 0), (DOWN, 2, 4, 1)),
    (3, 2): ((UP, 1, 4, 1),),
    (3, 4): ((GATE, 0, 1, 0), (GATE, 1, 1, 0), (KERN, 0, 0, 0), (KERN, 0, 1, 1), (GATE, 0, 2, 1)),
    (3, 5): ((DOWN, 1, 4, 0), (UP, 1, 4, 0), (UP, 3, 1, 1), (GATE, 1, 2, 1), (DOWN, 3, 1, 1), (KEY, 0, 0, 1)),
    (3, 6): ((UP, 2, 3, 0), (UP, 2, 4, 1)),
    (4, 2): ((OUT, 0, 0, 0), (OUT, 1, 0, 0)),
    (4, 3): ((KEY, 0, 0, 0), (DOWN, 2, 4, 0)),
    (4, 4): ((UP, 2, 4, 0), (KEY, 0, 1, 1)),
    (4, 5): ((VALUE, 1, 0, 1), (KEY, 1, 0, 1)),
    (5, 2): ((GATE, 1, 2, 0), (GATE, 0, 2, 0), (GATE, 1, 3, 1)),
    (5, 3): ((VALUE, 1, 0, 0), (KEY, 1, 0, 0), (KERN, 0, 1, 0), (KERN, 0, 2, 1), (KEY, 1, 1, 1)),
    (5, 4): ((UP, 1, 5, 1), (UP, 2, 5, 1)),
    (5, 5): ((KEY, 0, 1, 0), (VALUE, 2, 0, 1), (GATE, 0, 3, 1), (KEY, 2, 0, 1), (KEY, 0, 2, 1)),
    (5, 7): ((ROW, 0, 0, 1), (DOWN, 0, 5, 1)),
    (5, 8): ((UP, 3, 1, 0), (DOWN, 3, 1, 0), (GATE, 1, 3, 0), (UP, 3, 2, 1), (DOWN, 3, 2, 1)),
    (5, 9): ((KEY, 1, 1, 0), (VALUE, 2, 0, 0), (KEY, 2, 0, 0), (UP, 1, 5, 0), (UP, 2, 5, 0), (VALUE, 1, 1, 1)),
    (5, 10): ((KEY, 2, 1, 1),),
    (5, 11): ((ROW, 1, 0, 1), (TAPS, 0, 0, 1)),
}
BACK_LEFT = (
    (KEY, 0, 2, 0),
    (GATE, 0, 3, 0),
    (KERN, 0, 2, 0),
    (KERN, 0, 3, 1),
    (TAPS, 0, 0, 0),
    (DOWN, 0, 5, 0),
    (VALUE, 2, 1, 1),
    (TAPS, 0, 1, 1),
    (KEY, 1, 2, 1),
    (VALUE, 1, 1, 0),
    (KEY, 0, 3, 1),
    (UP, 3, 2, 0),
    (DOWN, 3, 2, 0),
    (UP, 3, 3, 1),
    (KEY, 2, 1, 0),
    (VALUE, 1, 2, 1),
    (DOWN, 3, 3, 1),
    (KEY, 2, 2, 1),
    (KEY, 1, 2, 0),
    (KERN, 0, 3, 0),
    (KEY, 1, 3, 1),
    (KERN, 0, 4, 1),
    (VALUE, 2, 1, 0),
    (TAPS, 0, 1, 0),
    (VALUE, 2, 2, 1),
    (KEY, 0, 3, 0),
    (UP, 3, 3, 0),
    (VALUE, 1, 2, 0),
    (KEY, 2, 2, 0),
    (TAPS, 0, 2, 1),
    (ROW, 0, 0, 0),
    (UP, 3, 4, 1),
    (GATE, 1, 4, 1),
    (KEY, 1, 3, 0),
    (VALUE, 1, 3, 1),
    (GATE, 0, 4, 1),
    (KEY, 2, 3, 1),
    (VALUE, 2, 2, 0),
    (DOWN, 3, 3, 0),
    (VALUE, 2, 3, 1),
    (KERN, 0, 4, 0),
    (COEF, 0, 0, 1),
    (DOWN, 1, 5, 1),
    (DOWN, 3, 4, 1),
    (TAPS, 0, 2, 0),
    (TAPS, 0, 3, 1),
    (DOWN, 2, 5, 1),
    (ROW, 1, 0, 0),
    (COEF, 0, 0, 0),
    (COEF, 0, 1, 1),
    (UP, 3, 4, 0),
    (GATE, 1, 4, 0),
    (VALUE, 1, 3, 0),
    (UP, 3, 5, 1),
    (VALUE, 2, 3, 0),
    (KEY, 2, 3, 0),
    (GATE, 0, 4, 0),
    (VALUE, 1, 4, 1),
    (VALUE, 2, 4, 1),
    (KEY, 0, 4, 1),
    (KEY, 1, 4, 1),
    (TAPS, 0, 3, 0),
    (DOWN, 1, 5, 0),
    (COEF, 0, 1, 0),
    (COEF, 0, 2, 1),
    (TAPS, 0, 4, 1),
    (UP, 3, 5, 0),
    (KEY, 2, 4, 1),
    (DOWN, 2, 5, 0),
    (DOWN, 3, 4, 0),
    (DOWN, 3, 5, 1),
    (VALUE, 1, 4, 0),
    (VALUE, 2, 4, 0),
    (KEY, 1, 4, 0),
    (COEF, 0, 2, 0),
    (COEF, 0, 3, 1),
    (KEY, 0, 4, 0),
    (TAPS, 0, 4, 0),
    (KEY, 2, 4, 0),
    (DOWN, 3, 5, 0),
    (COEF, 0, 3, 0),
)


def mixer_back_body(
    lengths_ref, out_row_ref, d_state_ref, d_query_ref, mixed_ref, shifted_ref, k_ref, v_ref,
    wq_ref, wk_ref, wv_ref, kern_ref, tapspec_ref, table_ref, back_ref, gain_ref, gain_two_grad_ref,
    coef_ref, rate_ref, up_part_ref, down_part_ref, *rest,
):
    left = rest[: len(FEED_LEFT)]
    (
        a_one_hbm, x_hbm, d_hidden_hbm,
        out_ref, d_tokens_ref, gain_one_out, gain_two_out, taps_out, coef_out, rate_out, up_ref, down_ref,
        wout_out, query_out, key_out, value_out,
        total, spec_one, spec_two, prod, shift_prod, d_keys, d_values, d_x, a_one, x, d_hidden, d_taps, d_kern,
        taps_base, taps_sems, coef_base, coef_sems,
        kern_base, kv_base, left_sems, kern_sems, kv_sems, out_sems, row_sems, own_sems, in_sems, *lands,
    ) = rest[len(FEED_LEFT) :]
    j = pl.program_id(0)
    length, width = a_one.shape
    half = length // 2
    tile = k_ref.shape[1]
    tiles = width // tile
    blocks = length // BLOCK
    side = lax.axis_index("seq")
    live = lengths_ref[side]
    own_rows = pl.ds(pl.multiple_of(side * half, half), half)

    sums = {}
    lands = list(lands)

    def take(count):
        taken = lands[:count]
        del lands[:count]
        return taken

    for i, (name, index, exchange, _) in enumerate(FEED_LEFT):

        def keep(own, given, sideways, name=name, index=index):
            if name == UP:
                put(up_ref, index * width, own, given, sideways)
            elif name == DOWN:
                put(down_ref, 0, own, given, sideways)
            else:
                put((wout_out, query_out)[index], 0, own, given, sideways)

        order = ORDER[name][index]
        refs = [None] * (exchange + 1) + [left[i]] + take(len(order) + (3 if name == DOWN else 1) - exchange)
        if name == DOWN:
            sums[name, index] = Gather(index, refs, left_sems.at[i], order, keep)
        else:
            sums[name, index] = Sum(refs, left_sems.at[i], order, keep)

    states, channels = rate_ref.shape
    each = states // 16

    def keep_kern(own, given, sideways):
        put(d_kern, 0, own, given, sideways)
        steps = d_kern.shape[0]
        first = lax.convert_element_type(lax.axis_index("dp") * steps, F32)
        for low in range(0, channels, LANES):
            lanes = slice(low, low + LANES)
            rate = rate_ref[:, lanes]
            from_lane = pl.ds(pl.multiple_of(side * channels + low, LANES), LANES)

            def group(g, sums, rate=rate, from_lane=from_lane):
                coef_sum, rate_sum = sums
                rows = d_kern[pl.ds(pl.multiple_of(g * 8, 8), 8), from_lane]
                for i in range(8):
                    time = first + lax.convert_element_type(g * 8 + i, F32)
                    term = jnp.exp(rate * -time) * rows[i : i + 1]
                    coef_sum = coef_sum + term
                    rate_sum = rate_sum + term * time
                return coef_sum, rate_sum

            zeros = jnp.zeros((states, LANES), F32)
            coef_sum, rate_sum = lax.fori_loop(0, steps // 8, group, (zeros, zeros))
            rate_sum = -coef_ref[:, lanes] * rate_sum
            for owner, place in enumerate(places(lax.axis_index("dp"), 16, (1, 2, 4, 8))):
                rows = slice(owner * each, (owner + 1) * each)
                coef_base[(*place, slice(0, each), lanes)] = coef_sum[rows]
                coef_base[(*place, slice(each, 2 * each), lanes)] = rate_sum[rows]

    def keep_coef(value):
        coef_out[...] = value[:each]
        rate_out[...] = value[each:]

    def keep_taps(own, given, sideways):
        both = own + given
        taps_out[...] = jnp.where(side == 0, both[:each, :channels], both[:each, channels:])
        gain_each = gain_one_out.shape[1]
        gains = pltpu.roll(both, width - lax.axis_index("dp") * gain_each, 1)
        gain_one_out[...] = gains[each : each + 1, :gain_each]
        gain_two_out[...] = gains[each + 1 : each + 2, :gain_each]

    sums[COEF, 0] = Sum([coef_base] + take(4), coef_sems, "xnf", keep_coef, across=False)
    sums[TAPS, 0] = Sum([taps_base] + take(5), taps_sems, "xnf", keep_taps)

    for i in range(2):
        piece = pl.ds(i * (half // 2), half // 2)
        other = pl.ds(pl.multiple_of((1 - side) * half + i * (half // 2), half // 2), half // 2)
        sums[OUT, i] = Rows(out_row_ref.at[other], out_ref.at[side, piece], out_sems.at[i])
        sums[ROW, i] = Rows(d_x.at[0, piece], d_tokens_ref.at[side, piece], row_sems.at[i])
    kern_sideways = "y" in ORDER[KERN]
    sums[KERN, 0] = Sum([kern_base] + take(len(ORDER[KERN]) + 2), kern_sems, ORDER[KERN], keep_kern)
    share = width // 16
    for t in range(tiles):

        def keep_both(own, given, sideways, t=t):
            for i, target in enumerate((key_out, value_out)):
                part = slice(i * share, (i + 1) * share)
                put(target, t * tile, own[part], given[part], sideways)

        def keep_key(own, given, sideways, t=t):
            put(key_out, t * tile, own, given, sideways)

        def keep_value(own, given, sideways, t=t):
            put(value_out, t * tile, own, given, sideways)

        orders = ORDER[KV][t]
        if len(orders) == 1:
            sums[KEY, t] = Sum([kv_base.at[t]] + take(5), kv_sems.at[t, 0], orders[0], keep_both)
        else:
            for i, (name, keep) in enumerate(((KEY, keep_key), (VALUE, keep_value))):
                part = kv_base.at[t, :, :, :, :, i * share : (i + 1) * share]
                sums[name, t] = Sum([part] + take(5), kv_sems.at[t, i], orders[i], keep)

    def events(step, number):
        follow(sums, BACK_PLAN.get((step, number), ()))

    def slots(first, last, number):
        for step in range(first, last):
            if BACK_PLAN.get((step, number)):
                pl.when(j == step)(functools.partial(events, step, number))

    def keep_out():
        return pltpu.make_async_copy(out_row_ref.at[own_rows], out_ref.at[side], own_sems.at[0])

    def keep_row():
        return pltpu.make_async_copy(d_x.at[1], d_tokens_ref.at[side], own_sems.at[1])

    late = [
        pltpu.make_async_copy(source, target, in_sems.at[i])
        for i, (source, target) in enumerate(((a_one_hbm, a_one), (x_hbm, x), (d_hidden_hbm, d_hidden)))
    ]

    @pl.when(j == 0)
    def _():
        greet((CORE, MIDDLE, NEAR, FAR, SIDE))
        events(0, 0)
        keep_out().start()
        for copy in late:
            copy.start()
        up_ref[...] = up_part_ref[...]
        down_ref[...] = down_part_ref[...]

    def kernel_product(sign, re, im, lanes):
        s = [(spec_one[b, re, lanes], spec_one[b, im, lanes]) for b in range(blocks)]
        x = [(spec_two[b, re, lanes], spec_two[b, im, lanes]) for b in range(blocks)]
        after = None
        for d in range(blocks - 1, -1, -1):
            yr, yi = multiply_conj(*x[0], *s[d])
            for i in range(d + 1, blocks):
                pr, pi = multiply_conj(*x[i - d], *s[i])
                yr, yi = yr + pr, yi + pi
            if after is None:
                hr, hi = yr, yi
            else:
                hr, hi = yr + sign * after[1], yi - sign * after[0]
            after = (yr, yi)
            prod[d, re, lanes] = hr.astype(BF16)
            prod[d, im, lanes] = hi.astype(BF16)

    @pl.when(j < tiles)
    def _():
        for b in range(blocks):
            rows = slice(b * BLOCK, (b + 1) * BLOCK)
            spec_one[b] = dot(table_ref[...], d_state_ref[rows, :])
            spec_two[b] = dot(table_ref[...], mixed_ref[rows, :])

    slots(0, tiles, 1)

    @pl.when(j < tiles)
    def _():
        spectral_loop(tile, kernel_product)

    slots(0, tiles, 2)

    @pl.when(j < tiles)
    def _():
        parts = [dot(back_ref[...], prod[b]) * (1.0 / BLOCK) for b in range(blocks)]
        kern_parts = jnp.concatenate(parts, axis=0)
        if kern_sideways:
            columns = pl.ds(pl.multiple_of(j * (tile // 2), tile // 2), tile // 2)
        else:
            columns = pl.ds(pl.multiple_of(j * tile, tile), tile)
        spread(kern_parts, kern_base.at[..., columns], kern_sideways)

    @pl.when(j == tiles - 1)
    def _():
        total[...] = jnp.zeros_like(total)
        late[0].wait()

    slots(0, tiles, 3)

    def state_product(sign, re, im, lanes):
        s = [(spec_one[b, re, lanes], spec_one[b, im, lanes]) for b in range(blocks)]
        h = [(kern_ref[b, re, lanes].astype(F32), kern_ref[b, im, lanes].astype(F32)) for b in range(blocks)]
        for b in range(blocks):
            yr, yi = multiply_conj(*h[0], *s[b])
            for i in range(b + 1, blocks):
                pr, pi = multiply_conj(*h[i - b], *s[i])
                yr, yi = yr + pr, yi + pi
            prod[b, re, lanes] = yr.astype(BF16)
            prod[b, im, lanes] = yi.astype(BF16)

    @pl.when(j >= tiles)
    def _():
        for b in range(blocks):
            spec_one[b] = dot(table_ref[...], d_state_ref[b * BLOCK : (b + 1) * BLOCK, :])

    slots(tiles, 2 * tiles, 1)

    @pl.when(j >= tiles)
    def _():
        spectral_loop(tile, state_product)

    slots(tiles, 2 * tiles, 2)

    @pl.when(j >= tiles)
    def _():
        for b in range(blocks):
            rows = slice(b * BLOCK, (b + 1) * BLOCK)
            mask = live_rows(live, b * BLOCK, BLOCK)
            d_mixed = dot(back_ref[...], prod[b]).astype(BF16).astype(F32)
            d_values[rows, :] = (mask * d_mixed * shifted_ref[rows, :].astype(F32)).astype(BF16)
            d_shifted = (d_mixed * v_ref[rows, :].astype(F32)).astype(BF16)
            spec_one[b] = dot(table_ref[...], d_shifted)
            spec_two[b] = dot(table_ref[...], k_ref[rows, :])

    slots(tiles, 2 * tiles, 3)

    def shift_product(sign, re, im, lanes):
        tr = tapspec_ref[re, lanes]
        ti = tapspec_ref[im, lanes]
        s = [(spec_one[b, re, lanes], spec_one[b, im, lanes]) for b in range(blocks)]
        x = [(spec_two[b, re, lanes], spec_two[b, im, lanes]) for b in range(blocks)]
        u = [multiply_conj(tr, ti, *s[b]) for b in range(blocks)]
        sum_re, sum_im = multiply_conj(*x[0], *s[0])
        for b in range(blocks):
            yr, yi = u[b]
            if b < blocks - 1:
                yr, yi = yr + sign * u[b + 1][1], yi - sign * u[b + 1][0]
            prod[b, re, lanes] = yr.astype(BF16)
            prod[b, im, lanes] = yi.astype(BF16)
            if b > 0:
                wr = x[b][0] - sign * x[b - 1][1]
                wi = x[b][1] + sign * x[b - 1][0]
                pr, pi = multiply_conj(wr, wi, *s[b])
                sum_re, sum_im = sum_re + pr, sum_im + pi
        shift_prod[re, lanes] = sum_re.astype(BF16)
        shift_prod[im, lanes] = sum_im.astype(BF16)

    def token_grad(rows):
        return (
            total[rows, :]
            + dot_nt(d_query_ref[rows, :], wq_ref[...])
            + dot_nt(d_keys[rows, :], wk_ref[...])
            + dot_nt(d_values[rows, :], wv_ref[...])
        )

    @pl.when(j >= tiles)
    def _():
        spectral_loop(tile, shift_product)

    slots(tiles, 2 * tiles, 4)

    @pl.when(j >= tiles)
    def _():
        for b in range(blocks):
            rows = slice(b * BLOCK, (b + 1) * BLOCK)
            mask = live_rows(live, b * BLOCK, BLOCK)
            d_keys[rows, :] = (mask * dot(back_ref[...], prod[b])).astype(BF16)
        taps = d_taps.shape[0]
        columns = pl.ds(pl.multiple_of((j - tiles) * tile, tile), tile)
        d_taps[:, columns] = dot(back_ref[:taps, :], shift_prod[...]) * (1.0 / BLOCK)
        for i, source in enumerate((d_keys, d_values)):
            spread(dot_tn(a_one[...], source[...]), kv_base.at[j - tiles, :, :, :, :, i * share : (i + 1) * share])

    slots(tiles, 2 * tiles, 5)

    @pl.when(jnp.logical_and(j >= tiles, j < 2 * tiles - 1))
    def _():
        for b in range(blocks):
            rows = slice(b * BLOCK, (b + 1) * BLOCK)
            total[rows, :] = token_grad(rows)

    slots(tiles, 2 * tiles, 6)

    @pl.when(j == 2 * tiles - 1)
    def _():
        late[1].wait()
        late[2].wait()
        gain_sum = jnp.zeros((1, width), F32)
        count = half // BLOCK
        for b in range(2 * count):
            low = (1 - side if b < count else side) * half + (b % count) * BLOCK
            rows = pl.ds(pl.multiple_of(low, BLOCK), BLOCK)
            normed, inv = norm_stats(x[rows, :].astype(F32))
            grad_in = token_grad(rows)
            gain_sum = gain_sum + jnp.sum(grad_in * normed, axis=0, keepdims=True)
            pulled = d_hidden[rows, :] + norm_pull(grad_in, normed, inv, row_of(gain_ref))
            d_x[b // count, (b % count) * BLOCK : (b % count + 1) * BLOCK, :] = pulled.astype(BF16)
            events(2 * tiles - 1, 7 + b)
        keep_row().start()
        gains = jnp.concatenate([gain_sum, gain_two_grad_ref[...], jnp.zeros((6 - each, width), F32)], axis=0)
        for owner, place in enumerate(places(lax.axis_index("dp"), 16, (1, 2, 4, 8))):
            taps_base[(*place, slice(0, each))] = d_taps[owner * each : (owner + 1) * each, :]
            taps_base[(*place, slice(each, 8))] = gains
        events(2 * tiles - 1, 11)
        follow(sums, BACK_LEFT)
        keep_out().wait()
        keep_row().wait()


def mixer_back_call(
    lengths, out_row, a_one, d_state, d_query, mixed, shifted, k, v, wq, wk, wv, kern, tapspec, tables, x, gain, d_hidden,
    d_gain_two, coef, rate, begun, taps_count, tile,
):
    length, width = a_one.shape
    blocks = length // BLOCK
    half = length // 2
    table, back = tables
    share = width // 16
    ks = length // 16
    count = width // tile
    both = lambda j: (0, lax.rem(j, count))
    first = lambda j: (0, jnp.minimum(j, count - 1))
    second = lambda j: (0, jnp.maximum(j - count, 0))
    rows_second = pl.BlockSpec((length, tile), second)
    weight = pl.BlockSpec((width, tile), second)
    anywhere = pl.BlockSpec(memory_space=pl.ANY)
    low = lambda *shape: jax.ShapeDtypeStruct(shape, BF16)
    full = lambda *shape: jax.ShapeDtypeStruct(shape, F32)
    vmem = lambda *shape: pltpu.VMEM(shape, BF16)
    wide = lambda *shape: pltpu.VMEM(shape, F32)
    sems = lambda *shape: pltpu.SemaphoreType.DMA(shape)
    up_part, down_part, left = begun
    states, channels = rate.shape
    each = states // 16
    lands = []
    for name, index, exchange, _ in FEED_LEFT:
        order = ORDER[name][index]
        if name == DOWN:
            lands += gather_landings(*down_part.shape, order)[exchange + 1 :]
        else:
            lands += landings(share, width, order)[exchange + 1 :]
    bits = [(2, 2, 2), (2, 2), (2,), (), ()]
    lands += [wide(*bits[n], 2 * each, channels) for n in range(4)]
    lands += [wide(*bits[n], 8, width) for n in range(5)]
    lands += landings(ks, width, ORDER[KERN])
    for t in range(count):
        orders = ORDER[KV][t]
        for order in orders:
            lands += landings(2 * share // len(orders), tile, order)
    out_shape = [
        low(2, half, width),
        low(2, half, width),
        full(1, width // 16),
        full(1, width // 16),
        full(each, channels),
        full(each, channels),
        full(each, channels),
        full(*up_part.shape),
        full(*down_part.shape),
        full(share, width),
        full(share, width),
        full(share, width),
        full(share, width),
    ]
    return pl.pallas_call(
        mixer_back_body,
        grid=(2 * count,),
        in_specs=[pl.BlockSpec(memory_space=pltpu.SMEM), anywhere]
        + [pl.BlockSpec((length, tile), both), rows_second, pl.BlockSpec((length, tile), first)]
        + [rows_second] * 3
        + [weight] * 3
        + [
            pl.BlockSpec((blocks, 2 * BLOCK, tile), lambda j: (0, 0, jnp.maximum(j - count, 0))),
            pl.BlockSpec((2 * BLOCK, tile), second),
            once(table.shape),
            once(back.shape),
            once((width,)),
            once((1, width)),
            once(coef.shape),
            once(rate.shape),
            once(up_part.shape),
            once(down_part.shape),
        ]
        + [once(s.shape) for s in left]
        + [anywhere] * 3,
        out_specs=[anywhere, anywhere] + [once(s.shape) for s in out_shape[2:]],
        out_shape=out_shape,
        scratch_shapes=[
            wide(length, width),
            wide(blocks, 2 * BLOCK, tile),
            wide(blocks, 2 * BLOCK, tile),
            vmem(blocks, 2 * BLOCK, tile),
            vmem(2 * BLOCK, tile),
            vmem(length, tile),
            vmem(length, tile),
            vmem(2, half, width),
            vmem(length, width),
            vmem(length, width),
            wide(length, width),
            wide(taps_count, width),
            wide(ks, width),
            wide(2, 2, 2, 2, 8, width),
            sems(5, 2),
            wide(2, 2, 2, 2, 2 * each, channels),
            sems(4, 2),
            vmem(*base_shape(ks, width, ORDER[KERN])),
            vmem(count, *base_shape(2 * share, tile, "")),
            sems(len(left), 6, 2),
            sems(6, 2),
            sems(count, 2, 6, 2),
            sems(2, 2),
            sems(2, 2),
            sems(2),
            sems(3),
            *lands,
        ],
        compiler_params=pltpu.CompilerParams(
            vmem_limit_bytes=62 * 1024 * 1024, collective_id=2, has_side_effects=True
        ),
        cost_estimate=cost(26e9, 40e6),
        name="mixer_back",
    )(
        lengths, out_row, d_state, d_query, mixed, shifted, k, v, wq, wk, wv, kern, tapspec, table, back, gain,
        d_gain_two, coef, rate, up_part, down_part, *left, a_one, x, d_hidden,
    )


MICRO = 2


epsilon = 1e-05
highest = lax.Precision.HIGHEST


def layer_norm(rows, gain):
    center = rows - jnp.mean(rows, axis=-1, keepdims=True)
    spread = jnp.mean(center * center, axis=-1, keepdims=True)
    return center * lax.rsqrt(spread + epsilon) * gain


def exact_gelu(values):
    return jax.nn.gelu(values, approximate=False)


def project(rows, weight):
    return jnp.einsum("rtd,de->rte", rows, weight, preferred_element_type=jnp.float32)


def project_back(rows, weight):
    return jnp.einsum("rte,de->rtd", rows, weight, preferred_element_type=jnp.float32)


def weight_grad(left, right):
    return jnp.einsum("rtd,rte->de", left, right, preferred_element_type=jnp.float32)


def depth_conv(signal, kernel_taps):
    channels = signal.shape[2]
    return lax.conv_general_dilated(
        signal,
        kernel_taps,
        (1,),
        "VALID",
        dimension_numbers=("NWC", "WIO", "NWC"),
        feature_group_count=channels,
        precision=highest,
    )


def shift_conv(extended, taps, length):
    flipped = jnp.transpose(taps[:, ::-1])[:, None, :]
    return depth_conv(extended[:, 1:, :], flipped)[:, :length, :]


def shift_back(extended, taps, length):
    forward_taps = jnp.transpose(taps)[:, None, :]
    return depth_conv(extended, forward_taps)[:, :length, :]


def taps_grad(grad_rows, extended, width_taps):
    rows_count, span, channels = extended.shape
    left = jnp.transpose(extended, (2, 0, 1)).reshape(1, channels * rows_count, span)
    right = jnp.transpose(grad_rows, (2, 0, 1))
    result = lax.conv_general_dilated(
        left,
        right,
        (1,),
        "VALID",
        dimension_numbers=("NCW", "OIW", "NCW"),
        feature_group_count=channels,
        precision=highest,
    )
    return result[0][:, ::-1][:, :width_taps]


def diag_kernel(coef, rate, length):
    steps = lax.iota(jnp.float32, length)
    return jnp.sum(coef[:, :, None] * jnp.exp(-rate[:, :, None] * steps), axis=1)


def dft_tables(length):
    period = 2 * length
    time_index = lax.iota(jnp.int32, length)[:, None]
    freq_index = lax.iota(jnp.int32, length + 1)[None, :]
    phase_index = time_index * freq_index % period
    angles = phase_index.astype(jnp.float32) * (2.0 * math.pi / period)
    cos_table = jnp.cos(angles)
    sin_table = jnp.sin(angles)
    edges = (freq_index == 0) | (freq_index == length)
    weights = jnp.where(edges, 1.0, 2.0).astype(jnp.float32) / period
    return (cos_table, sin_table, cos_table * weights, sin_table * weights)


def spectrum(signal, cos_table, sin_table):
    real_part = jnp.einsum("rtc,tf->rfc", signal, cos_table, precision=highest)
    imag_part = -jnp.einsum("rtc,tf->rfc", signal, sin_table, precision=highest)
    return (real_part, imag_part)


def inverse(real_part, imag_part, cos_weighted, sin_weighted):
    first = jnp.einsum("rfc,tf->rtc", real_part, cos_weighted, precision=highest)
    second = jnp.einsum("rfc,tf->rtc", imag_part, sin_weighted, precision=highest)
    return first - second


def split_channels(
    tokens,
    lengths,
    gain_one,
    w_query,
    w_key,
    w_value,
    w_out,
    gain_two,
    w_up,
    w_down,
    shift_taps,
    diag_coef,
    diag_rate,
    cotangent,
):
    rows_dev, tok_len, model_width = tokens.shape
    length = tok_len * lax.axis_size("seq")
    width_taps = shift_taps.shape[1]
    first_pos = lax.axis_index("seq") * tok_len
    positions = first_pos + lax.iota(jnp.int32, tok_len)
    mask_all = (positions[None, :] < lengths[:, None]).astype(jnp.float32)[:, :, None]
    cos_table, sin_table, cos_weighted, sin_weighted = dft_tables(length)

    def kernel_of(coef_in, rate_in):
        return diag_kernel(coef_in, rate_in, length)

    kernel, kernel_pull = jax.vjp(kernel_of, diag_coef, diag_rate)
    kernel_real = jnp.einsum("ct,tf->fc", kernel, cos_table, precision=highest)
    kernel_imag = -jnp.einsum("ct,tf->fc", kernel, sin_table, precision=highest)
    taps_acc = jnp.zeros(shift_taps.shape, jnp.float32)
    spec_real_acc = jnp.zeros((length + 1, shift_taps.shape[0]), jnp.float32)
    spec_imag_acc = jnp.zeros((length + 1, shift_taps.shape[0]), jnp.float32)
    grad_gain_one = jnp.zeros(gain_one.shape, jnp.float32)
    grad_gain_two = jnp.zeros(gain_two.shape, jnp.float32)
    grad_query = jnp.zeros(w_query.shape, jnp.float32)
    grad_key = jnp.zeros(w_key.shape, jnp.float32)
    grad_value = jnp.zeros(w_value.shape, jnp.float32)
    grad_out = jnp.zeros(w_out.shape, jnp.float32)
    grad_up = jnp.zeros(w_up.shape, jnp.float32)
    grad_down = jnp.zeros(w_down.shape, jnp.float32)
    rows_mb = rows_dev // MICRO
    out_list = []
    dx_list = []
    for micro_step in range(MICRO):
        low_row = micro_step * rows_mb
        x_rows = tokens[low_row : low_row + rows_mb].astype(jnp.float32)
        live_mask = mask_all[low_row : low_row + rows_mb]
        grad_rows = cotangent[low_row : low_row + rows_mb].astype(jnp.float32)
        norm_one, norm_one_pull = jax.vjp(layer_norm, x_rows, gain_one)
        a_one = norm_one.astype(jnp.bfloat16)
        query_rows = project(a_one, w_query)
        key_rows = (project(a_one, w_key) * live_mask).astype(jnp.bfloat16)
        value_rows = (project(a_one, w_value) * live_mask).astype(jnp.bfloat16)
        keys_ch, values_ch = (
            lax.all_to_all(key_rows, "seq", split_axis=2, concat_axis=1, tiled=True),
            lax.all_to_all(value_rows, "seq", split_axis=2, concat_axis=1, tiled=True),
        )
        key_ext = jnp.pad(keys_ch.astype(jnp.float32), ((0, 0), (width_taps, 0), (0, 0)))
        shifted = shift_conv(key_ext, shift_taps, length)
        values_here = values_ch.astype(jnp.float32)
        mixed_ch = (shifted * values_here).astype(jnp.bfloat16)
        mixed_real, mixed_imag = spectrum(mixed_ch.astype(jnp.float32), cos_table, sin_table)
        state = inverse(
            mixed_real * kernel_real - mixed_imag * kernel_imag,
            mixed_real * kernel_imag + mixed_imag * kernel_real,
            cos_weighted,
            sin_weighted,
        )
        state_tok = lax.all_to_all(
            state.astype(jnp.bfloat16), "seq", split_axis=1, concat_axis=2, tiled=True
        )
        state_rows = state_tok.astype(jnp.float32)
        gated_rows = (query_rows * state_rows).astype(jnp.bfloat16)
        hidden = x_rows + live_mask * project(gated_rows, w_out)
        norm_two, norm_two_pull = jax.vjp(layer_norm, hidden, gain_two)
        a_two = norm_two.astype(jnp.bfloat16)
        pre_act = project(a_two, w_up)
        act_value, gelu_pull = jax.vjp(exact_gelu, pre_act)
        activation = act_value.astype(jnp.bfloat16)
        result = hidden + live_mask * project(activation, w_down)
        out_list.append(result.astype(jnp.bfloat16))
        d_down = (live_mask * grad_rows).astype(jnp.bfloat16)
        grad_down = grad_down + weight_grad(activation, d_down)
        d_act = project_back(d_down, w_down)
        d_pre = gelu_pull(d_act)[0].astype(jnp.bfloat16)
        grad_up = grad_up + weight_grad(a_two, d_pre)
        d_a_two = project_back(d_pre, w_up)
        d_hidden_norm, d_gain_two = norm_two_pull(d_a_two)
        grad_gain_two = grad_gain_two + d_gain_two
        d_hidden = grad_rows + d_hidden_norm
        d_mixer = (live_mask * d_hidden).astype(jnp.bfloat16)
        grad_out = grad_out + weight_grad(gated_rows, d_mixer)
        d_gated = project_back(d_mixer, w_out)
        d_query = (d_gated * state_rows).astype(jnp.bfloat16)
        d_state = (d_gated * query_rows).astype(jnp.bfloat16)
        d_state_ch = lax.all_to_all(d_state, "seq", split_axis=2, concat_axis=1, tiled=True)
        grad_real, grad_imag = spectrum(d_state_ch.astype(jnp.float32), cos_table, sin_table)
        d_mixed = inverse(
            kernel_real * grad_real + kernel_imag * grad_imag,
            kernel_real * grad_imag - kernel_imag * grad_real,
            cos_weighted,
            sin_weighted,
        )
        spec_real_acc = spec_real_acc + jnp.sum(
            mixed_real * grad_real + mixed_imag * grad_imag, axis=0
        )
        spec_imag_acc = spec_imag_acc + jnp.sum(
            mixed_real * grad_imag - mixed_imag * grad_real, axis=0
        )
        d_mixed_low = d_mixed.astype(jnp.bfloat16)
        d_mix_ch = d_mixed_low.astype(jnp.float32)
        d_shifted = d_mix_ch * values_here
        d_values_ch = (d_mix_ch * shifted).astype(jnp.bfloat16)
        grad_ext = jnp.pad(d_shifted, ((0, 0), (0, width_taps), (0, 0)))
        d_keys_ch = shift_back(grad_ext, shift_taps, length).astype(jnp.bfloat16)
        taps_acc = taps_acc + taps_grad(d_shifted, key_ext, width_taps)
        keys_back, values_back = (
            lax.all_to_all(d_keys_ch, "seq", split_axis=1, concat_axis=2, tiled=True),
            lax.all_to_all(d_values_ch, "seq", split_axis=1, concat_axis=2, tiled=True),
        )
        mask_low = live_mask.astype(jnp.bfloat16)
        d_keys = keys_back * mask_low
        d_values = values_back * mask_low
        grad_query = grad_query + weight_grad(a_one, d_query)
        grad_key = grad_key + weight_grad(a_one, d_keys)
        grad_value = grad_value + weight_grad(a_one, d_values)
        d_a_one = (
            project_back(d_query, w_query)
            + project_back(d_keys, w_key)
            + project_back(d_values, w_value)
        )
        d_x_norm, d_gain_one = norm_one_pull(d_a_one)
        grad_gain_one = grad_gain_one + d_gain_one
        dx_list.append((d_hidden + d_x_norm).astype(jnp.bfloat16))
    d_kernel = jnp.einsum("fc,tf->ct", spec_real_acc, cos_weighted, precision=highest) - jnp.einsum(
        "fc,tf->ct", spec_imag_acc, sin_weighted, precision=highest
    )
    d_coef, d_rate = kernel_pull(d_kernel)
    taps_part, coef_part, rate_part = (
        lax.psum_scatter(
            taps_acc.astype(jnp.bfloat16), "dp", scatter_dimension=1, tiled=True
        ).astype(jnp.float32),
        lax.psum_scatter(d_coef.astype(jnp.bfloat16), "dp", scatter_dimension=1, tiled=True).astype(
            jnp.float32
        ),
        lax.psum_scatter(d_rate.astype(jnp.bfloat16), "dp", scatter_dimension=1, tiled=True).astype(
            jnp.float32
        ),
    )
    shares = (
        lax.psum_scatter(
            grad_gain_one.astype(jnp.bfloat16), "dp", scatter_dimension=0, tiled=True
        ).astype(jnp.float32),
        lax.psum_scatter(
            grad_query.astype(jnp.bfloat16), "dp", scatter_dimension=0, tiled=True
        ).astype(jnp.float32),
        lax.psum_scatter(
            grad_key.astype(jnp.bfloat16), "dp", scatter_dimension=0, tiled=True
        ).astype(jnp.float32),
        lax.psum_scatter(
            grad_value.astype(jnp.bfloat16), "dp", scatter_dimension=0, tiled=True
        ).astype(jnp.float32),
        lax.psum_scatter(
            grad_out.astype(jnp.bfloat16), "dp", scatter_dimension=0, tiled=True
        ).astype(jnp.float32),
        lax.psum_scatter(
            grad_gain_two.astype(jnp.bfloat16), "dp", scatter_dimension=0, tiled=True
        ).astype(jnp.float32),
        lax.psum_scatter(
            grad_up.astype(jnp.bfloat16), "dp", scatter_dimension=0, tiled=True
        ).astype(jnp.float32),
        lax.psum_scatter(
            grad_down.astype(jnp.bfloat16), "dp", scatter_dimension=0, tiled=True
        ).astype(jnp.float32),
    )
    totals = (
        lax.psum(shares[0].astype(jnp.bfloat16), "seq").astype(jnp.float32),
        lax.psum(shares[1].astype(jnp.bfloat16), "seq").astype(jnp.float32),
        lax.psum(shares[2].astype(jnp.bfloat16), "seq").astype(jnp.float32),
        lax.psum(shares[3].astype(jnp.bfloat16), "seq").astype(jnp.float32),
        lax.psum(shares[4].astype(jnp.bfloat16), "seq").astype(jnp.float32),
        lax.psum(shares[5].astype(jnp.bfloat16), "seq").astype(jnp.float32),
        lax.psum(shares[6].astype(jnp.bfloat16), "seq").astype(jnp.float32),
        lax.psum(shares[7].astype(jnp.bfloat16), "seq").astype(jnp.float32),
    )
    out_rows = jnp.concatenate(out_list, axis=0)
    dx_rows = jnp.concatenate(dx_list, axis=0)
    return (
        out_rows,
        dx_rows,
        totals[0],
        totals[1],
        totals[2],
        totals[3],
        totals[4],
        totals[5],
        totals[6],
        totals[7],
        taps_part,
        coef_part,
        rate_part,
    )


def settle_body(*refs):
    count = (len(refs) - 1) // 3
    sources, targets, held, sems = refs[:count], refs[count : 2 * count], refs[2 * count : 3 * count], refs[-1]
    reads = [pltpu.make_async_copy(sources[i], held[i], sems.at[0, i]) for i in range(count)]
    writes = [pltpu.make_async_copy(held[i], targets[i], sems.at[1, i]) for i in range(count)]
    for copy in reads:
        copy.start()
    for read, write in zip(reads, writes):
        read.wait()
        write.start()
    for copy in writes:
        copy.wait()


def settle_call(arrays):
    anywhere = pl.BlockSpec(memory_space=pl.ANY)
    return pl.pallas_call(
        settle_body,
        in_specs=[anywhere] * len(arrays),
        out_specs=[anywhere] * len(arrays),
        out_shape=[jax.ShapeDtypeStruct(array.shape, array.dtype) for array in arrays],
        scratch_shapes=[pltpu.VMEM(array.shape, array.dtype) for array in arrays]
        + [pltpu.SemaphoreType.DMA((2, len(arrays)))],
        compiler_params=params(),
        cost_estimate=cost(1e3, 10e6),
        name="settle",
    )(*arrays)


def split_rows(
    tokens, lengths, gain_one, w_query, w_key, w_value, w_out, gain_two, w_up, w_down,
    shift_taps, diag_coef, diag_rate, cotangent,
):
    states = diag_coef.shape[1]
    tile = 256
    tables = transform_tables()
    coef, rate, taps = diag_coef.T, diag_rate.T, shift_taps.T
    x, cot, a_one, q, k, v, kern, tapspec, hidden, a_two, shifted, mixed, state = mixer_call(
        lengths, tokens, cotangent, coef, rate, taps, gain_one, gain_two, w_query, w_key, w_value, w_out, tables, tile
    )
    out_row, d_hidden, d_query, d_state, d_gain_two, up_part, down_part, *left = ffn_call(
        lengths, a_two, cot, hidden, gain_two, w_up, w_down, w_out, state, q, a_one
    )
    out, d_tokens, gain_one_grad, gain_two_grad, taps_grad, coef_grad, rate_grad, up, down, wout, query, key, value = (
        settle_call(mixer_back_call(
            lengths, out_row, a_one, d_state, d_query, mixed, shifted, k, v, w_query, w_key, w_value, kern, tapspec,
            tables, x, gain_one, d_hidden, d_gain_two, coef, rate, (up_part, down_part, left), states, tile,
        ))
    )
    return (
        out,
        d_tokens,
        gain_one_grad.reshape(-1),
        query,
        key,
        value,
        wout,
        gain_two_grad.reshape(-1),
        up,
        down,
        taps_grad.T,
        coef_grad.T,
        rate_grad.T,
    )


def solution(mesh):
    in_specs = (
        P("dp", "seq", None),
        P("dp"),
        P(),
        P(),
        P(),
        P(),
        P(),
        P(),
        P(),
        P(),
        P("seq", None),
        P("seq", None),
        P("seq", None),
        P("dp", "seq", None),
    )
    out_specs = (
        P("dp", "seq", None),
        P("dp", "seq", None),
        P("dp"),
        P("dp", None),
        P("dp", None),
        P("dp", None),
        P("dp", None),
        P("dp"),
        P("dp", None),
        P("dp", None),
        P("seq", "dp"),
        P("seq", "dp"),
        P("seq", "dp"),
    )

    def per_device(*args):
        tokens, shift_taps = args[0], args[10]
        rows, positions, width = tokens.shape
        fits = (
            mesh.shape["seq"] == rows == 2
            and mesh.shape["dp"] == 16
            and positions * 2 % BLOCK == 0
            and width % 256 == 0
            and shift_taps.shape[1] <= BLOCK
        )
        return split_rows(*args) if fits else split_channels(*args)

    return jax.shard_map(
        per_device, mesh=mesh, in_specs=in_specs, out_specs=out_specs, check_vma=False
    )
```

```python
import functools
import math

import jax
import jax.numpy as jnp
import numpy as np
from jax import lax
from jax.experimental import pallas as pl
from jax.experimental.pallas import tpu as pltpu
from jax.sharding import PartitionSpec as P

BLOCK = 256
CHUNK = 16
LANES = 128
EPS = 1e-05
F32 = jnp.float32
BF16 = jnp.bfloat16
VMEM_BYTES = 60 * 1024 * 1024


def dot(a, b):
    return lax.dot_general(a, b, (((1,), (0,)), ((), ())), preferred_element_type=F32)


def dot_nt(a, b):
    return lax.dot_general(a, b, (((1,), (1,)), ((), ())), preferred_element_type=F32)


def dot_tn(a, b):
    return lax.dot_general(a, b, (((0,), (0,)), ((), ())), preferred_element_type=F32)


def params():
    return pltpu.CompilerParams(vmem_limit_bytes=VMEM_BYTES)


def cost(flops, byte_count):
    return pl.CostEstimate(flops=int(flops), bytes_accessed=int(byte_count), transcendentals=0)


def transform_tables():
    freq = np.concatenate([np.arange(0, BLOCK, 2), np.arange(1, BLOCK, 2)]).astype(np.float64)
    time = np.arange(BLOCK, dtype=np.float64)
    angle = (2.0 * math.pi / (2 * BLOCK)) * (freq[:, None] + 0.5) * time[None, :]
    table = np.concatenate([np.cos(angle), -np.sin(angle)], axis=0)
    return jnp.asarray(table, dtype=BF16), jnp.asarray(table.T.copy(), dtype=BF16)


def norm_stats(rows):
    center = rows - jnp.mean(rows, axis=-1, keepdims=True)
    spread = jnp.mean(center * center, axis=-1, keepdims=True)
    inv = lax.rsqrt(spread + EPS)
    return center * inv, inv


def norm_pull(grad, normed, inv, gain):
    scaled = grad * gain
    mean_one = jnp.mean(scaled, axis=-1, keepdims=True)
    mean_two = jnp.mean(scaled * normed, axis=-1, keepdims=True)
    return (scaled - mean_one - normed * mean_two) * inv


def live_rows(length, first, count):
    rows = lax.broadcasted_iota(jnp.int32, (count, 1), 0) + first
    return (rows < length).astype(F32)


def spectral_loop(channels, body):
    half = BLOCK // 2
    for parity in range(2):
        sign = 1.0 if parity == 0 else -1.0

        def step(index, carry, sign=sign, parity=parity):
            low = pl.multiple_of(parity * half + index * CHUNK, CHUNK)
            body(sign, pl.ds(low, CHUNK), pl.ds(low + BLOCK, CHUNK), slice(0, channels))
            return carry

        lax.fori_loop(0, half // CHUNK, step, 0)


def multiply(ar, ai, br, bi):
    return ar * br - ai * bi, ar * bi + ai * br


def multiply_conj(ar, ai, br, bi):
    return ar * br + ai * bi, ar * bi - ai * br


def gelu_pair(x):
    bell = jnp.exp(x * x * -0.5)
    size = jnp.abs(x)
    t = 1.0 / (1.0 + (0.3275911 / math.sqrt(2.0)) * size)
    poly = t * (
        0.5 * 0.254829592
        + t * (0.5 * -0.284496736 + t * (0.5 * 1.421413741 + t * (0.5 * -1.453152027 + t * (0.5 * 1.061405429))))
    )
    tail = poly * bell
    phi = jnp.where(x >= 0.0, 1.0 - tail, tail)
    return x * phi, phi + x * bell * (1.0 / math.sqrt(2.0 * math.pi))


def bit_of(index, bit):
    return lax.rem(index // bit, 2)


def partner(axis, bit):
    index = lax.axis_index(axis)
    return {axis: index + bit * (1 - 2 * bit_of(index, bit))}


UP, DOWN, GATE, KERN, KEY, VALUE, KV, OUT, ROW, COEF, TAPS = range(11)
CORE, MIDDLE, NEAR, FAR, SIDE = ("dp", 1), ("dp", 2), ("dp", 4), ("dp", 8), ("seq", 1)


def greet(partners):
    barrier = pltpu.get_barrier_semaphore()
    for axis, bit in partners:
        pl.semaphore_signal(barrier, inc=1, device_id=partner(axis, bit), device_id_type=pl.DeviceIdType.MESH)
    pl.semaphore_wait(barrier, len(partners))


def transfer(source, target, sems, to):
    return pltpu.make_async_remote_copy(
        src_ref=source,
        dst_ref=target,
        send_sem=sems.at[0],
        recv_sem=sems.at[1],
        device_id=partner(*to),
        device_id_type=pl.DeviceIdType.MESH,
    )


def add_into(target, other):
    *lead, rows, _ = target.shape
    for place in np.ndindex(*lead):
        for low in range(0, rows, 48):
            piece = (*place, slice(low, min(low + 48, rows)))
            target[piece] = target[piece] + other[piece]


def places(mine, owners, bits):
    own = [bit_of(mine, bit) for bit in bits]
    return [
        tuple(1 - own[i] if (owner // bit) % 2 else own[i] for i, bit in enumerate(bits)) for owner in range(owners)
    ]


def spread(value, base, sideways=False):
    value = value.astype(BF16)
    share = value.shape[0] // 16
    half = value.shape[1] // 2
    side = lax.axis_index("seq")
    for owner, (core, *place) in enumerate(places(lax.axis_index("dp"), 16, (1, 2, 4, 8))):
        rows = value[owner * share : (owner + 1) * share]
        if sideways:
            base[(core, side, *place)] = rows[:, :half]
            base[(core, 1 - side, *place)] = rows[:, half:]
        else:
            base[(core, *place)] = rows


AXES = {"c": CORE, "x": MIDDLE, "n": NEAR, "f": FAR, "y": SIDE}


class Sum:
    def __init__(self, refs, sems, order, final=None, across=True):
        self.refs, self.sems, self.final, self.across = refs, sems, final, across
        self.order = "c" + order
        self.sideways = "y" in order
        self.last = len(self.order)

    def part(self, step, half):
        ref = self.refs[step]
        if step == self.last:
            return ref
        left = [axis for axis in "cyxnf" if axis in self.order[step:]]
        return ref.at[(slice(None),) * left.index(self.order[step]) + (half,)]

    def copy(self, step):
        axis = AXES[(self.order + "y")[step]]
        return transfer(self.part(step, 1), self.refs[step + 1], self.sems.at[step], axis)

    def start(self, step):
        self.copy(step).start()

    def wait(self, step):
        self.copy(step).wait()
        if step < self.last:
            add_into(self.refs[step + 1], self.part(step, 0))
            if step == self.last - 1 and not self.across:
                self.final(self.refs[step + 1][...])
        else:
            self.final(self.refs[step][...], self.refs[step + 1][...], self.sideways)


class Gather:
    def __init__(self, z, refs, sems, order, final=None):
        self.refs, self.sems, self.final = refs, sems, final
        self.order = "c" + order
        self.sideways = "y" in order
        self.lead = len(self.order)
        self.last = self.lead + 2
        mine = lax.axis_index("dp")
        near = bit_of(mine, 4) == z % 2
        far = bit_of(mine, 8) == z // 2
        both = jnp.logical_and(near, far)
        self.gives = (jnp.logical_not(near), jnp.logical_and(near, jnp.logical_not(far)), both)
        self.takes = (near, both, both)

    def part(self, step, half):
        ref = self.refs[step]
        if step >= self.lead:
            return ref
        left = [axis for axis in "cyx" if axis in self.order[step:]]
        return ref.at[(slice(None),) * left.index(self.order[step]) + (half,)]

    def copy(self, step):
        axis = AXES[(self.order + "nfy")[step]]
        return transfer(self.part(step, 1), self.refs[step + 1], self.sems.at[step], axis)

    def start(self, step):
        if step < self.lead:
            self.copy(step).start()
        else:

            @pl.when(self.gives[step - self.lead])
            def _():
                self.copy(step).start()

    def wait(self, step):
        if step < self.lead:
            self.copy(step).wait()
            add_into(self.refs[step + 1], self.part(step, 0))
            return

        @pl.when(self.gives[step - self.lead])
        def _():
            self.copy(step).wait_send()

        @pl.when(self.takes[step - self.lead])
        def _():
            self.copy(step).wait_recv()
            if step < self.last:
                add_into(self.refs[step + 1], self.part(step, 0))
            else:
                self.final(self.refs[step][...], self.refs[step + 1][...], self.sideways)


class Rows:
    def __init__(self, source, target, sems):
        self.copy = transfer(source, target, sems, SIDE)

    def start(self, _):
        self.copy.start()

    def wait(self, _):
        self.copy.wait()


def follow(sums, events):
    for name, index, exchange, begin in events:
        if begin:
            sums[name, index].start(exchange)
        else:
            sums[name, index].wait(exchange)


def put(target, low, own, given, sideways):
    if sideways:
        side = lax.axis_index("seq")
        half = own.shape[-1]
        target[:, pl.ds(pl.multiple_of(low + side * half, LANES), half)] = own.astype(F32)
        target[:, pl.ds(pl.multiple_of(low + (1 - side) * half, LANES), half)] = given.astype(F32)
    else:
        target[:, low : low + own.shape[-1]] = own.astype(F32) + given.astype(F32)


def base_shape(rows, columns, order):
    return (2, 2, 2, 2, 2, rows, columns // 2) if "y" in order else (2, 2, 2, 2, rows, columns)


def landings(rows, columns, order):
    *bits, rows, columns = base_shape(rows, columns, order)
    return [pltpu.VMEM((*bits[n + 1 :], rows, columns), BF16) for n in range(len(bits))] + [pltpu.VMEM((rows, columns), BF16)]


def gather_landings(rows, columns, order):
    columns = columns // 2 if "y" in order else columns
    return [pltpu.VMEM((*(2,) * (len(order) - n), rows, columns), BF16) for n in range(len(order) + 1)] + [
        pltpu.VMEM((rows, columns), BF16) for _ in range(3)
    ]


def row_of(ref):
    return ref[...].reshape(1, ref.shape[0])


def once(shape):
    zeros = (0,) * len(shape)
    return pl.BlockSpec(shape, lambda *_: zeros, pipeline_mode=pl.Buffered(1))


def mixer_body(
    lengths_ref, tokens_hbm, cot_hbm, coef_ref, rate_ref, taps_ref, gain_one_ref, gain_two_ref, wq_hbm, wk_hbm, wv_hbm, wout_hbm,
    table_ref, back_ref,
    x_hbm, cot_out, a_one_hbm, q_hbm, k_hbm, v_hbm, kern_hbm, tapspec_hbm, hidden_hbm, a_two_hbm,
    shifted_ref, mixed_ref, state_ref,
    x, a_one, q, k, v, total, a_two, wq, wk, wv, wout, kern, tapspec, taps, other, current, kern_time, near, far,
    spec, prod, in_sems, own_sems, out_sems, token_sems, cot_sems, other_sems, taps_sems, unit_sems,
):
    j = pl.program_id(0)
    steps = pl.num_programs(0)
    length, width = x.shape
    half = length // 2
    tile = shifted_ref.shape[1]
    blocks = length // BLOCK
    states, channels = coef_ref.shape
    side = lax.axis_index("seq")
    live = lengths_ref[side]
    core = bit_of(lax.axis_index("dp"), 1)
    own_rows = pl.ds(pl.multiple_of(side * half, half), half)

    weights = [
        pltpu.make_async_copy(source, target, in_sems.at[i])
        for i, (source, target) in enumerate(((wq_hbm, wq), (wk_hbm, wk), (wv_hbm, wv), (wout_hbm, wout)))
    ]
    outs = [
        pltpu.make_async_copy(source, target, out_sems.at[i])
        for i, (source, target) in enumerate(
            (
                (x, x_hbm), (a_one, a_one_hbm), (q, q_hbm), (k, k_hbm), (v, v_hbm), (kern, kern_hbm),
                (tapspec, tapspec_hbm),
            )
        )
    ]
    own_x = pltpu.make_async_copy(tokens_hbm.at[side], x.at[own_rows], own_sems.at[0])
    own_cot = pltpu.make_async_copy(cot_hbm.at[side], cot_out.at[own_rows], own_sems.at[1])
    other_x = [
        transfer(
            tokens_hbm.at[1 - side, pl.ds(i * BLOCK, BLOCK)],
            x.at[pl.ds(pl.multiple_of(side * half + i * BLOCK, BLOCK), BLOCK)],
            token_sems.at[i],
            SIDE,
        )
        for i in range(half // BLOCK)
    ]
    other_cot = transfer(cot_hbm.at[1 - side], cot_out.at[own_rows], cot_sems, SIDE)
    wanted = pl.ds(pl.multiple_of(core * LANES, LANES), 2 * LANES)
    params = (coef_ref, rate_ref)
    other_params = [transfer(params[i].at[:, wanted], other.at[i], other_sems.at[i], SIDE) for i in range(2)]
    own_lanes = pl.ds(pl.multiple_of(side * channels, LANES), channels)
    other_taps = transfer(taps.at[:, own_lanes], taps.at[:, own_lanes], taps_sems, SIDE)

    def unit_columns(number, of_core):
        tile_of = (2 * of_core, 1, 2 * of_core)[number]
        half_of = (side, side + of_core - 2 * side * of_core, 1 - side)[number]
        return pl.ds(pl.multiple_of(half_of * channels + tile_of * LANES, LANES), LANES)

    def unit_copy(number):
        columns = unit_columns(number, core)
        return transfer(kern_time.at[:, columns], kern_time.at[:, columns], unit_sems.at[number], CORE)

    def unit(number):
        if number == 0:
            for part in range(2):
                current[part] = params[part][:, pl.ds(pl.multiple_of(core * 2 * LANES, LANES), LANES)]
        elif number == 1:

            @pl.when(core == 0)
            def _():
                for part in range(2):
                    current[part] = params[part][:, LANES : 2 * LANES]

            @pl.when(core == 1)
            def _():
                for part in range(2):
                    other_params[part].wait()
                    current[part] = other[part, :, :LANES]

        else:

            @pl.when(core == 0)
            def _():
                for part in range(2):
                    other_params[part].wait()
                    current[part] = other[part, :, :LANES]

            @pl.when(core == 1)
            def _():
                for part in range(2):
                    current[part] = other[part, :, LANES:]

        columns = unit_columns(number, core)
        step_count, together = 32, 8
        groups = length // step_count
        near_time = lax.broadcasted_iota(jnp.int32, (step_count, 1), 0).astype(F32)
        far_time = lax.broadcasted_iota(jnp.int32, (groups, 1), 0).astype(F32) * step_count

        def fill(n, carry):
            rate = current[1, pl.ds(n, 1), :]
            near[n] = jnp.exp(-rate * near_time)
            far_n = current[0, pl.ds(n, 1), :] * jnp.exp(-rate * far_time)
            for g in range(groups // together):
                far[g, n] = far_n[g * together : (g + 1) * together, :]
            return carry

        lax.fori_loop(0, states, fill, 0)

        def group(g, carry):
            def add(n, sums):
                near_n = near[n]
                return tuple(sums[i] + far[g, n, i : i + 1, :] * near_n for i in range(together))

            zeros = tuple(jnp.zeros((step_count, LANES), F32) for _ in range(together))
            sums = lax.fori_loop(0, states, add, zeros, unroll=4)
            for i in range(together):
                place = pl.multiple_of((g * together + i) * step_count, step_count)
                kern_time[pl.ds(place, step_count), columns] = sums[i].astype(BF16)
            return carry

        lax.fori_loop(0, groups // together, group, 0)
        unit_copy(number).start()

    def project_block(low):
        rows = pl.ds(pl.multiple_of(low, BLOCK), BLOCK)
        normed, _ = norm_stats(x[rows, :].astype(F32))
        a_rows = (normed * row_of(gain_one_ref)).astype(BF16)
        a_one[rows, :] = a_rows
        mask = live_rows(live, low, BLOCK)
        k[rows, :] = (dot(a_rows, wk[...]) * mask).astype(BF16)
        v[rows, :] = (dot(a_rows, wv[...]) * mask).astype(BF16)
        q[rows, :] = dot(a_rows, wq[...]).astype(BF16)

    @pl.when(j == 0)
    def _():
        own_x.start()
        own_cot.start()
        for copy in weights:
            copy.start()
        greet((CORE, SIDE))
        for copy in other_params:
            copy.start()
        taps[:, own_lanes] = taps_ref[...].astype(BF16)
        other_taps.start()
        total[...] = jnp.zeros_like(total)
        unit(0)
        for copy in other_x:
            copy.start()
        unit(1)
        unit(2)
        for copy in weights:
            copy.wait()
        own_x.wait()

        def own_block(b, carry):
            project_block(side * half + b * BLOCK)
            return carry

        lax.fori_loop(0, half // BLOCK, own_block, 0)
        other_taps.wait()
        for number in range(3):
            unit_copy(number).wait()

        def tile_spectra(t, carry):
            columns = pl.ds(pl.multiple_of(t * tile, tile), tile)
            for b in range(blocks):
                spec[b] = dot(table_ref[...], kern_time[b * BLOCK : (b + 1) * BLOCK, columns])

            def combine(sign, re, im, lanes):
                to = pl.ds(pl.multiple_of(t * tile + lanes.start, LANES), lanes.stop - lanes.start)
                for b in range(blocks):
                    out_re = spec[b, re, lanes]
                    out_im = spec[b, im, lanes]
                    if b > 0:
                        out_re = out_re - sign * spec[b - 1, im, lanes]
                        out_im = out_im + sign * spec[b - 1, re, lanes]
                    kern[b, re, to] = (out_re * (1.0 / BLOCK)).astype(BF16)
                    kern[b, im, to] = (out_im * (1.0 / BLOCK)).astype(BF16)

            spectral_loop(tile, combine)
            tapspec[:, columns] = dot(table_ref[:, : taps.shape[0]], taps[:, columns]) * (1.0 / BLOCK)
            return carry

        lax.fori_loop(0, width // tile, tile_spectra, 0)
        outs[5].start()
        outs[6].start()
        other_cot.start()
        for i, copy in enumerate(other_x):
            copy.wait()
            if i == len(other_x) - 1:
                outs[0].start()
            project_block((1 - side) * half + i * BLOCK)
        for copy in outs[1:5]:
            copy.start()

    @pl.when(j > 0)
    def _():
        t = j - 1
        columns = pl.ds(pl.multiple_of(t * tile, tile), tile)
        for b in range(blocks):
            spec[b] = dot(table_ref[...], k[b * BLOCK : (b + 1) * BLOCK, columns])

        def shift_product(sign, re, im, lanes):
            at = pl.ds(pl.multiple_of(t * tile + lanes.start, LANES), lanes.stop - lanes.start)
            tr = tapspec[re, at]
            ti = tapspec[im, at]
            before = None
            for b in range(blocks):
                xr = spec[b, re, lanes]
                xi = spec[b, im, lanes]
                if b == 0:
                    sr, si = xr, xi
                else:
                    sr, si = xr - sign * before[1], xi + sign * before[0]
                before = (xr, xi)
                yr, yi = multiply(sr, si, tr, ti)
                prod[b, re, lanes] = yr.astype(BF16)
                prod[b, im, lanes] = yi.astype(BF16)

        spectral_loop(tile, shift_product)
        for b in range(blocks):
            rows = slice(b * BLOCK, (b + 1) * BLOCK)
            shifted = dot(back_ref[...], prod[b])
            shifted_ref[rows, :] = shifted.astype(BF16)
            mixed_ref[rows, :] = (shifted * v[rows, columns].astype(F32)).astype(BF16)
            spec[b] = dot(table_ref[...], mixed_ref[rows, :])

        def state_product(sign, re, im, lanes):
            at = pl.ds(pl.multiple_of(t * tile + lanes.start, LANES), lanes.stop - lanes.start)
            s = [(spec[b, re, lanes], spec[b, im, lanes]) for b in range(blocks)]
            h = [(kern[b, re, at].astype(F32), kern[b, im, at].astype(F32)) for b in range(blocks)]
            for i in range(blocks):
                yr, yi = multiply(*s[i], *h[0])
                for d in range(1, i + 1):
                    pr, pi = multiply(*s[i - d], *h[d])
                    yr, yi = yr + pr, yi + pi
                prod[i, re, lanes] = yr.astype(BF16)
                prod[i, im, lanes] = yi.astype(BF16)

        spectral_loop(tile, state_product)
        for b in range(blocks):
            rows = slice(b * BLOCK, (b + 1) * BLOCK)
            state = dot(back_ref[...], prod[b]).astype(BF16)
            state_ref[rows, :] = state
            gated = (q[rows, columns].astype(F32) * state.astype(F32)).astype(BF16)
            total[rows, :] += dot(gated, wout[columns, :])

    @pl.when(j == steps - 1)
    def _():
        def last_copies(b):
            rows = pl.ds(pl.multiple_of(b * BLOCK, BLOCK), BLOCK)
            return [
                pltpu.make_async_copy(total.at[rows], hidden_hbm.at[rows], out_sems.at[7 + b]),
                pltpu.make_async_copy(a_two.at[rows], a_two_hbm.at[rows], out_sems.at[7 + blocks + b]),
            ]

        def block(b, carry):
            rows = pl.ds(pl.multiple_of(b * BLOCK, BLOCK), BLOCK)
            mask = live_rows(live, b * BLOCK, BLOCK)
            hidden = x[rows, :].astype(F32) + mask * total[rows, :]
            total[rows, :] = hidden
            normed, _ = norm_stats(hidden)
            a_two[rows, :] = (normed * row_of(gain_two_ref)).astype(BF16)
            for copy in last_copies(b):
                copy.start()
            return carry

        lax.fori_loop(0, blocks, block, 0)
        for b in range(blocks):
            for copy in last_copies(b):
                copy.wait()
        for copy in outs:
            copy.wait()
        own_cot.wait()
        other_cot.wait()


def mixer_call(lengths, tokens, cot, coef, rate, taps, gain_one, gain_two, wq, wk, wv, wout, tables, tile):
    _, half, width = tokens.shape
    length = 2 * half
    blocks = length // BLOCK
    table, back = tables
    states, channels = taps.shape
    anywhere = pl.BlockSpec(memory_space=pl.ANY)
    rows_tile = pl.BlockSpec((length, tile), lambda j: (0, jnp.maximum(j - 1, 0)))
    low = lambda *shape: jax.ShapeDtypeStruct(shape, BF16)
    full = lambda *shape: jax.ShapeDtypeStruct(shape, F32)
    vmem = lambda *shape: pltpu.VMEM(shape, BF16)
    wide = lambda *shape: pltpu.VMEM(shape, F32)
    sems = lambda *shape: pltpu.SemaphoreType.DMA(shape)
    rows = low(length, width)
    return pl.pallas_call(
        mixer_body,
        grid=(1 + width // tile,),
        in_specs=[
            pl.BlockSpec(memory_space=pltpu.SMEM),
            anywhere,
            anywhere,
            once(coef.shape),
            once(rate.shape),
            once(taps.shape),
            once((width,)),
            once((width,)),
            anywhere,
            anywhere,
            anywhere,
            anywhere,
            once(table.shape),
            once(back.shape),
        ],
        out_specs=[anywhere] * 10 + [rows_tile] * 3,
        out_shape=[
            rows, rows, rows, rows, rows, rows,
            low(blocks, 2 * BLOCK, width), full(2 * BLOCK, width), full(length, width), rows,
            rows, rows, rows,
        ],
        scratch_shapes=[
            vmem(length, width),
            vmem(length, width),
            vmem(length, width),
            vmem(length, width),
            vmem(length, width),
            wide(length, width),
            vmem(length, width),
            vmem(*wq.shape),
            vmem(*wk.shape),
            vmem(*wv.shape),
            vmem(*wout.shape),
            vmem(blocks, 2 * BLOCK, width),
            wide(2 * BLOCK, width),
            vmem(states, width),
            wide(2, states, 2 * LANES),
            wide(2, states, LANES),
            vmem(length, width),
            wide(states, 32, LANES),
            wide(length // 256, states, 8, LANES),
            wide(blocks, 2 * BLOCK, tile),
            vmem(blocks, 2 * BLOCK, tile),
            sems(4),
            sems(2),
            sems(7 + 2 * blocks),
            sems(half // BLOCK, 2),
            sems(2),
            sems(2, 2),
            sems(2),
            sems(3, 2),
        ],
        compiler_params=pltpu.CompilerParams(vmem_limit_bytes=VMEM_BYTES, collective_id=3, has_side_effects=True),
        cost_estimate=cost(16e9, 40e6),
        name="mixer_forward",
    )(lengths, tokens, cot, coef, rate, taps, gain_one, gain_two, wq, wk, wv, wout, table, back)


FIRST_ROWS = 128

ORDER = {UP: ["nyfx", "nfyx", "yxnf", "xynf"], DOWN: ["yx", "yx", "xy", "yx"], GATE: ["nfx", "xnf"], KERN: ["xnf", "nxf", "xnf"], KV: [["xnf"], ["xnf"], ["xnf", "xfn"]]}
FEED_PLAN = {
    (0, 4): ((DOWN, 0, 0, 1),),
    (0, 5): ((UP, 0, 0, 1),),
    (1, 1): ((DOWN, 0, 0, 0), (UP, 0, 0, 0), (UP, 0, 1, 1), (DOWN, 0, 1, 1)),
    (1, 4): ((DOWN, 1, 0, 1),),
    (1, 5): ((UP, 1, 0, 1),),
    (2, 1): ((DOWN, 1, 0, 0), (UP, 0, 1, 0), (DOWN, 0, 1, 0), (UP, 1, 0, 0), (UP, 1, 1, 1), (DOWN, 1, 1, 1), (DOWN, 0, 2, 1)),
    (2, 4): ((DOWN, 2, 0, 1),),
    (2, 5): ((UP, 2, 0, 1), (UP, 0, 2, 1)),
    (3, 0): ((DOWN, 0, 2, 0), (DOWN, 0, 3, 1)),
    (3, 1): ((DOWN, 2, 0, 0), (UP, 1, 1, 0), (DOWN, 1, 1, 0), (UP, 2, 0, 0), (UP, 2, 1, 1), (DOWN, 2, 1, 1)),
    (3, 2): ((UP, 1, 2, 1),),
    (3, 3): ((UP, 0, 2, 0),),
    (3, 4): ((DOWN, 3, 0, 1),),
    (3, 5): ((DOWN, 0, 3, 0), (UP, 3, 0, 1), (DOWN, 1, 2, 1)),
    (4, 2): ((UP, 0, 3, 1),),
    (4, 3): ((OUT, 2, 0, 1),),
    (4, 4): ((DOWN, 3, 0, 0),),
    (4, 5): ((UP, 2, 1, 0), (DOWN, 2, 1, 0), (UP, 3, 0, 0), (GATE, 0, 0, 1)),
    (4, 7): ((UP, 1, 2, 0), (GATE, 1, 0, 1)),
    (4, 8): ((OUT, 2, 0, 0),),
}
FEED_LEFT = (
    (UP, 3, 0, True),
    (DOWN, 3, 0, True),
    (UP, 2, 1, True),
    (DOWN, 2, 1, True),
    (UP, 1, 2, True),
    (DOWN, 0, 3, True),
    (DOWN, 1, 2, False),
    (GATE, 0, 0, False),
    (UP, 0, 3, False),
    (GATE, 1, 0, False),
)


def ffn_body(
    lengths_ref, a_two_ref, cot_ref, gain_ref, up_ref, down_ref, hidden_hbm, wout_hbm, state_hbm, q_hbm, a_one_hbm,
    out_hbm, d_hidden_hbm, d_query_hbm, d_state_hbm, out_first_hbm, gain_grad_ref, up_out, down_out, *rest,
):
    left = rest[: len(FEED_LEFT)]
    (
        total, back, act, d_pre, d_down, hidden, wout, state, q, a_one, in_sems, out_sems,
        up_flat, up_side, down_flat, down_side, gate_base, up_sems, down_sems, gate_sems, row_sems, *lands,
    ) = rest[len(FEED_LEFT) :]
    j = pl.program_id(0)
    quarters = 4
    length, width = a_two_ref.shape
    tile = up_ref.shape[1]
    live = lengths_ref[lax.axis_index("seq")]
    rows_count = 256

    sums = {}
    lands = list(lands)
    up_bases, down_bases = (up_flat, up_side), (down_flat, down_side)

    def take(count):
        taken = lands[:count]
        del lands[:count]
        return taken

    for t in range(quarters):
        order, gather = ORDER[UP][t], ORDER[DOWN][t]

        def keep_up(own, given, sideways, t=t):
            put(up_out, t * tile, own, given, sideways)

        def keep_down(own, given, sideways):
            put(down_out, 0, own, given, sideways)

        refs = [up_bases["y" in order]] + take(len(order) + 2)
        sums[UP, t] = Sum(refs, up_sems.at[t], order, keep_up)
        refs = [down_bases["y" in gather]] + take(len(gather) + 4)
        sums[DOWN, t] = Gather(t, refs, down_sems.at[t], gather, keep_down)
    for i in range(2):
        sums[GATE, i] = Sum([gate_base.at[i]] + take(5), gate_sems.at[i], ORDER[GATE][i])

    half = length // 2
    first = pl.ds(pl.multiple_of((1 - lax.axis_index("seq")) * half, half), out_first_hbm.shape[0])
    sums[OUT, 2] = Rows(d_pre.at[first], out_first_hbm, row_sems)

    def run(step, number):
        follow(sums, FEED_PLAN.get((step, number), ()))

    def slot(step, number):
        if FEED_PLAN.get((step, number)):

            @pl.when(j == step)
            def _():
                run(step, number)

    def slots(number):
        for step in range(quarters):
            slot(step, number)

    late = [
        pltpu.make_async_copy(source, target, in_sems.at[i])
        for i, (source, target) in enumerate(
            ((hidden_hbm, hidden), (q_hbm, q), (state_hbm, state), (wout_hbm, wout), (a_one_hbm, a_one))
        )
    ]

    @pl.when(j == 0)
    def _():
        for copy in late:
            copy.start()
        greet((CORE, MIDDLE, NEAR, FAR, SIDE))
        for low in range(0, length, rows_count):
            rows = slice(low, low + rows_count)
            d_down[rows, :] = (cot_ref[rows, :].astype(F32) * live_rows(live, low, rows_count)).astype(BF16)
        total[...] = jnp.zeros_like(total)
        back[...] = jnp.zeros_like(back)
        down_out[...] = jnp.zeros_like(down_out)
        up_out[...] = jnp.zeros_like(up_out)

    def chunk(low):
        rows = pl.ds(low, rows_count)
        pre = dot(a_two_ref[rows, :], up_ref[...])
        d_act = dot_nt(d_down[rows, :], down_ref[...])
        value, slope = gelu_pair(pre)
        act[rows, :] = value.astype(BF16)
        d_pre[rows, :] = (d_act * slope).astype(BF16)
        total[rows, :] += dot(act[rows, :], down_ref[...])
        back[rows, :] += dot_nt(d_pre[rows, :], up_ref[...])

    @pl.when(j < quarters)
    def _():
        def step(part, carry):
            chunk(pl.multiple_of(part * rows_count, rows_count))
            for t in range(1, quarters):
                for number in range(4):
                    if FEED_PLAN.get((t, number)):
                        pl.when(jnp.logical_and(j == t, part == number))(functools.partial(run, t, number))
            return carry

        lax.fori_loop(0, 4, step, 0)

    share = tile // 4
    for sideways in (False, True):
        steps = [t for t in range(quarters) if ("y" in ORDER[DOWN][t]) == sideways]

        @pl.when(functools.reduce(jnp.logical_or, [j == t for t in steps], False))
        def _(sideways=sideways):
            value = dot_tn(act[...], d_down[...]).astype(BF16)
            side = lax.axis_index("seq")
            for owner, (core, x) in enumerate(places(lax.axis_index("dp"), 4, (1, 2))):
                rows = value[owner * share : (owner + 1) * share]
                if sideways:
                    down_side[core, side, x] = rows[:, : width // 2]
                    down_side[core, 1 - side, x] = rows[:, width // 2 :]
                else:
                    down_flat[core, x] = rows

    slots(4)

    for sideways in (False, True):
        steps = [t for t in range(quarters) if ("y" in ORDER[UP][t]) == sideways]

        @pl.when(functools.reduce(jnp.logical_or, [j == t for t in steps], False))
        def _(sideways=sideways):
            spread(dot_tn(a_two_ref[...], d_pre[...]), up_bases[sideways], sideways)

    slots(5)

    def send(source, target, number):
        return pltpu.make_async_copy(source, target, out_sems.at[number])

    @pl.when(j == quarters)
    def _():
        run(4, 0)
        late[0].wait()
        late[1].wait()
        late[2].wait()
        gain_sum = jnp.zeros((1, width), F32)
        for low in range(0, length, rows_count):
            rows = slice(low, low + rows_count)
            mask = live_rows(live, low, rows_count)
            before = hidden[rows, :]
            d_pre[rows, :] = (before + mask * total[rows, :]).astype(BF16)
            normed, inv = norm_stats(before)
            grad_in = back[rows, :]
            gain_sum = gain_sum + jnp.sum(grad_in * normed, axis=0, keepdims=True)
            d_hidden = cot_ref[rows, :].astype(F32) + norm_pull(grad_in, normed, inv, row_of(gain_ref))
            back[rows, :] = d_hidden
            d_down[rows, :] = (mask * d_hidden).astype(BF16)
            gated = q[rows, :].astype(F32) * state[rows, :].astype(F32)
            act[rows, :] = gated.astype(BF16)
            run(4, 1 + low // rows_count)
        gain_grad_ref[...] = gain_sum
        copies = [send(d_pre, out_hbm, 0), send(back, d_hidden_hbm, 1)]
        for copy in copies:
            copy.start()
        spread(dot_tn(act[...], d_down[...]), gate_base.at[0])
        run(4, 5)
        late[3].wait()
        late[4].wait()
        for low in range(0, length, rows_count):
            rows = slice(low, low + rows_count)
            d_gated = dot_nt(d_down[rows, :], wout[...])
            total[rows, :] = d_gated
            act[rows, :] = (d_gated * state[rows, :].astype(F32)).astype(BF16)
        copies.append(send(act, d_query_hbm, 2))
        copies[2].start()
        run(4, 6)
        spread(dot_tn(a_one[...], act[...]), gate_base.at[1])
        run(4, 7)
        for low in range(0, length, rows_count):
            rows = slice(low, low + rows_count)
            d_down[rows, :] = (total[rows, :] * q[rows, :].astype(F32)).astype(BF16)
        copies.append(send(d_down, d_state_hbm, 3))
        copies[3].start()
        run(4, 8)
        for i, (name, index, exchange, waited) in enumerate(FEED_LEFT):
            if not waited:
                sums[name, index].wait(exchange)
            copies.append(send(sums[name, index].refs[exchange + 1], left[i], 4 + i))
            copies[-1].start()
        for copy in copies:
            copy.wait()


def ffn_call(lengths, a_two, cot, hidden, gain, up, down, wout, state, q, a_one):
    length, width = a_two.shape
    hidden_units = up.shape[1]
    tile = hidden_units // 4
    su, sd = width // 16, tile // 4
    rows_full = once((length, width))
    anywhere = pl.BlockSpec(memory_space=pl.ANY)
    low = lambda *shape: jax.ShapeDtypeStruct(shape, BF16)
    full = lambda *shape: jax.ShapeDtypeStruct(shape, F32)
    vmem = lambda *shape: pltpu.VMEM(shape, BF16)
    wide = lambda *shape: pltpu.VMEM(shape, F32)
    sems = lambda *shape: pltpu.SemaphoreType.DMA(shape)
    shape_of = {}
    for t in range(4):
        shape_of[UP, t] = landings(su, tile, ORDER[UP][t])
        shape_of[DOWN, t] = gather_landings(sd, width, ORDER[DOWN][t])
    for i in range(2):
        shape_of[GATE, i] = landings(su, width, ORDER[GATE][i])
    left = [low(*shape_of[name, index][exchange].shape) for name, index, exchange, _ in FEED_LEFT]
    for name, index, exchange, _ in FEED_LEFT:
        shapes = shape_of[name, index]
        shapes[exchange + 1 :] = [vmem(16, LANES)] * (len(shapes) - exchange - 1)
    lands = [shape for shapes in shape_of.values() for shape in shapes]
    return pl.pallas_call(
        ffn_body,
        grid=(5,),
        in_specs=[
            pl.BlockSpec(memory_space=pltpu.SMEM),
            rows_full,
            rows_full,
            once((width,)),
            pl.BlockSpec((width, tile), lambda j: (0, jnp.minimum(j, 3))),
            pl.BlockSpec((tile, width), lambda j: (jnp.minimum(j, 3), 0)),
        ]
        + [anywhere] * 5,
        out_specs=[anywhere] * 5 + [once((1, width)), once((su, hidden_units)), once((sd, width))] + [anywhere] * len(left),
        out_shape=[
            low(length, width),
            full(length, width),
            low(length, width),
            low(length, width),
            low(FIRST_ROWS, width),
            full(1, width),
            full(su, hidden_units),
            full(sd, width),
            *left,
        ],
        scratch_shapes=[
            wide(length, width),
            wide(length, width),
            vmem(length, tile),
            vmem(length, tile),
            vmem(length, width),
            wide(length, width),
            vmem(*wout.shape),
            vmem(length, width),
            vmem(length, width),
            vmem(length, width),
            sems(5),
            sems(4 + len(left)),
            vmem(*base_shape(su, tile, "")) if any("y" not in order for order in ORDER[UP]) else vmem(16, LANES),
            vmem(*base_shape(su, tile, "y")) if any("y" in order for order in ORDER[UP]) else vmem(16, LANES),
            vmem(2, 2, sd, width) if any("y" not in order for order in ORDER[DOWN]) else vmem(16, LANES),
            vmem(2, 2, 2, sd, width // 2) if any("y" in order for order in ORDER[DOWN]) else vmem(16, LANES),
            vmem(2, *base_shape(su, width, "")),
            sems(4, 6, 2),
            sems(4, 6, 2),
            sems(2, 5, 2),
            sems(2),
            *lands,
        ],
        compiler_params=pltpu.CompilerParams(vmem_limit_bytes=62 * 1024 * 1024, collective_id=1, has_side_effects=True),
        cost_estimate=cost(12 * length * width * hidden_units, 40e6),
        name="feed_forward",
    )(lengths, a_two, cot, gain, up, down, hidden, wout, state, q, a_one)


KERN_LAST = 2
BACK_PLAN = {
    (0, 0): ((UP, 3, 1, 1), (DOWN, 3, 1, 1), (UP, 2, 2, 1), (DOWN, 2, 2, 1), (UP, 1, 3, 1), (GATE, 0, 1, 1), (DOWN, 1, 3, 1), (GATE, 1, 1, 1), (DOWN, 0, 4, 1)),
    (0, 3): ((KERN, 0, 0, 1), (OUT, 0, 0, 1)),
    (1, 3): ((KERN, 0, 0, 0), (KERN, 1, 0, 1)),
    (2, 1): ((UP, 1, 3, 0), (KERN, 0, 1, 1), (OUT, 1, 0, 1)),
    (2, 2): ((DOWN, 1, 3, 0), (DOWN, 1, 4, 1)),
    (2, 3): ((DOWN, 0, 4, 0), (KERN, 1, 0, 0), (KERN, 2, 0, 1), (KERN, 1, 1, 1)),
    (3, 2): ((DOWN, 2, 2, 0), (UP, 2, 2, 0), (GATE, 0, 1, 0), (UP, 2, 3, 1)),
    (3, 3): ((KERN, 2, 0, 0),),
    (3, 5): ((KERN, 2, 1, 1), (KEY, 0, 0, 1), (DOWN, 2, 3, 1), (UP, 0, 4, 1), (UP, 1, 4, 1), (GATE, 0, 2, 1), (DOWN, 0, 5, 1)),
    (4, 3): ((KEY, 0, 0, 0), (DOWN, 3, 1, 0), (UP, 3, 1, 0), (GATE, 1, 1, 0), (KERN, 0, 1, 0), (UP, 2, 3, 0), (DOWN, 1, 4, 0), (KERN, 1, 1, 0), (KERN, 0, 2, 1), (KERN, 1, 2, 1), (UP, 3, 2, 1), (DOWN, 3, 2, 1), (KEY, 0, 1, 1)),
    (4, 4): ((DOWN, 1, 5, 1),),
    (4, 5): ((UP, 0, 4, 0), (UP, 1, 4, 0), (KEY, 1, 0, 1), (UP, 2, 4, 1), (UP, 0, 5, 1), (GATE, 1, 2, 1)),
    (4, 6): ((OUT, 0, 0, 0),),
    (5, 1): ((KERN, 2, 1, 0), (KERN, 2, 2, 1)),
    (5, 2): ((DOWN, 0, 5, 0), (UP, 1, 5, 1)),
    (5, 3): ((OUT, 1, 0, 0), (KEY, 1, 0, 0), (DOWN, 2, 3, 0), (GATE, 0, 2, 0), (KEY, 1, 1, 1), (DOWN, 2, 4, 1)),
    (5, 4): ((KERN, 0, 2, 0), (KERN, 1, 2, 0), (KERN, 0, 3, 1), (GATE, 0, 3, 1)),
    (5, 5): ((UP, 0, 5, 0), (UP, 3, 2, 0), (UP, 2, 4, 0), (VALUE, 2, 0, 1), (KERN, 1, 3, 1), (KEY, 2, 0, 1), (UP, 2, 5, 1)),
    (5, 7): ((DOWN, 1, 5, 0), (UP, 1, 5, 0), (ROW, 0, 0, 1), (UP, 3, 3, 1)),
    (5, 8): ((KERN, 2, 2, 0), (DOWN, 3, 2, 0), (ROW, 1, 0, 1), (KERN, 2, 3, 1)),
    (5, 9): ((VALUE, 2, 0, 0), (KEY, 2, 0, 0), (GATE, 1, 2, 0), (VALUE, 2, 1, 1), (KEY, 2, 1, 1)),
    (5, 10): ((KEY, 0, 1, 0), (DOWN, 3, 3, 1)),
    (5, 11): ((UP, 2, 5, 0), (TAPS, 0, 0, 1)),
}
BACK_LEFT = (
    (KEY, 0, 2, 1),
    (KERN, 0, 3, 0),
    (KERN, 0, 4, 1),
    (GATE, 1, 3, 1),
    (GATE, 0, 3, 0),
    (KERN, 1, 3, 0),
    (TAPS, 0, 0, 0),
    (KERN, 1, 4, 1),
    (TAPS, 0, 1, 1),
    (KEY, 1, 1, 0),
    (KERN, 2, 3, 0),
    (UP, 3, 3, 0),
    (KERN, 2, 4, 1),
    (UP, 3, 4, 1),
    (DOWN, 2, 4, 0),
    (KEY, 1, 2, 1),
    (KERN, 0, 4, 0),
    (DOWN, 2, 5, 1),
    (VALUE, 2, 1, 0),
    (KEY, 2, 1, 0),
    (VALUE, 2, 2, 1),
    (KEY, 2, 2, 1),
    (KERN, 1, 4, 0),
    (TAPS, 0, 1, 0),
    (GATE, 1, 3, 0),
    (KEY, 0, 2, 0),
    (KEY, 0, 3, 1),
    (KERN, 2, 4, 0),
    (COEF, 0, 0, 1),
    (TAPS, 0, 2, 1),
    (DOWN, 3, 3, 0),
    (UP, 3, 4, 0),
    (DOWN, 3, 4, 1),
    (COEF, 0, 0, 0),
    (COEF, 0, 1, 1),
    (UP, 3, 5, 1),
    (GATE, 0, 4, 1),
    (KEY, 2, 2, 0),
    (VALUE, 2, 2, 0),
    (VALUE, 2, 3, 1),
    (KEY, 2, 3, 1),
    (GATE, 1, 4, 1),
    (KEY, 1, 2, 0),
    (KEY, 1, 3, 1),
    (ROW, 0, 0, 0),
    (DOWN, 2, 5, 0),
    (TAPS, 0, 2, 0),
    (TAPS, 0, 3, 1),
    (KEY, 0, 3, 0),
    (KEY, 0, 4, 1),
    (COEF, 0, 1, 0),
    (COEF, 0, 2, 1),
    (UP, 3, 5, 0),
    (ROW, 1, 0, 0),
    (VALUE, 2, 3, 0),
    (VALUE, 2, 4, 1),
    (GATE, 0, 4, 0),
    (KEY, 2, 3, 0),
    (KEY, 2, 4, 1),
    (GATE, 1, 4, 0),
    (DOWN, 3, 4, 0),
    (DOWN, 3, 5, 1),
    (KEY, 0, 4, 0),
    (COEF, 0, 2, 0),
    (COEF, 0, 3, 1),
    (TAPS, 0, 3, 0),
    (TAPS, 0, 4, 1),
    (KEY, 1, 3, 0),
    (KEY, 1, 4, 1),
    (VALUE, 2, 4, 0),
    (KEY, 2, 4, 0),
    (COEF, 0, 3, 0),
    (TAPS, 0, 4, 0),
    (DOWN, 3, 5, 0),
    (KEY, 1, 4, 0),
)


def mixer_back_body(
    lengths_ref, out_row_ref, d_state_ref, d_query_ref, mixed_ref, shifted_ref, k_ref, v_ref,
    wq_ref, wk_ref, wv_ref, kern_ref, tapspec_ref, table_ref, back_ref, gain_ref, gain_two_grad_ref,
    coef_ref, rate_ref, up_part_ref, down_part_ref, *rest,
):
    left = rest[: len(FEED_LEFT)]
    (
        a_one_hbm, x_hbm, d_hidden_hbm,
        out_ref, d_tokens_ref, gain_one_out, gain_two_out, taps_out, coef_out, rate_out, up_ref, down_ref,
        wout_out, query_out, key_out, value_out,
        total, spec_one, spec_two, prod, shift_prod, d_keys, d_values, d_x, a_one, x, d_hidden, d_taps, d_kern,
        taps_base, taps_sems, coef_base, coef_sems,
        kern_base, kv_base, left_sems, kern_sems, kv_sems, out_sems, row_sems, own_sems, in_sems, *lands,
    ) = rest[len(FEED_LEFT) :]
    j = pl.program_id(0)
    length, width = a_one.shape
    half = length // 2
    tile = k_ref.shape[1]
    tiles = width // tile
    blocks = length // BLOCK
    side = lax.axis_index("seq")
    live = lengths_ref[side]
    own_rows = pl.ds(pl.multiple_of(side * half, half), half)

    sums = {}
    lands = list(lands)

    def take(count):
        taken = lands[:count]
        del lands[:count]
        return taken

    for i, (name, index, exchange, _) in enumerate(FEED_LEFT):

        def keep(own, given, sideways, name=name, index=index):
            if name == UP:
                put(up_ref, index * width, own, given, sideways)
            elif name == DOWN:
                put(down_ref, 0, own, given, sideways)
            else:
                put((wout_out, query_out)[index], 0, own, given, sideways)

        order = ORDER[name][index]
        refs = [None] * (exchange + 1) + [left[i]] + take(len(order) + (3 if name == DOWN else 1) - exchange)
        if name == DOWN:
            sums[name, index] = Gather(index, refs, left_sems.at[i], order, keep)
        else:
            sums[name, index] = Sum(refs, left_sems.at[i], order, keep)

    states, channels = rate_ref.shape
    each = states // 16

    def keep_kern(own, given, sideways, t):
        put(d_kern, t * tile, own, given, sideways)
        if t != KERN_LAST:
            return
        steps = d_kern.shape[0]
        first = lax.convert_element_type(lax.axis_index("dp") * steps, F32)
        for low in range(0, channels, LANES):
            lanes = slice(low, low + LANES)
            rate = rate_ref[:, lanes]
            from_lane = pl.ds(pl.multiple_of(side * channels + low, LANES), LANES)

            def group(g, sums, rate=rate, from_lane=from_lane):
                coef_sum, rate_sum = sums
                rows = d_kern[pl.ds(pl.multiple_of(g * 8, 8), 8), from_lane]
                for i in range(8):
                    time = first + lax.convert_element_type(g * 8 + i, F32)
                    term = jnp.exp(rate * -time) * rows[i : i + 1]
                    coef_sum = coef_sum + term
                    rate_sum = rate_sum + term * time
                return coef_sum, rate_sum

            zeros = jnp.zeros((states, LANES), F32)
            coef_sum, rate_sum = lax.fori_loop(0, steps // 8, group, (zeros, zeros))
            rate_sum = -coef_ref[:, lanes] * rate_sum
            for owner, place in enumerate(places(lax.axis_index("dp"), 16, (1, 2, 4, 8))):
                rows = slice(owner * each, (owner + 1) * each)
                coef_base[(*place, slice(0, each), lanes)] = coef_sum[rows]
                coef_base[(*place, slice(each, 2 * each), lanes)] = rate_sum[rows]

    def keep_coef(value):
        coef_out[...] = value[:each]
        rate_out[...] = value[each:]

    def keep_taps(own, given, sideways):
        both = own + given
        taps_out[...] = jnp.where(side == 0, both[:each, :channels], both[:each, channels:])
        gain_each = gain_one_out.shape[1]
        gains = pltpu.roll(both, width - lax.axis_index("dp") * gain_each, 1)
        gain_one_out[...] = gains[each : each + 1, :gain_each]
        gain_two_out[...] = gains[each + 1 : each + 2, :gain_each]

    sums[COEF, 0] = Sum([coef_base] + take(4), coef_sems, "xnf", keep_coef, across=False)
    sums[TAPS, 0] = Sum([taps_base] + take(5), taps_sems, "xnf", keep_taps)

    later = (half - FIRST_ROWS) // 2
    for i in range(2):
        low = FIRST_ROWS + i * later
        other = pl.ds(pl.multiple_of((1 - side) * half + low, 16), later)
        sums[OUT, i] = Rows(out_row_ref.at[other], out_ref.at[side, pl.ds(low, later)], out_sems.at[i])
        piece = pl.ds(i * (half // 2), half // 2)
        sums[ROW, i] = Rows(d_x.at[0, piece], d_tokens_ref.at[side, piece], row_sems.at[i])
    for t in range(tiles):
        keep = functools.partial(keep_kern, t=t)
        sums[KERN, t] = Sum([kern_base.at[t]] + take(5), kern_sems.at[t], ORDER[KERN][t], keep)
    share = width // 16
    for t in range(tiles):

        def keep_both(own, given, sideways, t=t):
            for i, target in enumerate((key_out, value_out)):
                part = slice(i * share, (i + 1) * share)
                put(target, t * tile, own[part], given[part], sideways)

        def keep_key(own, given, sideways, t=t):
            put(key_out, t * tile, own, given, sideways)

        def keep_value(own, given, sideways, t=t):
            put(value_out, t * tile, own, given, sideways)

        orders = ORDER[KV][t]
        if len(orders) == 1:
            sums[KEY, t] = Sum([kv_base.at[t]] + take(5), kv_sems.at[t, 0], orders[0], keep_both)
        else:
            for i, (name, keep) in enumerate(((KEY, keep_key), (VALUE, keep_value))):
                part = kv_base.at[t, :, :, :, :, i * share : (i + 1) * share]
                sums[name, t] = Sum([part] + take(5), kv_sems.at[t, i], orders[i], keep)

    def events(step, number):
        follow(sums, BACK_PLAN.get((step, number), ()))

    def slots(first, last, number):
        for step in range(first, last):
            if BACK_PLAN.get((step, number)):
                pl.when(j == step)(functools.partial(events, step, number))

    def keep_out():
        return pltpu.make_async_copy(out_row_ref.at[own_rows], out_ref.at[side], own_sems.at[0])

    def keep_row():
        return pltpu.make_async_copy(d_x.at[1], d_tokens_ref.at[side], own_sems.at[1])

    late = [
        pltpu.make_async_copy(source, target, in_sems.at[i])
        for i, (source, target) in enumerate(((a_one_hbm, a_one), (x_hbm, x), (d_hidden_hbm, d_hidden)))
    ]

    @pl.when(j == 0)
    def _():
        greet((CORE, MIDDLE, NEAR, FAR, SIDE))
        events(0, 0)
        keep_out().start()
        for copy in late:
            copy.start()
        up_ref[...] = up_part_ref[...]
        down_ref[...] = down_part_ref[...]

    def kernel_product(sign, re, im, lanes):
        s = [(spec_one[b, re, lanes], spec_one[b, im, lanes]) for b in range(blocks)]
        x = [(spec_two[b, re, lanes], spec_two[b, im, lanes]) for b in range(blocks)]
        after = None
        for d in range(blocks - 1, -1, -1):
            yr, yi = multiply_conj(*x[0], *s[d])
            for i in range(d + 1, blocks):
                pr, pi = multiply_conj(*x[i - d], *s[i])
                yr, yi = yr + pr, yi + pi
            if after is None:
                hr, hi = yr, yi
            else:
                hr, hi = yr + sign * after[1], yi - sign * after[0]
            after = (yr, yi)
            prod[d, re, lanes] = hr.astype(BF16)
            prod[d, im, lanes] = hi.astype(BF16)

    @pl.when(j < tiles)
    def _():
        for b in range(blocks):
            rows = slice(b * BLOCK, (b + 1) * BLOCK)
            spec_one[b] = dot(table_ref[...], d_state_ref[rows, :])
            spec_two[b] = dot(table_ref[...], mixed_ref[rows, :])

    slots(0, tiles, 1)

    @pl.when(j < tiles)
    def _():
        spectral_loop(tile, kernel_product)

    slots(0, tiles, 2)

    @pl.when(j < tiles)
    def _():
        parts = [dot(back_ref[...], prod[b]) * (1.0 / BLOCK) for b in range(blocks)]
        spread(jnp.concatenate(parts, axis=0), kern_base.at[j])

    @pl.when(j == tiles - 1)
    def _():
        total[...] = jnp.zeros_like(total)
        late[0].wait()

    slots(0, tiles, 3)

    def state_product(sign, re, im, lanes):
        s = [(spec_one[b, re, lanes], spec_one[b, im, lanes]) for b in range(blocks)]
        h = [(kern_ref[b, re, lanes].astype(F32), kern_ref[b, im, lanes].astype(F32)) for b in range(blocks)]
        for b in range(blocks):
            yr, yi = multiply_conj(*h[0], *s[b])
            for i in range(b + 1, blocks):
                pr, pi = multiply_conj(*h[i - b], *s[i])
                yr, yi = yr + pr, yi + pi
            prod[b, re, lanes] = yr.astype(BF16)
            prod[b, im, lanes] = yi.astype(BF16)

    @pl.when(j >= tiles)
    def _():
        for b in range(blocks):
            spec_one[b] = dot(table_ref[...], d_state_ref[b * BLOCK : (b + 1) * BLOCK, :])

    slots(tiles, 2 * tiles, 1)

    @pl.when(j >= tiles)
    def _():
        spectral_loop(tile, state_product)

    slots(tiles, 2 * tiles, 2)

    @pl.when(j >= tiles)
    def _():
        for b in range(blocks):
            rows = slice(b * BLOCK, (b + 1) * BLOCK)
            mask = live_rows(live, b * BLOCK, BLOCK)
            d_mixed = dot(back_ref[...], prod[b]).astype(BF16).astype(F32)
            d_values[rows, :] = (mask * d_mixed * shifted_ref[rows, :].astype(F32)).astype(BF16)
            d_shifted = (d_mixed * v_ref[rows, :].astype(F32)).astype(BF16)
            spec_one[b] = dot(table_ref[...], d_shifted)
            spec_two[b] = dot(table_ref[...], k_ref[rows, :])

    slots(tiles, 2 * tiles, 3)

    def shift_product(sign, re, im, lanes):
        tr = tapspec_ref[re, lanes]
        ti = tapspec_ref[im, lanes]
        s = [(spec_one[b, re, lanes], spec_one[b, im, lanes]) for b in range(blocks)]
        x = [(spec_two[b, re, lanes], spec_two[b, im, lanes]) for b in range(blocks)]
        u = [multiply_conj(tr, ti, *s[b]) for b in range(blocks)]
        sum_re, sum_im = multiply_conj(*x[0], *s[0])
        for b in range(blocks):
            yr, yi = u[b]
            if b < blocks - 1:
                yr, yi = yr + sign * u[b + 1][1], yi - sign * u[b + 1][0]
            prod[b, re, lanes] = yr.astype(BF16)
            prod[b, im, lanes] = yi.astype(BF16)
            if b > 0:
                wr = x[b][0] - sign * x[b - 1][1]
                wi = x[b][1] + sign * x[b - 1][0]
                pr, pi = multiply_conj(wr, wi, *s[b])
                sum_re, sum_im = sum_re + pr, sum_im + pi
        shift_prod[re, lanes] = sum_re.astype(BF16)
        shift_prod[im, lanes] = sum_im.astype(BF16)

    def token_grad(rows):
        return (
            total[rows, :]
            + dot_nt(d_query_ref[rows, :], wq_ref[...])
            + dot_nt(d_keys[rows, :], wk_ref[...])
            + dot_nt(d_values[rows, :], wv_ref[...])
        )

    @pl.when(j >= tiles)
    def _():
        spectral_loop(tile, shift_product)

    slots(tiles, 2 * tiles, 4)

    @pl.when(j >= tiles)
    def _():
        for b in range(blocks):
            rows = slice(b * BLOCK, (b + 1) * BLOCK)
            mask = live_rows(live, b * BLOCK, BLOCK)
            d_keys[rows, :] = (mask * dot(back_ref[...], prod[b])).astype(BF16)
        taps = d_taps.shape[0]
        columns = pl.ds(pl.multiple_of((j - tiles) * tile, tile), tile)
        d_taps[:, columns] = dot(back_ref[:taps, :], shift_prod[...]) * (1.0 / BLOCK)
        for i, source in enumerate((d_keys, d_values)):
            spread(dot_tn(a_one[...], source[...]), kv_base.at[j - tiles, :, :, :, :, i * share : (i + 1) * share])

    slots(tiles, 2 * tiles, 5)

    @pl.when(jnp.logical_and(j >= tiles, j < 2 * tiles - 1))
    def _():
        for b in range(blocks):
            rows = slice(b * BLOCK, (b + 1) * BLOCK)
            total[rows, :] = token_grad(rows)

    slots(tiles, 2 * tiles, 6)

    @pl.when(j == 2 * tiles - 1)
    def _():
        late[1].wait()
        late[2].wait()
        gain_sum = jnp.zeros((1, width), F32)
        count = half // BLOCK
        for b in range(2 * count):
            low = (1 - side if b < count else side) * half + (b % count) * BLOCK
            rows = pl.ds(pl.multiple_of(low, BLOCK), BLOCK)
            normed, inv = norm_stats(x[rows, :].astype(F32))
            grad_in = token_grad(rows)
            gain_sum = gain_sum + jnp.sum(grad_in * normed, axis=0, keepdims=True)
            pulled = d_hidden[rows, :] + norm_pull(grad_in, normed, inv, row_of(gain_ref))
            d_x[b // count, (b % count) * BLOCK : (b % count + 1) * BLOCK, :] = pulled.astype(BF16)
            events(2 * tiles - 1, 7 + b)
        keep_row().start()
        gains = jnp.concatenate([gain_sum, gain_two_grad_ref[...], jnp.zeros((6 - each, width), F32)], axis=0)
        for owner, place in enumerate(places(lax.axis_index("dp"), 16, (1, 2, 4, 8))):
            taps_base[(*place, slice(0, each))] = d_taps[owner * each : (owner + 1) * each, :]
            taps_base[(*place, slice(each, 8))] = gains
        events(2 * tiles - 1, 11)
        follow(sums, BACK_LEFT)
        keep_out().wait()
        keep_row().wait()


def mixer_back_call(
    lengths, out_row, a_one, d_state, d_query, mixed, shifted, k, v, wq, wk, wv, kern, tapspec, tables, x, gain, d_hidden,
    d_gain_two, coef, rate, begun, taps_count, tile,
):
    length, width = a_one.shape
    blocks = length // BLOCK
    half = length // 2
    table, back = tables
    share = width // 16
    ks = length // 16
    count = width // tile
    both = lambda j: (0, lax.rem(j, count))
    first = lambda j: (0, jnp.minimum(j, count - 1))
    second = lambda j: (0, jnp.maximum(j - count, 0))
    rows_second = pl.BlockSpec((length, tile), second)
    weight = pl.BlockSpec((width, tile), second)
    anywhere = pl.BlockSpec(memory_space=pl.ANY)
    low = lambda *shape: jax.ShapeDtypeStruct(shape, BF16)
    full = lambda *shape: jax.ShapeDtypeStruct(shape, F32)
    vmem = lambda *shape: pltpu.VMEM(shape, BF16)
    wide = lambda *shape: pltpu.VMEM(shape, F32)
    sems = lambda *shape: pltpu.SemaphoreType.DMA(shape)
    up_part, down_part, left = begun
    states, channels = rate.shape
    each = states // 16
    lands = []
    for name, index, exchange, _ in FEED_LEFT:
        order = ORDER[name][index]
        if name == DOWN:
            lands += gather_landings(*down_part.shape, order)[exchange + 1 :]
        else:
            lands += landings(share, width, order)[exchange + 1 :]
    bits = [(2, 2, 2), (2, 2), (2,), (), ()]
    lands += [wide(*bits[n], 2 * each, channels) for n in range(4)]
    lands += [wide(*bits[n], 8, width) for n in range(5)]
    for t in range(count):
        lands += landings(ks, tile, ORDER[KERN][t])
    for t in range(count):
        orders = ORDER[KV][t]
        for order in orders:
            lands += landings(2 * share // len(orders), tile, order)
    out_shape = [
        low(2, half, width),
        low(2, half, width),
        full(1, width // 16),
        full(1, width // 16),
        full(each, channels),
        full(each, channels),
        full(each, channels),
        full(*up_part.shape),
        full(*down_part.shape),
        full(share, width),
        full(share, width),
        full(share, width),
        full(share, width),
    ]
    return pl.pallas_call(
        mixer_back_body,
        grid=(2 * count,),
        in_specs=[pl.BlockSpec(memory_space=pltpu.SMEM), anywhere]
        + [pl.BlockSpec((length, tile), both), rows_second, pl.BlockSpec((length, tile), first)]
        + [rows_second] * 3
        + [weight] * 3
        + [
            pl.BlockSpec((blocks, 2 * BLOCK, tile), lambda j: (0, 0, jnp.maximum(j - count, 0))),
            pl.BlockSpec((2 * BLOCK, tile), second),
            once(table.shape),
            once(back.shape),
            once((width,)),
            once((1, width)),
            once(coef.shape),
            once(rate.shape),
            once(up_part.shape),
            once(down_part.shape),
        ]
        + [once(s.shape) for s in left]
        + [anywhere] * 3,
        out_specs=[anywhere, anywhere] + [once(s.shape) for s in out_shape[2:]],
        out_shape=out_shape,
        scratch_shapes=[
            wide(length, width),
            wide(blocks, 2 * BLOCK, tile),
            wide(blocks, 2 * BLOCK, tile),
            vmem(blocks, 2 * BLOCK, tile),
            vmem(2 * BLOCK, tile),
            vmem(length, tile),
            vmem(length, tile),
            vmem(2, half, width),
            vmem(length, width),
            vmem(length, width),
            wide(length, width),
            wide(taps_count, width),
            wide(ks, width),
            wide(2, 2, 2, 2, 8, width),
            sems(5, 2),
            wide(2, 2, 2, 2, 2 * each, channels),
            sems(4, 2),
            vmem(count, *base_shape(ks, tile, "")),
            vmem(count, *base_shape(2 * share, tile, "")),
            sems(len(left), 6, 2),
            sems(count, 5, 2),
            sems(count, 2, 6, 2),
            sems(2, 2),
            sems(2, 2),
            sems(2),
            sems(3),
            *lands,
        ],
        compiler_params=pltpu.CompilerParams(
            vmem_limit_bytes=62 * 1024 * 1024, collective_id=2, has_side_effects=True
        ),
        cost_estimate=cost(26e9, 40e6),
        name="mixer_back",
    )(
        lengths, out_row, d_state, d_query, mixed, shifted, k, v, wq, wk, wv, kern, tapspec, table, back, gain,
        d_gain_two, coef, rate, up_part, down_part, *left, a_one, x, d_hidden,
    )


MICRO = 2


epsilon = 1e-05
highest = lax.Precision.HIGHEST


def layer_norm(rows, gain):
    center = rows - jnp.mean(rows, axis=-1, keepdims=True)
    spread = jnp.mean(center * center, axis=-1, keepdims=True)
    return center * lax.rsqrt(spread + epsilon) * gain


def exact_gelu(values):
    return jax.nn.gelu(values, approximate=False)


def project(rows, weight):
    return jnp.einsum("rtd,de->rte", rows, weight, preferred_element_type=jnp.float32)


def project_back(rows, weight):
    return jnp.einsum("rte,de->rtd", rows, weight, preferred_element_type=jnp.float32)


def weight_grad(left, right):
    return jnp.einsum("rtd,rte->de", left, right, preferred_element_type=jnp.float32)


def depth_conv(signal, kernel_taps):
    channels = signal.shape[2]
    return lax.conv_general_dilated(
        signal,
        kernel_taps,
        (1,),
        "VALID",
        dimension_numbers=("NWC", "WIO", "NWC"),
        feature_group_count=channels,
        precision=highest,
    )


def shift_conv(extended, taps, length):
    flipped = jnp.transpose(taps[:, ::-1])[:, None, :]
    return depth_conv(extended[:, 1:, :], flipped)[:, :length, :]


def shift_back(extended, taps, length):
    forward_taps = jnp.transpose(taps)[:, None, :]
    return depth_conv(extended, forward_taps)[:, :length, :]


def taps_grad(grad_rows, extended, width_taps):
    rows_count, span, channels = extended.shape
    left = jnp.transpose(extended, (2, 0, 1)).reshape(1, channels * rows_count, span)
    right = jnp.transpose(grad_rows, (2, 0, 1))
    result = lax.conv_general_dilated(
        left,
        right,
        (1,),
        "VALID",
        dimension_numbers=("NCW", "OIW", "NCW"),
        feature_group_count=channels,
        precision=highest,
    )
    return result[0][:, ::-1][:, :width_taps]


def diag_kernel(coef, rate, length):
    steps = lax.iota(jnp.float32, length)
    return jnp.sum(coef[:, :, None] * jnp.exp(-rate[:, :, None] * steps), axis=1)


def dft_tables(length):
    period = 2 * length
    time_index = lax.iota(jnp.int32, length)[:, None]
    freq_index = lax.iota(jnp.int32, length + 1)[None, :]
    phase_index = time_index * freq_index % period
    angles = phase_index.astype(jnp.float32) * (2.0 * math.pi / period)
    cos_table = jnp.cos(angles)
    sin_table = jnp.sin(angles)
    edges = (freq_index == 0) | (freq_index == length)
    weights = jnp.where(edges, 1.0, 2.0).astype(jnp.float32) / period
    return (cos_table, sin_table, cos_table * weights, sin_table * weights)


def spectrum(signal, cos_table, sin_table):
    real_part = jnp.einsum("rtc,tf->rfc", signal, cos_table, precision=highest)
    imag_part = -jnp.einsum("rtc,tf->rfc", signal, sin_table, precision=highest)
    return (real_part, imag_part)


def inverse(real_part, imag_part, cos_weighted, sin_weighted):
    first = jnp.einsum("rfc,tf->rtc", real_part, cos_weighted, precision=highest)
    second = jnp.einsum("rfc,tf->rtc", imag_part, sin_weighted, precision=highest)
    return first - second


def split_channels(
    tokens,
    lengths,
    gain_one,
    w_query,
    w_key,
    w_value,
    w_out,
    gain_two,
    w_up,
    w_down,
    shift_taps,
    diag_coef,
    diag_rate,
    cotangent,
):
    rows_dev, tok_len, model_width = tokens.shape
    length = tok_len * lax.axis_size("seq")
    width_taps = shift_taps.shape[1]
    first_pos = lax.axis_index("seq") * tok_len
    positions = first_pos + lax.iota(jnp.int32, tok_len)
    mask_all = (positions[None, :] < lengths[:, None]).astype(jnp.float32)[:, :, None]
    cos_table, sin_table, cos_weighted, sin_weighted = dft_tables(length)

    def kernel_of(coef_in, rate_in):
        return diag_kernel(coef_in, rate_in, length)

    kernel, kernel_pull = jax.vjp(kernel_of, diag_coef, diag_rate)
    kernel_real = jnp.einsum("ct,tf->fc", kernel, cos_table, precision=highest)
    kernel_imag = -jnp.einsum("ct,tf->fc", kernel, sin_table, precision=highest)
    taps_acc = jnp.zeros(shift_taps.shape, jnp.float32)
    spec_real_acc = jnp.zeros((length + 1, shift_taps.shape[0]), jnp.float32)
    spec_imag_acc = jnp.zeros((length + 1, shift_taps.shape[0]), jnp.float32)
    grad_gain_one = jnp.zeros(gain_one.shape, jnp.float32)
    grad_gain_two = jnp.zeros(gain_two.shape, jnp.float32)
    grad_query = jnp.zeros(w_query.shape, jnp.float32)
    grad_key = jnp.zeros(w_key.shape, jnp.float32)
    grad_value = jnp.zeros(w_value.shape, jnp.float32)
    grad_out = jnp.zeros(w_out.shape, jnp.float32)
    grad_up = jnp.zeros(w_up.shape, jnp.float32)
    grad_down = jnp.zeros(w_down.shape, jnp.float32)
    rows_mb = rows_dev // MICRO
    out_list = []
    dx_list = []
    for micro_step in range(MICRO):
        low_row = micro_step * rows_mb
        x_rows = tokens[low_row : low_row + rows_mb].astype(jnp.float32)
        live_mask = mask_all[low_row : low_row + rows_mb]
        grad_rows = cotangent[low_row : low_row + rows_mb].astype(jnp.float32)
        norm_one, norm_one_pull = jax.vjp(layer_norm, x_rows, gain_one)
        a_one = norm_one.astype(jnp.bfloat16)
        query_rows = project(a_one, w_query)
        key_rows = (project(a_one, w_key) * live_mask).astype(jnp.bfloat16)
        value_rows = (project(a_one, w_value) * live_mask).astype(jnp.bfloat16)
        keys_ch, values_ch = (
            lax.all_to_all(key_rows, "seq", split_axis=2, concat_axis=1, tiled=True),
            lax.all_to_all(value_rows, "seq", split_axis=2, concat_axis=1, tiled=True),
        )
        key_ext = jnp.pad(keys_ch.astype(jnp.float32), ((0, 0), (width_taps, 0), (0, 0)))
        shifted = shift_conv(key_ext, shift_taps, length)
        values_here = values_ch.astype(jnp.float32)
        mixed_ch = (shifted * values_here).astype(jnp.bfloat16)
        mixed_real, mixed_imag = spectrum(mixed_ch.astype(jnp.float32), cos_table, sin_table)
        state = inverse(
            mixed_real * kernel_real - mixed_imag * kernel_imag,
            mixed_real * kernel_imag + mixed_imag * kernel_real,
            cos_weighted,
            sin_weighted,
        )
        state_tok = lax.all_to_all(
            state.astype(jnp.bfloat16), "seq", split_axis=1, concat_axis=2, tiled=True
        )
        state_rows = state_tok.astype(jnp.float32)
        gated_rows = (query_rows * state_rows).astype(jnp.bfloat16)
        hidden = x_rows + live_mask * project(gated_rows, w_out)
        norm_two, norm_two_pull = jax.vjp(layer_norm, hidden, gain_two)
        a_two = norm_two.astype(jnp.bfloat16)
        pre_act = project(a_two, w_up)
        act_value, gelu_pull = jax.vjp(exact_gelu, pre_act)
        activation = act_value.astype(jnp.bfloat16)
        result = hidden + live_mask * project(activation, w_down)
        out_list.append(result.astype(jnp.bfloat16))
        d_down = (live_mask * grad_rows).astype(jnp.bfloat16)
        grad_down = grad_down + weight_grad(activation, d_down)
        d_act = project_back(d_down, w_down)
        d_pre = gelu_pull(d_act)[0].astype(jnp.bfloat16)
        grad_up = grad_up + weight_grad(a_two, d_pre)
        d_a_two = project_back(d_pre, w_up)
        d_hidden_norm, d_gain_two = norm_two_pull(d_a_two)
        grad_gain_two = grad_gain_two + d_gain_two
        d_hidden = grad_rows + d_hidden_norm
        d_mixer = (live_mask * d_hidden).astype(jnp.bfloat16)
        grad_out = grad_out + weight_grad(gated_rows, d_mixer)
        d_gated = project_back(d_mixer, w_out)
        d_query = (d_gated * state_rows).astype(jnp.bfloat16)
        d_state = (d_gated * query_rows).astype(jnp.bfloat16)
        d_state_ch = lax.all_to_all(d_state, "seq", split_axis=2, concat_axis=1, tiled=True)
        grad_real, grad_imag = spectrum(d_state_ch.astype(jnp.float32), cos_table, sin_table)
        d_mixed = inverse(
            kernel_real * grad_real + kernel_imag * grad_imag,
            kernel_real * grad_imag - kernel_imag * grad_real,
            cos_weighted,
            sin_weighted,
        )
        spec_real_acc = spec_real_acc + jnp.sum(
            mixed_real * grad_real + mixed_imag * grad_imag, axis=0
        )
        spec_imag_acc = spec_imag_acc + jnp.sum(
            mixed_real * grad_imag - mixed_imag * grad_real, axis=0
        )
        d_mixed_low = d_mixed.astype(jnp.bfloat16)
        d_mix_ch = d_mixed_low.astype(jnp.float32)
        d_shifted = d_mix_ch * values_here
        d_values_ch = (d_mix_ch * shifted).astype(jnp.bfloat16)
        grad_ext = jnp.pad(d_shifted, ((0, 0), (0, width_taps), (0, 0)))
        d_keys_ch = shift_back(grad_ext, shift_taps, length).astype(jnp.bfloat16)
        taps_acc = taps_acc + taps_grad(d_shifted, key_ext, width_taps)
        keys_back, values_back = (
            lax.all_to_all(d_keys_ch, "seq", split_axis=1, concat_axis=2, tiled=True),
            lax.all_to_all(d_values_ch, "seq", split_axis=1, concat_axis=2, tiled=True),
        )
        mask_low = live_mask.astype(jnp.bfloat16)
        d_keys = keys_back * mask_low
        d_values = values_back * mask_low
        grad_query = grad_query + weight_grad(a_one, d_query)
        grad_key = grad_key + weight_grad(a_one, d_keys)
        grad_value = grad_value + weight_grad(a_one, d_values)
        d_a_one = (
            project_back(d_query, w_query)
            + project_back(d_keys, w_key)
            + project_back(d_values, w_value)
        )
        d_x_norm, d_gain_one = norm_one_pull(d_a_one)
        grad_gain_one = grad_gain_one + d_gain_one
        dx_list.append((d_hidden + d_x_norm).astype(jnp.bfloat16))
    d_kernel = jnp.einsum("fc,tf->ct", spec_real_acc, cos_weighted, precision=highest) - jnp.einsum(
        "fc,tf->ct", spec_imag_acc, sin_weighted, precision=highest
    )
    d_coef, d_rate = kernel_pull(d_kernel)
    taps_part, coef_part, rate_part = (
        lax.psum_scatter(
            taps_acc.astype(jnp.bfloat16), "dp", scatter_dimension=1, tiled=True
        ).astype(jnp.float32),
        lax.psum_scatter(d_coef.astype(jnp.bfloat16), "dp", scatter_dimension=1, tiled=True).astype(
            jnp.float32
        ),
        lax.psum_scatter(d_rate.astype(jnp.bfloat16), "dp", scatter_dimension=1, tiled=True).astype(
            jnp.float32
        ),
    )
    shares = (
        lax.psum_scatter(
            grad_gain_one.astype(jnp.bfloat16), "dp", scatter_dimension=0, tiled=True
        ).astype(jnp.float32),
        lax.psum_scatter(
            grad_query.astype(jnp.bfloat16), "dp", scatter_dimension=0, tiled=True
        ).astype(jnp.float32),
        lax.psum_scatter(
            grad_key.astype(jnp.bfloat16), "dp", scatter_dimension=0, tiled=True
        ).astype(jnp.float32),
        lax.psum_scatter(
            grad_value.astype(jnp.bfloat16), "dp", scatter_dimension=0, tiled=True
        ).astype(jnp.float32),
        lax.psum_scatter(
            grad_out.astype(jnp.bfloat16), "dp", scatter_dimension=0, tiled=True
        ).astype(jnp.float32),
        lax.psum_scatter(
            grad_gain_two.astype(jnp.bfloat16), "dp", scatter_dimension=0, tiled=True
        ).astype(jnp.float32),
        lax.psum_scatter(
            grad_up.astype(jnp.bfloat16), "dp", scatter_dimension=0, tiled=True
        ).astype(jnp.float32),
        lax.psum_scatter(
            grad_down.astype(jnp.bfloat16), "dp", scatter_dimension=0, tiled=True
        ).astype(jnp.float32),
    )
    totals = (
        lax.psum(shares[0].astype(jnp.bfloat16), "seq").astype(jnp.float32),
        lax.psum(shares[1].astype(jnp.bfloat16), "seq").astype(jnp.float32),
        lax.psum(shares[2].astype(jnp.bfloat16), "seq").astype(jnp.float32),
        lax.psum(shares[3].astype(jnp.bfloat16), "seq").astype(jnp.float32),
        lax.psum(shares[4].astype(jnp.bfloat16), "seq").astype(jnp.float32),
        lax.psum(shares[5].astype(jnp.bfloat16), "seq").astype(jnp.float32),
        lax.psum(shares[6].astype(jnp.bfloat16), "seq").astype(jnp.float32),
        lax.psum(shares[7].astype(jnp.bfloat16), "seq").astype(jnp.float32),
    )
    out_rows = jnp.concatenate(out_list, axis=0)
    dx_rows = jnp.concatenate(dx_list, axis=0)
    return (
        out_rows,
        dx_rows,
        totals[0],
        totals[1],
        totals[2],
        totals[3],
        totals[4],
        totals[5],
        totals[6],
        totals[7],
        taps_part,
        coef_part,
        rate_part,
    )


def settle_body(first_ref, *refs):
    count = (len(refs) - 1) // 3
    sources, targets, held, sems = refs[:count], refs[count : 2 * count], refs[2 * count : 3 * count], refs[-1]
    reads = [pltpu.make_async_copy(sources[i], held[i], sems.at[0, i]) for i in range(count)]
    writes = [pltpu.make_async_copy(held[i], targets[i], sems.at[1, i]) for i in range(count)]
    place = held[0].at[1 - lax.axis_index("seq"), pl.ds(0, first_ref.shape[0])]
    first = pltpu.make_async_copy(first_ref, place, sems.at[0, count])
    for copy in reads:
        copy.start()
    reads[0].wait()
    first.start()
    for read, write in zip(reads[1:], writes[1:]):
        read.wait()
        write.start()
    first.wait()
    writes[0].start()
    for copy in writes:
        copy.wait()


def settle_call(first, arrays):
    anywhere = pl.BlockSpec(memory_space=pl.ANY)
    return pl.pallas_call(
        settle_body,
        in_specs=[anywhere] * (1 + len(arrays)),
        out_specs=[anywhere] * len(arrays),
        out_shape=[jax.ShapeDtypeStruct(array.shape, array.dtype) for array in arrays],
        scratch_shapes=[pltpu.VMEM(array.shape, array.dtype) for array in arrays]
        + [pltpu.SemaphoreType.DMA((2, len(arrays) + 1))],
        compiler_params=params(),
        cost_estimate=cost(1e3, 10e6),
        name="settle",
    )(first, *arrays)


def split_rows(
    tokens, lengths, gain_one, w_query, w_key, w_value, w_out, gain_two, w_up, w_down,
    shift_taps, diag_coef, diag_rate, cotangent,
):
    states = diag_coef.shape[1]
    tile = 256
    tables = transform_tables()
    coef, rate, taps = diag_coef.T, diag_rate.T, shift_taps.T
    x, cot, a_one, q, k, v, kern, tapspec, hidden, a_two, shifted, mixed, state = mixer_call(
        lengths, tokens, cotangent, coef, rate, taps, gain_one, gain_two, w_query, w_key, w_value, w_out, tables, tile
    )
    out_row, d_hidden, d_query, d_state, out_first, d_gain_two, up_part, down_part, *left = ffn_call(
        lengths, a_two, cot, hidden, gain_two, w_up, w_down, w_out, state, q, a_one
    )
    out, d_tokens, gain_one_grad, gain_two_grad, taps_grad, coef_grad, rate_grad, up, down, wout, query, key, value = (
        settle_call(out_first, mixer_back_call(
            lengths, out_row, a_one, d_state, d_query, mixed, shifted, k, v, w_query, w_key, w_value, kern, tapspec,
            tables, x, gain_one, d_hidden, d_gain_two, coef, rate, (up_part, down_part, left), states, tile,
        ))
    )
    return (
        out,
        d_tokens,
        gain_one_grad.reshape(-1),
        query,
        key,
        value,
        wout,
        gain_two_grad.reshape(-1),
        up,
        down,
        taps_grad.T,
        coef_grad.T,
        rate_grad.T,
    )


def solution(mesh):
    in_specs = (
        P("dp", "seq", None),
        P("dp"),
        P(),
        P(),
        P(),
        P(),
        P(),
        P(),
        P(),
        P(),
        P("seq", None),
        P("seq", None),
        P("seq", None),
        P("dp", "seq", None),
    )
    out_specs = (
        P("dp", "seq", None),
        P("dp", "seq", None),
        P("dp"),
        P("dp", None),
        P("dp", None),
        P("dp", None),
        P("dp", None),
        P("dp"),
        P("dp", None),
        P("dp", None),
        P("seq", "dp"),
        P("seq", "dp"),
        P("seq", "dp"),
    )

    def per_device(*args):
        tokens, shift_taps = args[0], args[10]
        rows, positions, width = tokens.shape
        fits = (
            mesh.shape["seq"] == rows == 2
            and mesh.shape["dp"] == 16
            and positions * 2 % BLOCK == 0
            and width % 256 == 0
            and shift_taps.shape[1] <= BLOCK
        )
        return split_rows(*args) if fits else split_channels(*args)

    return jax.shard_map(
        per_device, mesh=mesh, in_specs=in_specs, out_specs=out_specs, check_vma=False
    )
```
